32 devices in a mesh: group: 8 (over y, x, core), mp: 4 (over z).
Axes of the slice: x: 2, y: 2, z: 4, core: 2. Of those that a mesh axis runs over, the one named last changes fastest.
Arguments:
- hidden_in: bfloat16 [4096, 1024], P('group'), may hold values from -8 to 8
- request_ids: int32 [4096], P('group'), may hold values from 63 to 4095, as said below
- w_qkv: float32 [1024, 3072], P(('group', 'mp')), may hold values from -1 to 1
- w_out: float32 [1024, 1024], P(('group', 'mp')), may hold values from -0.1875 to 0.1875
- w_up: float32 [1024, 4096], P(('group', 'mp')), may hold values from -0.1875 to 0.1875
- w_down: float32 [1024, 4096], P(('group', 'mp')), may hold values from -0.09375 to 0.09375
- ln1_gain: float32 [1024], replicated, may hold values from 0.25 to 1.75
- ln1_shift: float32 [1024], replicated, may hold values from -3 to 3
- ln2_gain: float32 [1024], replicated, may hold values from 0.25 to 1.75
- ln2_shift: float32 [1024], replicated, may hold values from -3 to 3
Outputs:
- hidden_out: bfloat16 [4096, 1024], P(('group', 'mp'))
- keys_cache: bfloat16 [4096, 1024], P('group', 'mp')
- values_cache: bfloat16 [4096, 1024], P('group', 'mp')
The draws below stay inside these ranges and needn't reach their ends.
Inputs may be any that keep to these rules, and one draw needn't show every extreme that they name: `request_ids`: each slot holds the index of the last slot of its request. In groups 2i and 2i+1 (of 512 slots each) one request of exactly 512 slots ends the first group and begins the second, at least 64 of its slots in each; every other request lies within one aligned block of 64 slots, one or two requests a block, and some blocks hold one request of exactly 64 slots.
All inputs are finite; a program needn't handle non-finite values.
Results may differ from the reference program's by a relative error of at most 0.011.
Values may be sent and summed in bfloat16 or wider, within the bound.
A program may use at most 64 MiB of HBM per device.

```python
import jax
import jax.numpy as jnp
from jax import lax

D = 1024
HEADS = 16
HD = 64
FF = 4096
TOK_G = 512
SHORT = 64
TOKENS = 4096
N_GROUP = 8


def draw_hidden_in(key, part):
    base_values = jnp.clip(jax.random.normal(key, (TOKENS, D), jnp.float32), -6.0, 6.0)
    return base_values.astype(jnp.bfloat16)


def draw_w_qkv(key, part):
    base_values = jnp.clip(jax.random.normal(key, (D, 3 * D), jnp.float32), -5.0, 5.0) * D ** (-0.5)
    sharpen = jnp.concatenate([jnp.full((2 * D,), 1.7, jnp.float32), jnp.ones((D,), jnp.float32)])
    base_values = base_values * sharpen
    return jnp.clip(base_values, -1.0, 1.0)


def draw_request_ids(key, part):
    block_total = TOKENS // SHORT
    per_group = TOK_G // SHORT
    pair_total = TOKENS // (2 * TOK_G)
    long_tail = jax.random.randint(jax.random.fold_in(key, 1), (pair_total,), 1, per_group)
    split_flag = jax.random.randint(jax.random.fold_in(key, 2), (block_total,), 0, 2)
    split_flag = split_flag.at[0].set(0)
    cut_point = jax.random.randint(jax.random.fold_in(key, 3), (block_total,), 1, SHORT)
    position = jnp.arange(TOKENS, dtype=jnp.int32)
    group_of = position // TOK_G
    block_of = position // SHORT
    in_block = position % SHORT
    within = position % TOK_G // SHORT
    pair_of = group_of // 2
    tail_here = long_tail[pair_of]
    is_long = jnp.where(group_of % 2 == 0, within >= per_group - tail_here, within < per_group - tail_here)
    long_end = (2 * pair_of + 1) * TOK_G + (per_group - tail_here) * SHORT - 1
    block_start = block_of * SHORT
    cut_here = cut_point[block_of]
    short_end = jnp.where((split_flag[block_of] == 1) & (in_block < cut_here), block_start + cut_here - 1, block_start + SHORT - 1)
    return jnp.where(is_long, long_end, short_end).astype(jnp.int32)


def levels(rng, dims, pieces, least, high):
    level, own = 1.0, jax.random.fold_in(rng, 6)
    for dim, blocks in pieces:
        heights = jnp.exp(jax.random.uniform(jax.random.fold_in(own, dim), (blocks,), jnp.float32, least / len(pieces), high / len(pieces)))
        level = level * jnp.repeat(heights, dims[dim] // blocks).reshape([-1 if axis == dim else 1 for axis in range(len(dims))])
    return level


def gaussian(rng, extent, width, most, shards=(), kind=jnp.bfloat16):
    entries = jax.random.normal(rng, extent, jnp.float32) * width
    if len(shards) > 0:
        entries = levels(rng, extent, shards, -0.22, 0.18) * entries
    return jnp.clip(entries, min=-most, max=most).astype(kind)


def setup_inputs(seed: int = 0) -> dict:
    key_list = jax.random.split(jax.random.key(seed), 11)
    return {
        "hidden_in": draw_hidden_in(jax.random.fold_in(key_list[10], 71), 0),
        "request_ids": draw_request_ids(jax.random.fold_in(key_list[10], 71), 0),
        "w_qkv": draw_w_qkv(jax.random.fold_in(key_list[10], 71), 0),
        "w_out": gaussian(key_list[3], (D, D), D ** -0.5, 0.1875, ((0, 32),), jnp.float32),
        "w_up": gaussian(key_list[4], (D, FF), D ** -0.5, 0.1875, ((0, 32),), jnp.float32),
        "w_down": gaussian(key_list[5], (D, FF), FF ** -0.5, 0.09375, ((0, 32),), jnp.float32),
        "ln1_gain": jnp.clip(1.0 + 0.15 * jax.random.normal(key_list[6], (D,), jnp.float32), 0.25, 1.75),
        "ln1_shift": gaussian(key_list[7], (D,), 0.5, 3.0, (), jnp.float32),
        "ln2_gain": jnp.clip(1.0 + 0.15 * jax.random.normal(key_list[8], (D,), jnp.float32), 0.25, 1.75),
        "ln2_shift": gaussian(key_list[9], (D,), 0.5, 3.0, (), jnp.float32),
    }


def layer_norm(values_in, norm_gain, norm_shift):
    center = values_in - lax.optimization_barrier(jnp.mean(values_in, axis=-1, keepdims=True))
    spread = lax.optimization_barrier(jnp.mean(center * center, axis=-1, keepdims=True))
    return center * lax.rsqrt(spread + 1e-05) * norm_gain + norm_shift

def reference(hidden_in, request_ids, w_qkv, w_out, w_up, w_down, ln1_gain, ln1_shift, ln2_gain, ln2_shift):
    qkv_weight = w_qkv.astype(jnp.bfloat16)
    out_weight = w_out.astype(jnp.bfloat16)
    up_weight = w_up.astype(jnp.bfloat16)
    down_weight = w_down.astype(jnp.bfloat16)
    projected = jnp.dot(hidden_in, qkv_weight, preferred_element_type=jnp.float32)
    queries, key_rows, value_rows = lax.optimization_barrier((projected[:, :D].astype(jnp.bfloat16), projected[:, D:2 * D].astype(jnp.bfloat16), projected[:, 2 * D:].astype(jnp.bfloat16)))
    pair_count = N_GROUP // 2
    pair_span = 2 * TOK_G

    def pair_attend(pair_block):
        pair_queries, pair_keys, pair_values, pair_ids = pair_block
        heads_q = pair_queries.astype(jnp.float32).reshape(pair_span, HEADS, HD)
        heads_k = pair_keys.astype(jnp.float32).reshape(pair_span, HEADS, HD)
        heads_v = pair_values.astype(jnp.float32).reshape(pair_span, HEADS, HD)
        scores = jnp.einsum('qhd,khd->hqk', heads_q, heads_k) * HD ** (-0.5)
        allowed = pair_ids[:, None] == pair_ids[None, :]
        scores = jnp.where(allowed[None], scores, -1e+30)
        row_peak = lax.optimization_barrier(jnp.max(scores, axis=-1, keepdims=True))
        weights = lax.optimization_barrier(jnp.exp(scores - row_peak).astype(jnp.bfloat16)).astype(jnp.float32)
        totals = lax.optimization_barrier(jnp.sum(weights, axis=-1))
        mixed_heads = jnp.einsum('hqk,khd->qhd', weights, heads_v) / jnp.transpose(totals)[:, :, None]
        return mixed_heads.astype(jnp.bfloat16).reshape(pair_span, D)
    attended = lax.map(pair_attend, (queries.reshape(pair_count, pair_span, D), key_rows.reshape(pair_count, pair_span, D), value_rows.reshape(pair_count, pair_span, D), request_ids.reshape(pair_count, pair_span))).reshape(TOKENS, D)
    attn_sum = jnp.dot(attended, out_weight.T, preferred_element_type=jnp.float32)
    attn_normed = layer_norm(hidden_in.astype(jnp.float32) + attn_sum, ln1_gain, ln1_shift).astype(jnp.bfloat16)
    activated = jax.nn.gelu(jnp.dot(attn_normed, up_weight, preferred_element_type=jnp.float32), approximate=False).astype(jnp.bfloat16)
    feed_sum = jnp.dot(activated, down_weight.T, preferred_element_type=jnp.float32)
    output_rows = layer_norm(attn_normed.astype(jnp.float32) + feed_sum, ln2_gain, ln2_shift).astype(jnp.bfloat16)
    return (output_rows, key_rows, value_rows)
```

```python
import functools

import jax
import jax.numpy as jnp
from jax import lax
from jax.experimental import pallas as pl
from jax.experimental.pallas import tpu as pltpu
from jax.sharding import PartitionSpec as P

HD = 64
SHORT = 64


def swapped(value, axis, distance):
    return lax.ppermute(value, axis, [(i, i ^ 1 << distance) for i in range(lax.axis_size(axis))])


def layer_norm(values_in, norm_gain, norm_shift):
    center = values_in - jnp.mean(values_in, axis=-1, keepdims=True)
    spread = jnp.mean(center * center, axis=-1, keepdims=True)
    return center * lax.rsqrt(spread + 1e-05) * norm_gain + norm_shift


def plain_body(
    hidden_in, request_ids, w_qkv, w_out, w_up, w_down, ln1_gain, ln1_shift, ln2_gain, ln2_shift
):
    groups = lax.axis_size("group")
    shards = lax.axis_size("mp")
    model_width = hidden_in.shape[1]
    local_width = model_width // shards
    local_hidden = w_up.shape[1] // shards
    tok_rows = hidden_in.shape[0]
    part_rows = w_qkv.shape[0]
    pieces = (
        w_qkv.astype(jnp.bfloat16).reshape(part_rows, 3, shards, local_width),
        w_out.astype(jnp.bfloat16).reshape(part_rows, 1, shards, local_width),
        w_up.astype(jnp.bfloat16).reshape(part_rows, 1, shards, local_hidden),
        w_down.astype(jnp.bfloat16).reshape(part_rows, 1, shards, local_hidden),
    )
    gathered = (
        lax.all_gather(pieces[0], "group", axis=0, tiled=True),
        lax.all_gather(pieces[1], "group", axis=0, tiled=True),
        lax.all_gather(pieces[2], "group", axis=0, tiled=True),
        lax.all_gather(pieces[3], "group", axis=0, tiled=True),
    )
    exchanged = (
        lax.all_to_all(gathered[0], "mp", split_axis=2, concat_axis=0, tiled=True),
        lax.all_to_all(gathered[1], "mp", split_axis=2, concat_axis=0, tiled=True),
        lax.all_to_all(gathered[2], "mp", split_axis=2, concat_axis=0, tiled=True),
        lax.all_to_all(gathered[3], "mp", split_axis=2, concat_axis=0, tiled=True),
    )
    served = tuple(
        (
            jnp.transpose(
                weight_piece.reshape(shards, groups, part_rows, -1), (1, 0, 2, 3)
            ).reshape(model_width, -1)
            for weight_piece in exchanged
        )
    )
    qkv_local, out_local, up_local, down_local = served
    projected = jnp.dot(hidden_in, qkv_local, preferred_element_type=jnp.float32)
    queries = projected[:, :local_width].astype(jnp.bfloat16)
    key_rows = projected[:, local_width : 2 * local_width].astype(jnp.bfloat16)
    value_rows = projected[:, 2 * local_width :].astype(jnp.bfloat16)
    partner_keys, partner_values = swapped((key_rows, value_rows), "group", 0)
    group_index = lax.axis_index("group")
    parity = group_index % 2
    long_id = jnp.where(parity == 0, request_ids[-1], request_ids[0])
    own_long = request_ids == long_id
    local_heads = local_width // HD
    score_scale = HD ** (-0.5)
    block_total = tok_rows // SHORT
    short_q = queries.reshape(block_total, SHORT, local_heads, HD)
    short_k = key_rows.reshape(block_total, SHORT, local_heads, HD)
    short_v = value_rows.reshape(block_total, SHORT, local_heads, HD)
    short_ids = request_ids.reshape(block_total, SHORT)
    short_scores = (
        jnp.einsum("bqhd,bkhd->bhqk", short_q, short_k, preferred_element_type=jnp.float32)
        * score_scale
    )
    short_mask = short_ids[:, :, None] == short_ids[:, None, :]
    short_scores = jnp.where(short_mask[:, None], short_scores, -1e30)
    short_peak = jnp.max(short_scores, axis=-1, keepdims=True)
    short_weights = jnp.exp(short_scores - short_peak).astype(jnp.bfloat16)
    short_totals = jnp.sum(short_weights.astype(jnp.float32), axis=-1)
    short_mixed = jnp.einsum(
        "bhqk,bkhd->bqhd", short_weights, short_v, preferred_element_type=jnp.float32
    )
    short_out = (
        (short_mixed / jnp.transpose(short_totals, (0, 2, 1))[:, :, :, None])
        .astype(jnp.bfloat16)
        .reshape(tok_rows, local_width)
    )
    first_keys = jnp.where(parity == 0, key_rows, partner_keys)
    second_keys = jnp.where(parity == 0, partner_keys, key_rows)
    first_values = jnp.where(parity == 0, value_rows, partner_values)
    second_values = jnp.where(parity == 0, partner_values, value_rows)
    pair_base = (group_index - parity) * tok_rows
    span_start = long_id - tok_rows + 1 - pair_base
    long_keys = lax.dynamic_slice_in_dim(
        jnp.concatenate([first_keys, second_keys], 0), span_start, tok_rows, 0
    ).reshape(tok_rows, local_heads, HD)
    long_values = lax.dynamic_slice_in_dim(
        jnp.concatenate([first_values, second_values], 0), span_start, tok_rows, 0
    ).reshape(tok_rows, local_heads, HD)
    query_rows = min(512, tok_rows)
    query_blocks = tok_rows // query_rows

    def long_attend(block_queries):
        heads_view = block_queries.reshape(query_rows, local_heads, HD)
        scores = (
            jnp.einsum("qhd,khd->hqk", heads_view, long_keys, preferred_element_type=jnp.float32)
            * score_scale
        )
        row_peak = jnp.max(scores, axis=-1, keepdims=True)
        weights = jnp.exp(scores - row_peak).astype(jnp.bfloat16)
        totals = jnp.sum(weights.astype(jnp.float32), axis=-1)
        mixed_heads = jnp.einsum(
            "hqk,khd->qhd", weights, long_values, preferred_element_type=jnp.float32
        )
        return (
            (mixed_heads / jnp.transpose(totals)[:, :, None])
            .astype(jnp.bfloat16)
            .reshape(query_rows, local_width)
        )

    def skipped(block_queries):
        return jnp.zeros((query_rows, local_width), jnp.bfloat16)

    def long_block(query_block):
        block_queries, block_long = query_block
        return lax.cond(jnp.any(block_long), long_attend, skipped, block_queries)

    long_out = lax.map(
        long_block,
        (
            queries.reshape(query_blocks, query_rows, local_width),
            own_long.reshape(query_blocks, query_rows),
        ),
    ).reshape(tok_rows, local_width)
    attended = jnp.where(own_long[:, None], long_out, short_out)
    share_rows = tok_rows // shards
    row_start = lax.axis_index("mp") * share_rows

    def combine(term_fn, residual, norm_gain, norm_shift):
        summed = lax.psum(term_fn(0, tok_rows), "mp")
        whole_rows = layer_norm(
            residual.astype(jnp.float32) + summed, norm_gain, norm_shift
        ).astype(jnp.bfloat16)
        normed = lax.dynamic_slice_in_dim(whole_rows, row_start, share_rows, 0)
        return (normed, whole_rows)

    def attn_term(row_begin, row_count):
        return lax.dot_general(
            attended, out_local, (((1,), (1,)), ((), ())), preferred_element_type=jnp.float32
        )

    attn_share, attn_normed = combine(attn_term, hidden_in, ln1_gain, ln1_shift)
    activated = jax.nn.gelu(
        jnp.dot(attn_normed, up_local, preferred_element_type=jnp.float32), approximate=False
    ).astype(jnp.bfloat16)

    def feed_term(row_begin, row_count):
        return lax.dot_general(
            activated, down_local, (((1,), (1,)), ((), ())), preferred_element_type=jnp.float32
        )

    final_share, unused = combine(feed_term, attn_normed, ln2_gain, ln2_shift)
    return (final_share, key_rows, value_rows)


MESH = pl.DeviceIdType.MESH
Q, O, U, W = range(4)


def layer_kernel(
    shards, hid, id_col, id_row, w_qkv, w_out, w_up, w_down, gain1, shift1, gain2, shift2,
    out, k_out, v_out,
    stage_q, stage_o, stage_u, stage_d, full_q, full_o, full_u, full_d,
    bias, queries, keys, vals, att, sums, normed, act, rs_send, rs_recv,
    z_send, z_recv, p_send, p_recv, kv_send, kv_recv, a_send, a_recv, r_send, r_recv,
):
    g = lax.axis_index("group")
    m = lax.axis_index("mp")
    core = lax.rem(g, 2)
    sib = g + 1 - 2 * core
    gx = g + 2 - 4 * lax.rem(g // 2, 2)
    gy = g + 4 - 8 * (g // 4)
    gd = gx + gy - g
    rows = hid.shape[0]
    width = hid.shape[1]
    part = w_qkv.shape[0]
    lw = queries.shape[1]
    lh = act.shape[1]
    pairs = lw // 128
    share = rows // shards
    f32, b16 = jnp.float32, jnp.bfloat16
    fulls = (full_q, full_o, full_u, full_d)
    stages = (stage_q, stage_o, stage_u, stage_d)
    peers = [lax.rem(m + k, shards) for k in range(1, shards)]
    mine = g * shards + m

    def z_copy(kind, k):
        chunk = stages[kind].at[0] if kind == O else stages[kind].at[peers[k]]
        return pltpu.make_async_remote_copy(
            src_ref=chunk, dst_ref=fulls[kind].at[mine],
            send_sem=z_send.at[kind, k], recv_sem=z_recv.at[kind, k],
            device_id=(g, peers[k]), device_id_type=MESH)

    fwd_to = gy * (1 - core) + gx * core
    fwd_block = gx * (1 - core) + gy * core
    hops = ((g, gx), (g, gy), (fwd_block, fwd_to), (g, sib), (gx, sib), (gy, sib), (gd, sib))

    def p_copy(kind, step):
        block, target = hops[step]
        place = fulls[kind].at[pl.ds(block * shards, shards)]
        return pltpu.make_async_remote_copy(
            src_ref=place, dst_ref=place,
            send_sem=p_send.at[kind, step], recv_sem=p_recv.at[kind, step],
            device_id=(target, m), device_id_type=MESH)

    def first_hop(kind):
        for k in range(shards - 1):
            z_copy(kind, k).wait_recv()
        for step in (0, 1, 3):
            p_copy(kind, step).start()

    def second_hop(kind):
        p_copy(kind, 0).wait_recv()
        p_copy(kind, 1).wait_recv()
        for step in (2, 4, 5):
            p_copy(kind, step).start()

    def third_hop(kind):
        p_copy(kind, 2).wait_recv()
        p_copy(kind, 6).start()

    def finish(kind):
        for step in (3, 4, 5, 6):
            p_copy(kind, step).wait_recv()

    def kv_copy(buf, i):
        return pltpu.make_async_remote_copy(
            src_ref=buf.at[0], dst_ref=buf.at[1],
            send_sem=kv_send.at[i], recv_sem=kv_recv.at[i],
            device_id=(sib, m), device_id_type=MESH)

    def a_copy(p, k):
        place = att.at[m * pairs + p]
        return pltpu.make_async_remote_copy(
            src_ref=place, dst_ref=place,
            send_sem=a_send.at[p, k], recv_sem=a_recv.at[p, k],
            device_id=(g, peers[k]), device_id_type=MESH)

    tiles = rs_send.shape[0]
    tile = rs_send.shape[2]

    def r_copy(n, k):
        return pltpu.make_async_remote_copy(
            src_ref=rs_send.at[n, pl.ds(pl.multiple_of(peers[k] * share, share), share)],
            dst_ref=rs_recv.at[k, n],
            send_sem=r_send.at[n, k], recv_sem=r_recv.at[n, k],
            device_id=(g, peers[k]), device_id_type=MESH)

    def stage(kind):
        if kind == Q:
            for d in range(shards):
                for j in range(3):
                    stage_q[d, :, j * lw:(j + 1) * lw] = w_qkv[
                        :, j * width + d * lw:j * width + (d + 1) * lw].astype(b16)
        elif kind == O:
            stage_o[0] = w_out[...].astype(b16)
        else:
            source = w_up if kind == U else w_down
            for d in range(shards):
                stages[kind][d] = source[:, d * lh:(d + 1) * lh].astype(b16)
        fulls[kind][mine] = stages[kind][0 if kind == O else m]

    stage(Q)
    barrier = pltpu.get_barrier_semaphore()
    everyone = [(g, peer) for peer in peers] + [(gx, m), (gy, m), (sib, m)]
    for target in everyone:
        pl.semaphore_signal(barrier, inc=1, device_id=target, device_id_type=MESH)
    pl.semaphore_wait(barrier, len(everyone))
    for kind in (Q, O, U, W):
        if kind != Q:
            stage(kind)
        for k in range(shards - 1):
            z_copy(kind, k).start()

    long_id = jnp.where(core == 0, id_col[rows - 1:rows, :], id_col[0:1, :])
    bias[:, :rows] = jnp.where(id_col[...] == id_row[...], 0.0, -1e30).astype(f32)
    slot = sib * rows + lax.broadcasted_iota(jnp.int32, (1, rows), 1)
    reach = jnp.where((slot > long_id - rows) & (slot <= long_id), long_id, -1)
    bias[:, rows:] = jnp.where(id_col[...] == reach, 0.0, -1e30).astype(f32)

    first_hop(Q)
    second_hop(Q)
    first_hop(O)
    third_hop(Q)
    finish(Q)

    def project(j):
        return jnp.dot(
            hid[...], full_q[:, :, j * lw:(j + 1) * lw].reshape(width, lw),
            preferred_element_type=f32).astype(b16)

    key_rows = project(1)
    keys[0] = key_rows
    kv_copy(keys, 0).start()
    k_out[...] = key_rows
    value_rows = project(2)
    vals[0] = value_rows
    kv_copy(vals, 1).start()
    v_out[...] = value_rows
    queries[...] = project(0) * jnp.asarray(HD ** -0.5, b16)
    first_hop(U)
    kv_copy(keys, 0).wait_recv()
    kv_copy(vals, 1).wait_recv()

    q_tile = min(128, rows)
    lane = lax.broadcasted_iota(jnp.int32, (q_tile, 128), 1)

    def attend(p):
        cols = slice(p * 128, (p + 1) * 128)
        pair_keys = keys[:, :, cols].reshape(2 * rows, 128)
        pair_vals = jnp.concatenate(
            [vals[:, :, cols].reshape(2 * rows, 128), jnp.ones((2 * rows, 128), b16)], axis=1)

        def step(i, carry):
            here = pl.ds(pl.multiple_of(i * q_tile, q_tile), q_tile)
            pair_q = queries[here, cols]
            mask = bias[here, :]
            halves = []
            for h in range(2):
                own = (lane < HD) if h == 0 else (lane >= HD)
                head_q = jnp.where(own, pair_q, jnp.zeros_like(pair_q))
                scores = lax.dot_general(
                    head_q, pair_keys, (((1,), (1,)), ((), ())), preferred_element_type=f32) + mask
                peak = jnp.max(scores, axis=-1, keepdims=True)
                weights = jnp.exp(scores - peak).astype(b16)
                mixed = jnp.dot(weights, pair_vals, preferred_element_type=f32)
                halves.append(mixed[:, :128] / mixed[:, 128:])
            att[m * pairs + p, here, :] = jnp.where(lane < HD, halves[0], halves[1]).astype(b16)
            return carry

        lax.fori_loop(0, rows // q_tile, step, 0)
        for k in range(shards - 1):
            a_copy(p, k).start()

    attend(0)
    second_hop(O)
    for p in range(1, pairs):
        attend(p)
    third_hop(O)
    first_hop(W)
    second_hop(U)
    third_hop(U)
    second_hop(W)
    finish(O)
    for p in range(pairs):
        for k in range(shards - 1):
            a_copy(p, k).wait_recv()

    n_wide = 256
    o_parts = n_wide // part
    joined = jnp.concatenate([att[i] for i in range(shards * pairs)], axis=1)

    def out_step(n, carry):
        block = full_o[pl.ds(n * o_parts, o_parts)].reshape(n_wide, width)
        sums[:, pl.ds(pl.multiple_of(n * n_wide, n_wide), n_wide)] = lax.dot_general(
            joined, block, (((1,), (1,)), ((), ())), preferred_element_type=f32)
        return carry

    lax.fori_loop(0, width // n_wide, out_step, 0)
    ln_tile = 64

    def ln_step(i, carry):
        here = pl.ds(pl.multiple_of(i * ln_tile, ln_tile), ln_tile)
        normed[here, :] = layer_norm(
            hid[here, :].astype(f32) + sums[here, :], gain1[...], shift1[...]).astype(b16)
        return carry

    lax.fori_loop(0, rows // ln_tile, ln_step, 0)
    third_hop(W)
    finish(U)

    def up_step(n, carry):
        here = pl.ds(pl.multiple_of(n * n_wide, n_wide), n_wide)
        pre = jnp.dot(
            normed[...], full_u[:, :, here].reshape(width, n_wide), preferred_element_type=f32)
        act[:, here] = (0.5 * pre * (1.0 + lax.erf(pre * (0.5 ** 0.5)))).astype(b16)
        return carry

    lax.fori_loop(0, lh // n_wide, up_step, 0)
    finish(W)
    d_parts = tile // part
    for n in range(tiles):
        block = full_d[n * d_parts:(n + 1) * d_parts].reshape(tile, lh)
        term = lax.dot_general(
            act[...], block, (((1,), (1,)), ((), ())), preferred_element_type=f32)
        rs_send[n] = term.astype(b16)
        for k in range(shards - 1):
            r_copy(n, k).start()
        sums[:, n * tile:(n + 1) * tile] = term
    own_rows = pl.ds(pl.multiple_of(m * share, share), share)
    for n in range(tiles):
        cols = slice(n * tile, (n + 1) * tile)
        total = normed[own_rows, cols].astype(f32) + sums[own_rows, cols]
        for k in range(shards - 1):
            r_copy(n, k).wait_recv()
            total = total + rs_recv[k, n].astype(f32)
        sums[0:share, cols] = total
    out[...] = layer_norm(sums[0:share, :], gain2[...], shift2[...]).astype(b16)

    for kind in (Q, O, U, W):
        for k in range(shards - 1):
            z_copy(kind, k).wait_send()
        for step in range(len(hops)):
            p_copy(kind, step).wait_send()
    kv_copy(keys, 0).wait_send()
    kv_copy(vals, 1).wait_send()
    for k in range(shards - 1):
        for p in range(pairs):
            a_copy(p, k).wait_send()
        for n in range(tiles):
            r_copy(n, k).wait_send()


def kernel_body(
    hidden_in, request_ids, w_qkv, w_out, w_up, w_down, ln1_gain, ln1_shift, ln2_gain, ln2_shift
):
    groups = lax.axis_size("group")
    shards = lax.axis_size("mp")
    rows, width = hidden_in.shape
    part = w_qkv.shape[0]
    parts = groups * shards
    lw = width // shards
    lh = w_up.shape[1] // shards
    share = rows // shards
    pairs = lw // 128
    tile = 256
    tiles = width // tile
    b16, f32 = jnp.bfloat16, jnp.float32
    vmem = pl.BlockSpec(memory_space=pltpu.VMEM)
    dma = pltpu.SemaphoreType.DMA
    others = shards - 1
    return pl.pallas_call(
        functools.partial(layer_kernel, shards),
        out_shape=(
            jax.ShapeDtypeStruct((share, width), b16),
            jax.ShapeDtypeStruct((rows, lw), b16),
            jax.ShapeDtypeStruct((rows, lw), b16),
        ),
        in_specs=[vmem] * 11,
        out_specs=(vmem,) * 3,
        scratch_shapes=[
            pltpu.VMEM((shards, part, 3 * lw), b16),
            pltpu.VMEM((1, part, width), b16),
            pltpu.VMEM((shards, part, lh), b16),
            pltpu.VMEM((shards, part, lh), b16),
            pltpu.VMEM((parts, part, 3 * lw), b16),
            pltpu.VMEM((parts, part, width), b16),
            pltpu.VMEM((parts, part, lh), b16),
            pltpu.VMEM((parts, part, lh), b16),
            pltpu.VMEM((rows, 2 * rows), f32),
            pltpu.VMEM((rows, lw), b16),
            pltpu.VMEM((2, rows, lw), b16),
            pltpu.VMEM((2, rows, lw), b16),
            pltpu.VMEM((shards * pairs, rows, 128), b16),
            pltpu.VMEM((rows, width), f32),
            pltpu.VMEM((rows, width), b16),
            pltpu.VMEM((rows, lh), b16),
            pltpu.VMEM((tiles, rows, tile), b16),
            pltpu.VMEM((others, tiles, share, tile), b16),
            dma((4, others)), dma((4, others)),
            dma((4, 7)), dma((4, 7)),
            dma((2,)), dma((2,)),
            dma((pairs, others)), dma((pairs, others)),
            dma((tiles, others)), dma((tiles, others)),
        ],
        compiler_params=pltpu.CompilerParams(
            collective_id=0, has_side_effects=True, vmem_limit_bytes=48 * 1024 * 1024),
        cost_estimate=pl.CostEstimate(
            flops=6 * rows * width * (4 * lw + 2 * lh), bytes_accessed=16 * 1024 * 1024,
            transcendentals=0),
        name="encoder_layer",
    )(
        hidden_in, request_ids.reshape(rows, 1), request_ids.reshape(1, rows),
        w_qkv, w_out, w_up, w_down,
        ln1_gain.reshape(1, width), ln1_shift.reshape(1, width),
        ln2_gain.reshape(1, width), ln2_shift.reshape(1, width),
    )


def solution(mesh):
    in_specs = (
        P("group", None),
        P("group"),
        P(("group", "mp"), None),
        P(("group", "mp"), None),
        P(("group", "mp"), None),
        P(("group", "mp"), None),
        P(),
        P(),
        P(),
        P(),
    )
    out_specs = (P(("group", "mp"), None), P("group", "mp"), P("group", "mp"))
    whole_tiles = mesh.shape["group"] == 8 and mesh.shape["mp"] == 4
    body = kernel_body if whole_tiles else plain_body
    return jax.shard_map(body, mesh=mesh, in_specs=in_specs, out_specs=out_specs, check_vma=False)
```

```python
import functools

import jax
import jax.numpy as jnp
from jax import lax
from jax.experimental import pallas as pl
from jax.experimental.pallas import tpu as pltpu
from jax.sharding import PartitionSpec as P

HD = 64
SHORT = 64


def swapped(value, axis, distance):
    return lax.ppermute(value, axis, [(i, i ^ 1 << distance) for i in range(lax.axis_size(axis))])


def layer_norm(values_in, norm_gain, norm_shift):
    center = values_in - jnp.mean(values_in, axis=-1, keepdims=True)
    spread = jnp.mean(center * center, axis=-1, keepdims=True)
    return center * lax.rsqrt(spread + 1e-05) * norm_gain + norm_shift


def plain_body(
    hidden_in, request_ids, w_qkv, w_out, w_up, w_down, ln1_gain, ln1_shift, ln2_gain, ln2_shift
):
    groups = lax.axis_size("group")
    shards = lax.axis_size("mp")
    model_width = hidden_in.shape[1]
    local_width = model_width // shards
    local_hidden = w_up.shape[1] // shards
    tok_rows = hidden_in.shape[0]
    part_rows = w_qkv.shape[0]
    pieces = (
        w_qkv.astype(jnp.bfloat16).reshape(part_rows, 3, shards, local_width),
        w_out.astype(jnp.bfloat16).reshape(part_rows, 1, shards, local_width),
        w_up.astype(jnp.bfloat16).reshape(part_rows, 1, shards, local_hidden),
        w_down.astype(jnp.bfloat16).reshape(part_rows, 1, shards, local_hidden),
    )
    gathered = (
        lax.all_gather(pieces[0], "group", axis=0, tiled=True),
        lax.all_gather(pieces[1], "group", axis=0, tiled=True),
        lax.all_gather(pieces[2], "group", axis=0, tiled=True),
        lax.all_gather(pieces[3], "group", axis=0, tiled=True),
    )
    exchanged = (
        lax.all_to_all(gathered[0], "mp", split_axis=2, concat_axis=0, tiled=True),
        lax.all_to_all(gathered[1], "mp", split_axis=2, concat_axis=0, tiled=True),
        lax.all_to_all(gathered[2], "mp", split_axis=2, concat_axis=0, tiled=True),
        lax.all_to_all(gathered[3], "mp", split_axis=2, concat_axis=0, tiled=True),
    )
    served = tuple(
        (
            jnp.transpose(
                weight_piece.reshape(shards, groups, part_rows, -1), (1, 0, 2, 3)
            ).reshape(model_width, -1)
            for weight_piece in exchanged
        )
    )
    qkv_local, out_local, up_local, down_local = served
    projected = jnp.dot(hidden_in, qkv_local, preferred_element_type=jnp.float32)
    queries = projected[:, :local_width].astype(jnp.bfloat16)
    key_rows = projected[:, local_width : 2 * local_width].astype(jnp.bfloat16)
    value_rows = projected[:, 2 * local_width :].astype(jnp.bfloat16)
    partner_keys, partner_values = swapped((key_rows, value_rows), "group", 0)
    group_index = lax.axis_index("group")
    parity = group_index % 2
    long_id = jnp.where(parity == 0, request_ids[-1], request_ids[0])
    own_long = request_ids == long_id
    local_heads = local_width // HD
    score_scale = HD ** (-0.5)
    block_total = tok_rows // SHORT
    short_q = queries.reshape(block_total, SHORT, local_heads, HD)
    short_k = key_rows.reshape(block_total, SHORT, local_heads, HD)
    short_v = value_rows.reshape(block_total, SHORT, local_heads, HD)
    short_ids = request_ids.reshape(block_total, SHORT)
    short_scores = (
        jnp.einsum("bqhd,bkhd->bhqk", short_q, short_k, preferred_element_type=jnp.float32)
        * score_scale
    )
    short_mask = short_ids[:, :, None] == short_ids[:, None, :]
    short_scores = jnp.where(short_mask[:, None], short_scores, -1e30)
    short_peak = jnp.max(short_scores, axis=-1, keepdims=True)
    short_weights = jnp.exp(short_scores - short_peak).astype(jnp.bfloat16)
    short_totals = jnp.sum(short_weights.astype(jnp.float32), axis=-1)
    short_mixed = jnp.einsum(
        "bhqk,bkhd->bqhd", short_weights, short_v, preferred_element_type=jnp.float32
    )
    short_out = (
        (short_mixed / jnp.transpose(short_totals, (0, 2, 1))[:, :, :, None])
        .astype(jnp.bfloat16)
        .reshape(tok_rows, local_width)
    )
    first_keys = jnp.where(parity == 0, key_rows, partner_keys)
    second_keys = jnp.where(parity == 0, partner_keys, key_rows)
    first_values = jnp.where(parity == 0, value_rows, partner_values)
    second_values = jnp.where(parity == 0, partner_values, value_rows)
    pair_base = (group_index - parity) * tok_rows
    span_start = long_id - tok_rows + 1 - pair_base
    long_keys = lax.dynamic_slice_in_dim(
        jnp.concatenate([first_keys, second_keys], 0), span_start, tok_rows, 0
    ).reshape(tok_rows, local_heads, HD)
    long_values = lax.dynamic_slice_in_dim(
        jnp.concatenate([first_values, second_values], 0), span_start, tok_rows, 0
    ).reshape(tok_rows, local_heads, HD)
    query_rows = min(512, tok_rows)
    query_blocks = tok_rows // query_rows

    def long_attend(block_queries):
        heads_view = block_queries.reshape(query_rows, local_heads, HD)
        scores = (
            jnp.einsum("qhd,khd->hqk", heads_view, long_keys, preferred_element_type=jnp.float32)
            * score_scale
        )
        row_peak = jnp.max(scores, axis=-1, keepdims=True)
        weights = jnp.exp(scores - row_peak).astype(jnp.bfloat16)
        totals = jnp.sum(weights.astype(jnp.float32), axis=-1)
        mixed_heads = jnp.einsum(
            "hqk,khd->qhd", weights, long_values, preferred_element_type=jnp.float32
        )
        return (
            (mixed_heads / jnp.transpose(totals)[:, :, None])
            .astype(jnp.bfloat16)
            .reshape(query_rows, local_width)
        )

    def skipped(block_queries):
        return jnp.zeros((query_rows, local_width), jnp.bfloat16)

    def long_block(query_block):
        block_queries, block_long = query_block
        return lax.cond(jnp.any(block_long), long_attend, skipped, block_queries)

    long_out = lax.map(
        long_block,
        (
            queries.reshape(query_blocks, query_rows, local_width),
            own_long.reshape(query_blocks, query_rows),
        ),
    ).reshape(tok_rows, local_width)
    attended = jnp.where(own_long[:, None], long_out, short_out)
    share_rows = tok_rows // shards
    row_start = lax.axis_index("mp") * share_rows

    def combine(term_fn, residual, norm_gain, norm_shift):
        summed = lax.psum(term_fn(0, tok_rows), "mp")
        whole_rows = layer_norm(
            residual.astype(jnp.float32) + summed, norm_gain, norm_shift
        ).astype(jnp.bfloat16)
        normed = lax.dynamic_slice_in_dim(whole_rows, row_start, share_rows, 0)
        return (normed, whole_rows)

    def attn_term(row_begin, row_count):
        return lax.dot_general(
            attended, out_local, (((1,), (1,)), ((), ())), preferred_element_type=jnp.float32
        )

    attn_share, attn_normed = combine(attn_term, hidden_in, ln1_gain, ln1_shift)
    activated = jax.nn.gelu(
        jnp.dot(attn_normed, up_local, preferred_element_type=jnp.float32), approximate=False
    ).astype(jnp.bfloat16)

    def feed_term(row_begin, row_count):
        return lax.dot_general(
            activated, down_local, (((1,), (1,)), ((), ())), preferred_element_type=jnp.float32
        )

    final_share, unused = combine(feed_term, attn_normed, ln2_gain, ln2_shift)
    return (final_share, key_rows, value_rows)


MESH = pl.DeviceIdType.MESH
Q, O, U, W = range(4)


def layer_kernel(
    shards, hid_in, id_col, id_row, w_qkv_in, w_out_in, w_up_in, w_down_in,
    gain1, shift1, gain2, shift2,
    out, k_out, v_out,
    hid, w_qkv, w_out, w_up, w_down,
    stage_q, stage_o, stage_u, stage_d, full_q, full_o, full_u, full_d,
    bias, queries, keys, vals, att, att_in, sums, normed, act, rs_send, rs_recv,
    in_sem, z_send, z_recv, p_send, p_recv, kv_send, kv_recv, a_send, a_recv,
    n_send, n_recv, r_send, r_recv,
):
    g = lax.axis_index("group")
    m = lax.axis_index("mp")
    core = lax.rem(g, 2)
    x = lax.rem(g // 2, 2)
    y = g // 4
    half = m // 2
    side = lax.rem(m, 2)
    sib = g + 1 - 2 * core
    gx = g + 2 - 4 * x
    gy = g + 4 - 8 * y
    gd = gx + gy - g
    m1 = m + 1 - 2 * side
    m2 = m + 2 - 4 * half
    rows = hid.shape[0]
    width = hid.shape[1]
    part = w_qkv.shape[0]
    lw = queries.shape[1]
    lh = act.shape[1]
    pairs = lw // 128
    share = rows // shards
    f32, b16 = jnp.float32, jnp.bfloat16
    fulls = (full_q, full_o, full_u, full_d)
    stages = (stage_q, stage_o, stage_u, stage_d)
    peers = [lax.rem(m + k, shards) for k in range(1, shards)]
    spot = 2 * x + side
    square = ((g, m1), (gx, m), (gx, m1))
    square_spot = (2 * x + 1 - side, 2 - 2 * x + side, 3 - 2 * x - side)

    def block_at(on_y, on_core, on_half):
        return (on_y * 2 + on_core) * 2 + on_half

    mine = (g * shards + m,) * 2 + (block_at(y, core, half) * 4 + spot,) * 2

    def z_copy(kind, k):
        if kind == Q:
            chunk, target = stage_q.at[peers[k]], (g, peers[k])
        elif kind == O:
            chunk, target = stage_o.at[0], (g, peers[k])
        else:
            chunk, target = stages[kind].at[square_spot[k]], square[k]
        return pltpu.make_async_remote_copy(
            src_ref=chunk, dst_ref=fulls[kind].at[mine[kind]],
            send_sem=z_send.at[kind, k], recv_sem=z_recv.at[kind, k],
            device_id=target, device_id_type=MESH)

    fwd_to = gy * (1 - core) + gx * core
    fwd_block = gx * (1 - core) + gy * core
    plane_hops = (
        (g, (gx, m)), (g, (gy, m)), (fwd_block, (fwd_to, m)),
        (g, (sib, m)), (gx, (sib, m)), (gy, (sib, m)), (gd, (sib, m)))
    b_own = block_at(y, core, half)
    b_z = block_at(y, core, 1 - half)
    b_y = block_at(1 - y, core, half)
    b_d = block_at(1 - y, core, 1 - half)
    hidden_hops = (
        (b_own, (g, m2)), (b_own, (gy, m)), (b_z, (gy, m)),
        (b_own, (sib, m)), (b_z, (sib, m)), (b_y, (sib, m)), (b_d, (sib, m)))

    def p_copy(kind, step):
        block, target = (plane_hops if kind in (Q, O) else hidden_hops)[step]
        place = fulls[kind].at[pl.ds(block * 4, 4)]
        return pltpu.make_async_remote_copy(
            src_ref=place, dst_ref=place,
            send_sem=p_send.at[kind, step], recv_sem=p_recv.at[kind, step],
            device_id=target, device_id_type=MESH)

    def arrived(kind):
        for k in range(shards - 1):
            z_copy(kind, k).wait_recv()

    def go(kind, *steps):
        for step in steps:
            p_copy(kind, step).start()

    def landed(kind, *steps):
        for step in steps:
            p_copy(kind, step).wait_recv()

    def kv_copy(buf, i):
        return pltpu.make_async_remote_copy(
            src_ref=buf.at[0], dst_ref=buf.at[1],
            send_sem=kv_send.at[i], recv_sem=kv_recv.at[i],
            device_id=(sib, m), device_id_type=MESH)

    def a_copy(p, k):
        return pltpu.make_async_remote_copy(
            src_ref=att.at[p, pl.ds(pl.multiple_of(peers[k] * share, share), share)],
            dst_ref=att_in.at[m * pairs + p],
            send_sem=a_send.at[p, k], recv_sem=a_recv.at[p, k],
            device_id=(g, peers[k]), device_id_type=MESH)

    def n_copy(k):
        return pltpu.make_async_remote_copy(
            src_ref=normed.at[spot], dst_ref=normed.at[spot],
            send_sem=n_send.at[k], recv_sem=n_recv.at[k],
            device_id=square[k], device_id_type=MESH)

    tiles = rs_send.shape[0]
    tile = rs_send.shape[2]

    def r_copy(n, k):
        return pltpu.make_async_remote_copy(
            src_ref=rs_send.at[n, pl.ds(pl.multiple_of(square_spot[k] * share, share), share)],
            dst_ref=rs_recv.at[k, n],
            send_sem=r_send.at[n, k], recv_sem=r_recv.at[n, k],
            device_id=square[k], device_id_type=MESH)

    loads = [
        pltpu.make_async_copy(far, near, in_sem.at[i])
        for i, (far, near) in enumerate((
            (w_qkv_in, w_qkv), (w_out_in, w_out), (w_up_in, w_up), (w_down_in, w_down),
            (hid_in, hid)))
    ]

    def stage(kind):
        loads[kind].wait()
        if kind == Q:
            for d in range(shards):
                for j in range(3):
                    stage_q[d, :, j * lw:(j + 1) * lw] = w_qkv[
                        :, j * width + d * lw:j * width + (d + 1) * lw].astype(b16)
        elif kind == O:
            stage_o[0] = w_out[...].astype(b16)
        else:
            source = w_up if kind == U else w_down
            for d in range(shards):
                stages[kind][d] = source[:, d * lh:(d + 1) * lh].astype(b16)
        fulls[kind][mine[kind]] = stages[kind][(m, 0, spot, spot)[kind]]

    barrier = pltpu.get_barrier_semaphore()
    everyone = [(g, peer) for peer in peers] + [(gx, m), (gy, m), (sib, m), (gx, m1)]
    for target in everyone:
        pl.semaphore_signal(barrier, inc=1, device_id=target, device_id_type=MESH)
    for load in loads:
        load.start()
    stage(Q)
    pl.semaphore_wait(barrier, len(everyone))
    for kind in (Q, U, O, W):
        if kind != Q:
            stage(kind)
        for k in range(shards - 1):
            z_copy(kind, k).start()

    long_id = jnp.where(core == 0, id_col[rows - 1:rows, :], id_col[0:1, :])
    bias[:, :rows] = jnp.where(id_col[...] == id_row[...], 0.0, -1e30).astype(f32)
    slot = sib * rows + lax.broadcasted_iota(jnp.int32, (1, rows), 1)
    reach = jnp.where((slot > long_id - rows) & (slot <= long_id), long_id, -1)
    bias[:, rows:] = jnp.where(id_col[...] == reach, 0.0, -1e30).astype(f32)

    arrived(Q)
    go(Q, 0, 1, 3)
    arrived(U)
    go(U, 0)
    loads[4].wait()
    landed(Q, 0, 1)
    go(Q, 2, 4, 5)
    arrived(O)
    go(O, 0, 1, 3)
    arrived(W)
    go(W, 0)
    landed(Q, 2)
    go(Q, 6)
    landed(Q, 3, 4, 5, 6)

    def project(j):
        return jnp.dot(
            hid[...], full_q[:, :, j * lw:(j + 1) * lw].reshape(width, lw),
            preferred_element_type=f32).astype(b16)

    key_rows = project(1)
    keys[0] = key_rows
    kv_copy(keys, 0).start()
    k_out[...] = key_rows
    value_rows = project(2)
    vals[0] = value_rows
    kv_copy(vals, 1).start()
    v_out[...] = value_rows
    queries[...] = project(0) * jnp.asarray(HD ** -0.5, b16)
    go(U, 1, 3)
    kv_copy(keys, 0).wait_recv()
    kv_copy(vals, 1).wait_recv()

    q_tile = min(128, rows)
    lane = lax.broadcasted_iota(jnp.int32, (q_tile, 128), 1)
    own_rows = pl.ds(pl.multiple_of(m * share, share), share)

    def attend(p):
        cols = slice(p * 128, (p + 1) * 128)
        pair_keys = keys[:, :, cols].reshape(2 * rows, 128)
        pair_vals = jnp.concatenate(
            [vals[:, :, cols].reshape(2 * rows, 128), jnp.ones((2 * rows, 128), b16)], axis=1)

        def step(i, carry):
            here = pl.ds(pl.multiple_of(i * q_tile, q_tile), q_tile)
            pair_q = queries[here, cols]
            mask = bias[here, :]
            halves = []
            for h in range(2):
                own = (lane < HD) if h == 0 else (lane >= HD)
                head_q = jnp.where(own, pair_q, jnp.zeros_like(pair_q))
                scores = lax.dot_general(
                    head_q, pair_keys, (((1,), (1,)), ((), ())), preferred_element_type=f32) + mask
                peak = jnp.max(scores, axis=-1, keepdims=True)
                weights = jnp.exp(scores - peak).astype(b16)
                mixed = jnp.dot(weights, pair_vals, preferred_element_type=f32)
                halves.append(mixed[:, :128] / mixed[:, 128:])
            att[p, here, :] = jnp.where(lane < HD, halves[0], halves[1]).astype(b16)
            return carry

        lax.fori_loop(0, rows // q_tile, step, 0)
        for k in range(shards - 1):
            a_copy(p, k).start()
        att_in[m * pairs + p] = att[p, own_rows, :]

    attend(0)
    landed(O, 0, 1)
    go(O, 2, 4, 5)
    for p in range(1, pairs):
        attend(p)
    landed(O, 2)
    go(O, 6)
    go(W, 1, 3)
    landed(U, 0, 1)
    go(U, 2, 4, 5)
    landed(O, 3, 4, 5, 6)
    for p in range(pairs):
        for k in range(shards - 1):
            a_copy(p, k).wait_recv()

    n_wide = 256
    o_parts = n_wide // part
    joined = jnp.concatenate([att_in[i] for i in range(shards * pairs)], axis=1)

    for n in range(width // n_wide):
        block = full_o[n * o_parts:(n + 1) * o_parts].reshape(n_wide, width)
        sums[0:share, n * n_wide:(n + 1) * n_wide] = lax.dot_general(
            joined, block, (((1,), (1,)), ((), ())), preferred_element_type=f32)
    normed[spot] = layer_norm(
        hid[own_rows, :].astype(f32) + sums[0:share, :], gain1[...], shift1[...]).astype(b16)
    for k in range(3):
        n_copy(k).start()
    landed(U, 2)
    go(U, 6)
    landed(W, 0, 1)
    go(W, 2, 4, 5)
    landed(U, 3, 4, 5, 6)
    for k in range(3):
        n_copy(k).wait_recv()

    order = []
    for r in range(8 * shards):
        group_r, z_r = r // shards, r % shards
        order.append(((group_r // 4 * 2 + group_r % 2) * 2 + z_r // 2) * 4
                     + group_r // 2 % 2 * 2 + z_r % 2)
    tokens = normed[...].reshape(rows, width)

    def up_step(n, carry):
        here = pl.ds(pl.multiple_of(n * n_wide, n_wide), n_wide)
        block = jnp.concatenate([full_u[r, :, here] for r in order], axis=0)
        pre = jnp.dot(tokens, block, preferred_element_type=f32)
        act[:, here] = (0.5 * pre * (1.0 + lax.erf(pre * (0.5 ** 0.5)))).astype(b16)
        return carry

    lax.fori_loop(0, lh // n_wide, up_step, 0)
    landed(W, 2)
    go(W, 6)
    landed(W, 3, 4, 5, 6)
    d_parts = tile // part
    for n in range(tiles):
        block = jnp.concatenate(
            [full_d[r] for r in order[n * d_parts:(n + 1) * d_parts]], axis=0)
        term = lax.dot_general(
            act[...], block, (((1,), (1,)), ((), ())), preferred_element_type=f32)
        rs_send[n] = term.astype(b16)
        for k in range(3):
            r_copy(n, k).start()
        sums[:, n * tile:(n + 1) * tile] = term
    spot_rows = pl.ds(pl.multiple_of(spot * share, share), share)
    for n in range(tiles):
        cols = slice(n * tile, (n + 1) * tile)
        total = normed[spot, :, cols].astype(f32) + sums[spot_rows, cols]
        for k in range(3):
            r_copy(n, k).wait_recv()
            total = total + rs_recv[k, n].astype(f32)
        sums[0:share, cols] = total
    out[...] = layer_norm(sums[0:share, :], gain2[...], shift2[...]).astype(b16)

    for kind in (Q, O, U, W):
        for k in range(shards - 1):
            z_copy(kind, k).wait_send()
        for step in range(7):
            p_copy(kind, step).wait_send()
    kv_copy(keys, 0).wait_send()
    kv_copy(vals, 1).wait_send()
    for k in range(shards - 1):
        n_copy(k).wait_send()
        for p in range(pairs):
            a_copy(p, k).wait_send()
        for n in range(tiles):
            r_copy(n, k).wait_send()


def kernel_body(
    hidden_in, request_ids, w_qkv, w_out, w_up, w_down, ln1_gain, ln1_shift, ln2_gain, ln2_shift
):
    groups = lax.axis_size("group")
    shards = lax.axis_size("mp")
    rows, width = hidden_in.shape
    part = w_qkv.shape[0]
    parts = groups * shards
    lw = width // shards
    lh = w_up.shape[1] // shards
    share = rows // shards
    pairs = lw // 128
    tile = 256
    tiles = width // tile
    b16, f32 = jnp.bfloat16, jnp.float32
    vmem = pl.BlockSpec(memory_space=pltpu.VMEM)
    hbm = pl.BlockSpec(memory_space=pl.ANY)
    dma = pltpu.SemaphoreType.DMA
    others = shards - 1
    return pl.pallas_call(
        functools.partial(layer_kernel, shards),
        out_shape=(
            jax.ShapeDtypeStruct((share, width), b16),
            jax.ShapeDtypeStruct((rows, lw), b16),
            jax.ShapeDtypeStruct((rows, lw), b16),
        ),
        in_specs=[hbm] + [vmem] * 2 + [hbm] * 4 + [vmem] * 4,
        out_specs=(vmem,) * 3,
        scratch_shapes=[
            pltpu.VMEM((rows, width), b16),
            pltpu.VMEM(w_qkv.shape, f32),
            pltpu.VMEM(w_out.shape, f32),
            pltpu.VMEM(w_up.shape, f32),
            pltpu.VMEM(w_down.shape, f32),
            pltpu.VMEM((shards, part, 3 * lw), b16),
            pltpu.VMEM((1, part, width), b16),
            pltpu.VMEM((shards, part, lh), b16),
            pltpu.VMEM((shards, part, lh), b16),
            pltpu.VMEM((parts, part, 3 * lw), b16),
            pltpu.VMEM((parts, part, width), b16),
            pltpu.VMEM((parts, part, lh), b16),
            pltpu.VMEM((parts, part, lh), b16),
            pltpu.VMEM((rows, 2 * rows), f32),
            pltpu.VMEM((rows, lw), b16),
            pltpu.VMEM((2, rows, lw), b16),
            pltpu.VMEM((2, rows, lw), b16),
            pltpu.VMEM((pairs, rows, 128), b16),
            pltpu.VMEM((shards * pairs, share, 128), b16),
            pltpu.VMEM((rows, width), f32),
            pltpu.VMEM((shards, share, width), b16),
            pltpu.VMEM((rows, lh), b16),
            pltpu.VMEM((tiles, rows, tile), b16),
            pltpu.VMEM((others, tiles, share, tile), b16),
            dma((5,)),
            dma((4, others)), dma((4, others)),
            dma((4, 7)), dma((4, 7)),
            dma((2,)), dma((2,)),
            dma((pairs, others)), dma((pairs, others)),
            dma((others,)), dma((others,)),
            dma((tiles, others)), dma((tiles, others)),
        ],
        compiler_params=pltpu.CompilerParams(
            collective_id=0, has_side_effects=True, vmem_limit_bytes=48 * 1024 * 1024),
        cost_estimate=pl.CostEstimate(
            flops=6 * rows * width * (4 * lw + 2 * lh), bytes_accessed=16 * 1024 * 1024,
            transcendentals=0),
        name="encoder_layer",
    )(
        hidden_in, request_ids.reshape(rows, 1), request_ids.reshape(1, rows),
        w_qkv, w_out, w_up, w_down,
        ln1_gain.reshape(1, width), ln1_shift.reshape(1, width),
        ln2_gain.reshape(1, width), ln2_shift.reshape(1, width),
    )


def solution(mesh):
    in_specs = (
        P("group", None),
        P("group"),
        P(("group", "mp"), None),
        P(("group", "mp"), None),
        P(("group", "mp"), None),
        P(("group", "mp"), None),
        P(),
        P(),
        P(),
        P(),
    )
    out_specs = (P(("group", "mp"), None), P("group", "mp"), P("group", "mp"))
    whole_tiles = mesh.shape["group"] == 8 and mesh.shape["mp"] == 4
    body = kernel_body if whole_tiles else plain_body
    return jax.shard_map(body, mesh=mesh, in_specs=in_specs, out_specs=out_specs, check_vma=False)
```

```python
import functools

import jax
import jax.numpy as jnp
from jax import lax
from jax.experimental import pallas as pl
from jax.experimental.pallas import tpu as pltpu
from jax.sharding import PartitionSpec as P

HD = 64
SHORT = 64


def swapped(value, axis, distance):
    return lax.ppermute(value, axis, [(i, i ^ 1 << distance) for i in range(lax.axis_size(axis))])


def layer_norm(values_in, norm_gain, norm_shift):
    center = values_in - jnp.mean(values_in, axis=-1, keepdims=True)
    spread = jnp.mean(center * center, axis=-1, keepdims=True)
    return center * lax.rsqrt(spread + 1e-05) * norm_gain + norm_shift


def plain_body(
    hidden_in, request_ids, w_qkv, w_out, w_up, w_down, ln1_gain, ln1_shift, ln2_gain, ln2_shift
):
    groups = lax.axis_size("group")
    shards = lax.axis_size("mp")
    model_width = hidden_in.shape[1]
    local_width = model_width // shards
    local_hidden = w_up.shape[1] // shards
    tok_rows = hidden_in.shape[0]
    part_rows = w_qkv.shape[0]
    pieces = (
        w_qkv.astype(jnp.bfloat16).reshape(part_rows, 3, shards, local_width),
        w_out.astype(jnp.bfloat16).reshape(part_rows, 1, shards, local_width),
        w_up.astype(jnp.bfloat16).reshape(part_rows, 1, shards, local_hidden),
        w_down.astype(jnp.bfloat16).reshape(part_rows, 1, shards, local_hidden),
    )
    gathered = (
        lax.all_gather(pieces[0], "group", axis=0, tiled=True),
        lax.all_gather(pieces[1], "group", axis=0, tiled=True),
        lax.all_gather(pieces[2], "group", axis=0, tiled=True),
        lax.all_gather(pieces[3], "group", axis=0, tiled=True),
    )
    exchanged = (
        lax.all_to_all(gathered[0], "mp", split_axis=2, concat_axis=0, tiled=True),
        lax.all_to_all(gathered[1], "mp", split_axis=2, concat_axis=0, tiled=True),
        lax.all_to_all(gathered[2], "mp", split_axis=2, concat_axis=0, tiled=True),
        lax.all_to_all(gathered[3], "mp", split_axis=2, concat_axis=0, tiled=True),
    )
    served = tuple(
        (
            jnp.transpose(
                weight_piece.reshape(shards, groups, part_rows, -1), (1, 0, 2, 3)
            ).reshape(model_width, -1)
            for weight_piece in exchanged
        )
    )
    qkv_local, out_local, up_local, down_local = served
    projected = jnp.dot(hidden_in, qkv_local, preferred_element_type=jnp.float32)
    queries = projected[:, :local_width].astype(jnp.bfloat16)
    key_rows = projected[:, local_width : 2 * local_width].astype(jnp.bfloat16)
    value_rows = projected[:, 2 * local_width :].astype(jnp.bfloat16)
    partner_keys, partner_values = swapped((key_rows, value_rows), "group", 0)
    group_index = lax.axis_index("group")
    parity = group_index % 2
    long_id = jnp.where(parity == 0, request_ids[-1], request_ids[0])
    own_long = request_ids == long_id
    local_heads = local_width // HD
    score_scale = HD ** (-0.5)
    block_total = tok_rows // SHORT
    short_q = queries.reshape(block_total, SHORT, local_heads, HD)
    short_k = key_rows.reshape(block_total, SHORT, local_heads, HD)
    short_v = value_rows.reshape(block_total, SHORT, local_heads, HD)
    short_ids = request_ids.reshape(block_total, SHORT)
    short_scores = (
        jnp.einsum("bqhd,bkhd->bhqk", short_q, short_k, preferred_element_type=jnp.float32)
        * score_scale
    )
    short_mask = short_ids[:, :, None] == short_ids[:, None, :]
    short_scores = jnp.where(short_mask[:, None], short_scores, -1e30)
    short_peak = jnp.max(short_scores, axis=-1, keepdims=True)
    short_weights = jnp.exp(short_scores - short_peak).astype(jnp.bfloat16)
    short_totals = jnp.sum(short_weights.astype(jnp.float32), axis=-1)
    short_mixed = jnp.einsum(
        "bhqk,bkhd->bqhd", short_weights, short_v, preferred_element_type=jnp.float32
    )
    short_out = (
        (short_mixed / jnp.transpose(short_totals, (0, 2, 1))[:, :, :, None])
        .astype(jnp.bfloat16)
        .reshape(tok_rows, local_width)
    )
    first_keys = jnp.where(parity == 0, key_rows, partner_keys)
    second_keys = jnp.where(parity == 0, partner_keys, key_rows)
    first_values = jnp.where(parity == 0, value_rows, partner_values)
    second_values = jnp.where(parity == 0, partner_values, value_rows)
    pair_base = (group_index - parity) * tok_rows
    span_start = long_id - tok_rows + 1 - pair_base
    long_keys = lax.dynamic_slice_in_dim(
        jnp.concatenate([first_keys, second_keys], 0), span_start, tok_rows, 0
    ).reshape(tok_rows, local_heads, HD)
    long_values = lax.dynamic_slice_in_dim(
        jnp.concatenate([first_values, second_values], 0), span_start, tok_rows, 0
    ).reshape(tok_rows, local_heads, HD)
    query_rows = min(512, tok_rows)
    query_blocks = tok_rows // query_rows

    def long_attend(block_queries):
        heads_view = block_queries.reshape(query_rows, local_heads, HD)
        scores = (
            jnp.einsum("qhd,khd->hqk", heads_view, long_keys, preferred_element_type=jnp.float32)
            * score_scale
        )
        row_peak = jnp.max(scores, axis=-1, keepdims=True)
        weights = jnp.exp(scores - row_peak).astype(jnp.bfloat16)
        totals = jnp.sum(weights.astype(jnp.float32), axis=-1)
        mixed_heads = jnp.einsum(
            "hqk,khd->qhd", weights, long_values, preferred_element_type=jnp.float32
        )
        return (
            (mixed_heads / jnp.transpose(totals)[:, :, None])
            .astype(jnp.bfloat16)
            .reshape(query_rows, local_width)
        )

    def skipped(block_queries):
        return jnp.zeros((query_rows, local_width), jnp.bfloat16)

    def long_block(query_block):
        block_queries, block_long = query_block
        return lax.cond(jnp.any(block_long), long_attend, skipped, block_queries)

    long_out = lax.map(
        long_block,
        (
            queries.reshape(query_blocks, query_rows, local_width),
            own_long.reshape(query_blocks, query_rows),
        ),
    ).reshape(tok_rows, local_width)
    attended = jnp.where(own_long[:, None], long_out, short_out)
    share_rows = tok_rows // shards
    row_start = lax.axis_index("mp") * share_rows

    def combine(term_fn, residual, norm_gain, norm_shift):
        summed = lax.psum(term_fn(0, tok_rows), "mp")
        whole_rows = layer_norm(
            residual.astype(jnp.float32) + summed, norm_gain, norm_shift
        ).astype(jnp.bfloat16)
        normed = lax.dynamic_slice_in_dim(whole_rows, row_start, share_rows, 0)
        return (normed, whole_rows)

    def attn_term(row_begin, row_count):
        return lax.dot_general(
            attended, out_local, (((1,), (1,)), ((), ())), preferred_element_type=jnp.float32
        )

    attn_share, attn_normed = combine(attn_term, hidden_in, ln1_gain, ln1_shift)
    activated = jax.nn.gelu(
        jnp.dot(attn_normed, up_local, preferred_element_type=jnp.float32), approximate=False
    ).astype(jnp.bfloat16)

    def feed_term(row_begin, row_count):
        return lax.dot_general(
            activated, down_local, (((1,), (1,)), ((), ())), preferred_element_type=jnp.float32
        )

    final_share, unused = combine(feed_term, attn_normed, ln2_gain, ln2_shift)
    return (final_share, key_rows, value_rows)


MESH = pl.DeviceIdType.MESH
Q, O, U, W = range(4)


def layer_kernel(
    shards, hid_in, id_col, id_row, w_qkv_in, w_out_in, w_up_in, w_down_in,
    gain1, shift1, gain2, shift2,
    out, k_out, v_out,
    hid, w_qkv, w_out, w_up, w_down,
    stage_q, stage_o, stage_u, stage_d, full_q, full_o, full_u, full_d,
    bias, queries, keys, vals, att, att_in, sums, normed, act, rs_send, rs_recv,
    in_sem, z_send, z_recv, p_send, p_recv, kv_send, kv_recv, a_send, a_recv,
    n_send, n_recv, r_send, r_recv,
):
    g = lax.axis_index("group")
    m = lax.axis_index("mp")
    core = lax.rem(g, 2)
    x = lax.rem(g // 2, 2)
    y = g // 4
    half = m // 2
    side = lax.rem(m, 2)
    sib = g + 1 - 2 * core
    gx = g + 2 - 4 * x
    gy = g + 4 - 8 * y
    gd = gx + gy - g
    m1 = m + 1 - 2 * side
    m2 = m + 2 - 4 * half
    rows = hid.shape[0]
    width = hid.shape[1]
    part = w_qkv.shape[0]
    lw = queries.shape[1]
    lh = act.shape[2]
    pairs = lw // 128
    share = rows // shards
    f32, b16 = jnp.float32, jnp.bfloat16
    fulls = (full_q, full_o, full_u, full_d)
    stages = (stage_q, stage_o, stage_u, stage_d)
    peers = [lax.rem(m + k, shards) for k in range(1, shards)]
    spot = 2 * x + side
    square = ((g, m1), (gx, m), (gx, m1))
    square_spot = (2 * x + 1 - side, 2 - 2 * x + side, 3 - 2 * x - side)

    def block_at(on_y, on_core, on_half):
        return (on_y * 2 + on_core) * 2 + on_half

    mine = (g * shards + m,) * 2 + (block_at(y, core, half) * 4 + spot,) * 2

    def z_copy(kind, k):
        if kind == Q:
            chunk, target = stage_q.at[peers[k]], (g, peers[k])
        elif kind == O:
            chunk, target = stage_o.at[0], (g, peers[k])
        else:
            chunk, target = stages[kind].at[square_spot[k]], square[k]
        return pltpu.make_async_remote_copy(
            src_ref=chunk, dst_ref=fulls[kind].at[mine[kind]],
            send_sem=z_send.at[kind, k], recv_sem=z_recv.at[kind, k],
            device_id=target, device_id_type=MESH)

    plane_hops = (
        (g, (gx, m)), (g, (gy, m)), (gy, (gx, m)),
        (g, (sib, m)), (gx, (sib, m)), (gy, (sib, m)), (gd, (sib, m)))
    b_own = block_at(y, core, half)
    b_z = block_at(y, core, 1 - half)
    b_y = block_at(1 - y, core, half)
    b_d = block_at(1 - y, core, 1 - half)
    hidden_hops = (
        (b_own, (g, m2)), (b_own, (gy, m)), (b_z, (gy, m)),
        (b_own, (sib, m)), (b_z, (sib, m)), (b_y, (sib, m)), (b_d, (sib, m)))

    def p_copy(kind, step):
        block, target = (plane_hops if kind in (Q, O) else hidden_hops)[step]
        place = fulls[kind].at[pl.ds(block * 4, 4)]
        return pltpu.make_async_remote_copy(
            src_ref=place, dst_ref=place,
            send_sem=p_send.at[kind, step], recv_sem=p_recv.at[kind, step],
            device_id=target, device_id_type=MESH)

    def arrived(kind):
        for k in range(shards - 1):
            z_copy(kind, k).wait_recv()

    def go(kind, *steps):
        for step in steps:
            p_copy(kind, step).start()

    def landed(kind, *steps):
        for step in steps:
            p_copy(kind, step).wait_recv()

    def kv_copy(buf, i):
        return pltpu.make_async_remote_copy(
            src_ref=buf.at[0], dst_ref=buf.at[1],
            send_sem=kv_send.at[i], recv_sem=kv_recv.at[i],
            device_id=(sib, m), device_id_type=MESH)

    def a_copy(p, k):
        return pltpu.make_async_remote_copy(
            src_ref=att.at[p, k],
            dst_ref=att_in.at[m * pairs + p],
            send_sem=a_send.at[p, k], recv_sem=a_recv.at[p, k],
            device_id=(g, peers[k]), device_id_type=MESH)

    def n_copy(k):
        return pltpu.make_async_remote_copy(
            src_ref=normed.at[spot], dst_ref=normed.at[spot],
            send_sem=n_send.at[k], recv_sem=n_recv.at[k],
            device_id=square[k], device_id_type=MESH)

    tiles = rs_send.shape[1]
    tile = rs_send.shape[3]

    def r_copy(n, k):
        return pltpu.make_async_remote_copy(
            src_ref=rs_send.at[k, n],
            dst_ref=rs_recv.at[k, n],
            send_sem=r_send.at[n, k], recv_sem=r_recv.at[n, k],
            device_id=square[k], device_id_type=MESH)

    loads = [
        pltpu.make_async_copy(far, near, in_sem.at[i])
        for i, (far, near) in enumerate((
            (w_qkv_in, w_qkv), (w_out_in, w_out), (w_up_in, w_up), (w_down_in, w_down),
            (hid_in, hid)))
    ]

    def stage(kind):
        loads[kind].wait()
        if kind == Q:
            for d in range(shards):
                for j in range(3):
                    stage_q[d, :, j * lw:(j + 1) * lw] = w_qkv[
                        :, j * width + d * lw:j * width + (d + 1) * lw].astype(b16)
        elif kind == O:
            stage_o[0] = w_out[...].astype(b16)
        else:
            source = w_up if kind == U else w_down
            for d in range(shards):
                stages[kind][d] = source[:, d * lh:(d + 1) * lh].astype(b16)
        fulls[kind][mine[kind]] = stages[kind][(m, 0, spot, spot)[kind]]

    barrier = pltpu.get_barrier_semaphore()
    everyone = [(g, peer) for peer in peers] + [(gx, m), (gy, m), (sib, m), (gx, m1)]
    for target in everyone:
        pl.semaphore_signal(barrier, inc=1, device_id=target, device_id_type=MESH)
    for load in loads:
        load.start()
    stage(Q)
    pl.semaphore_wait(barrier, len(everyone))

    def depart(kind):
        for k in range(shards - 1):
            z_copy(kind, k).start()

    depart(Q)
    stage(U)
    depart(U)
    stage(O)
    stage(W)

    long_id = jnp.where(core == 0, id_col[rows - 1:rows, :], id_col[0:1, :])
    bias[:, :rows] = jnp.where(id_col[...] == id_row[...], 0.0, -1e30).astype(f32)
    slot = sib * rows + lax.broadcasted_iota(jnp.int32, (1, rows), 1)
    reach = jnp.where((slot > long_id - rows) & (slot <= long_id), long_id, -1)
    bias[:, rows:] = jnp.where(id_col[...] == reach, 0.0, -1e30).astype(f32)

    arrived(Q)
    go(Q, 0, 1, 3)
    depart(O)
    arrived(U)
    go(U, 0)
    depart(W)
    loads[4].wait()
    landed(Q, 0, 1)
    go(Q, 2, 4, 5)
    arrived(O)
    go(O, 0, 1, 3)
    landed(Q, 2)
    go(Q, 6)
    landed(Q, 3, 4, 5, 6)

    def project(j):
        return jnp.dot(
            hid[...], full_q[:, :, j * lw:(j + 1) * lw].reshape(width, lw),
            preferred_element_type=f32).astype(b16)

    key_rows = project(1)
    keys[0] = key_rows
    kv_copy(keys, 0).start()
    k_out[...] = key_rows
    value_rows = project(2)
    vals[0] = value_rows
    kv_copy(vals, 1).start()
    v_out[...] = value_rows
    queries[...] = project(0) * jnp.asarray(HD ** -0.5, b16)
    go(U, 1, 3)
    arrived(W)
    go(W, 0)
    kv_copy(keys, 0).wait_recv()
    kv_copy(vals, 1).wait_recv()

    q_tile = share
    lane = lax.broadcasted_iota(jnp.int32, (q_tile, 128), 1)
    own_rows = pl.ds(pl.multiple_of(m * share, share), share)

    def attend(p):
        cols = slice(p * 128, (p + 1) * 128)
        pair_keys = keys[:, :, cols].reshape(2 * rows, 128)
        pair_vals = jnp.concatenate(
            [vals[:, :, cols].reshape(2 * rows, 128), jnp.ones((2 * rows, 128), b16)], axis=1)

        for k in range(shards):
            target = peers[k] if k < shards - 1 else m
            here = pl.ds(pl.multiple_of(target * q_tile, q_tile), q_tile)
            pair_q = queries[here, cols]
            mask = bias[here, :]
            halves = []
            for h in range(2):
                own = (lane < HD) if h == 0 else (lane >= HD)
                head_q = jnp.where(own, pair_q, jnp.zeros_like(pair_q))
                scores = lax.dot_general(
                    head_q, pair_keys, (((1,), (1,)), ((), ())), preferred_element_type=f32) + mask
                peak = jnp.max(scores, axis=-1, keepdims=True)
                weights = jnp.exp(scores - peak).astype(b16)
                mixed = jnp.dot(weights, pair_vals, preferred_element_type=f32)
                halves.append(mixed[:, :128] / mixed[:, 128:])
            mixed_rows = jnp.where(lane < HD, halves[0], halves[1]).astype(b16)
            if k < shards - 1:
                att[p, k] = mixed_rows
                a_copy(p, k).start()
            else:
                att_in[m * pairs + p] = mixed_rows

    attend(0)
    landed(O, 0, 1)
    go(O, 2, 4, 5)
    for p in range(1, pairs):
        attend(p)
    landed(O, 2)
    go(O, 6)
    go(W, 1, 3)
    landed(U, 0, 1)
    go(U, 2, 4, 5)
    landed(O, 3, 4, 5, 6)
    for p in range(pairs):
        for k in range(shards - 1):
            a_copy(p, k).wait_recv()

    n_wide = 256
    o_parts = n_wide // part
    joined = jnp.concatenate([att_in[i] for i in range(shards * pairs)], axis=1)

    for n in range(width // n_wide):
        block = full_o[n * o_parts:(n + 1) * o_parts].reshape(n_wide, width)
        sums[:, n * n_wide:(n + 1) * n_wide] = lax.dot_general(
            joined, block, (((1,), (1,)), ((), ())), preferred_element_type=f32)
    normed[spot] = layer_norm(
        hid[own_rows, :].astype(f32) + sums[...], gain1[...], shift1[...]).astype(b16)
    for k in (1, 0, 2):
        n_copy(k).start()
    landed(U, 2)
    go(U, 6)
    landed(W, 0, 1)
    go(W, 2, 4, 5)
    landed(U, 3, 4, 5, 6)

    order = []
    for r in range(8 * shards):
        group_r, z_r = r // shards, r % shards
        order.append(((group_r // 4 * 2 + group_r % 2) * 2 + z_r // 2) * 4
                     + group_r // 2 % 2 * 2 + z_r % 2)
    d_parts = tile // part

    def up(batch, spots):
        tokens = jnp.concatenate([normed[i] for i in spots], axis=0)

        def up_step(n, carry):
            here = pl.ds(pl.multiple_of(n * n_wide, n_wide), n_wide)
            block = jnp.concatenate([full_u[r, :, here] for r in order], axis=0)
            pre = jnp.dot(tokens, block, preferred_element_type=f32)
            act[batch, :, here] = (0.5 * pre * (1.0 + lax.erf(pre * (0.5 ** 0.5)))).astype(b16)
            return carry

        lax.fori_loop(0, lh // n_wide, up_step, 0)

    def down(batch, n):
        block = jnp.concatenate(
            [full_d[r] for r in order[n * d_parts:(n + 1) * d_parts]], axis=0)
        return lax.dot_general(
            act[batch], block, (((1,), (1,)), ((), ())), preferred_element_type=f32)

    n_copy(1).wait_recv()
    up(0, (spot, square_spot[1]))
    landed(W, 2)
    go(W, 6)
    landed(W, 3, 4, 5, 6)
    for n in range(tiles):
        term = down(0, n)
        rs_send[1, n] = term[share:].astype(b16)
        r_copy(n, 1).start()
        sums[:, n * tile:(n + 1) * tile] = term[:share]
    n_copy(0).wait_recv()
    n_copy(2).wait_recv()
    up(1, (square_spot[2], square_spot[0]))
    for n in range(tiles):
        term = down(1, n)
        rs_send[2, n] = term[:share].astype(b16)
        r_copy(n, 2).start()
        rs_send[0, n] = term[share:].astype(b16)
        r_copy(n, 0).start()
    for n in range(tiles):
        cols = slice(n * tile, (n + 1) * tile)
        total = normed[spot, :, cols].astype(f32) + sums[:, cols]
        for k in (1, 0, 2):
            r_copy(n, k).wait_recv()
            total = total + rs_recv[k, n].astype(f32)
        sums[:, cols] = total
    out[...] = layer_norm(sums[...], gain2[...], shift2[...]).astype(b16)

    for kind in (Q, O, U, W):
        for k in range(shards - 1):
            z_copy(kind, k).wait_send()
        for step in range(7):
            p_copy(kind, step).wait_send()
    kv_copy(keys, 0).wait_send()
    kv_copy(vals, 1).wait_send()
    for k in range(shards - 1):
        n_copy(k).wait_send()
        for p in range(pairs):
            a_copy(p, k).wait_send()
        for n in range(tiles):
            r_copy(n, k).wait_send()


def kernel_body(
    hidden_in, request_ids, w_qkv, w_out, w_up, w_down, ln1_gain, ln1_shift, ln2_gain, ln2_shift
):
    groups = lax.axis_size("group")
    shards = lax.axis_size("mp")
    rows, width = hidden_in.shape
    part = w_qkv.shape[0]
    parts = groups * shards
    lw = width // shards
    lh = w_up.shape[1] // shards
    share = rows // shards
    pairs = lw // 128
    tile = 256
    tiles = width // tile
    b16, f32 = jnp.bfloat16, jnp.float32
    vmem = pl.BlockSpec(memory_space=pltpu.VMEM)
    hbm = pl.BlockSpec(memory_space=pltpu.HBM)
    dma = pltpu.SemaphoreType.DMA
    others = shards - 1
    return pl.pallas_call(
        functools.partial(layer_kernel, shards),
        out_shape=(
            jax.ShapeDtypeStruct((share, width), b16),
            jax.ShapeDtypeStruct((rows, lw), b16),
            jax.ShapeDtypeStruct((rows, lw), b16),
        ),
        in_specs=[hbm] + [vmem] * 2 + [hbm] * 4 + [vmem] * 4,
        out_specs=(vmem,) * 3,
        scratch_shapes=[
            pltpu.VMEM((rows, width), b16),
            pltpu.VMEM(w_qkv.shape, f32),
            pltpu.VMEM(w_out.shape, f32),
            pltpu.VMEM(w_up.shape, f32),
            pltpu.VMEM(w_down.shape, f32),
            pltpu.VMEM((shards, part, 3 * lw), b16),
            pltpu.VMEM((1, part, width), b16),
            pltpu.VMEM((shards, part, lh), b16),
            pltpu.VMEM((shards, part, lh), b16),
            pltpu.VMEM((parts, part, 3 * lw), b16),
            pltpu.VMEM((parts, part, width), b16),
            pltpu.VMEM((parts, part, lh), b16),
            pltpu.VMEM((parts, part, lh), b16),
            pltpu.VMEM((rows, 2 * rows), f32),
            pltpu.VMEM((rows, lw), b16),
            pltpu.VMEM((2, rows, lw), b16),
            pltpu.VMEM((2, rows, lw), b16),
            pltpu.VMEM((pairs, others, share, 128), b16),
            pltpu.VMEM((shards * pairs, share, 128), b16),
            pltpu.VMEM((share, width), f32),
            pltpu.VMEM((shards, share, width), b16),
            pltpu.VMEM((2, rows // 2, lh), b16),
            pltpu.VMEM((others, tiles, share, tile), b16),
            pltpu.VMEM((others, tiles, share, tile), b16),
            dma((5,)),
            dma((4, others)), dma((4, others)),
            dma((4, 7)), dma((4, 7)),
            dma((2,)), dma((2,)),
            dma((pairs, others)), dma((pairs, others)),
            dma((others,)), dma((others,)),
            dma((tiles, others)), dma((tiles, others)),
        ],
        compiler_params=pltpu.CompilerParams(
            collective_id=0, has_side_effects=True, vmem_limit_bytes=60 * 1024 * 1024),
        cost_estimate=pl.CostEstimate(
            flops=6 * rows * width * (4 * lw + 2 * lh), bytes_accessed=16 * 1024 * 1024,
            transcendentals=0),
        name="encoder_layer",
    )(
        hidden_in, request_ids.reshape(rows, 1), request_ids.reshape(1, rows),
        w_qkv, w_out, w_up, w_down,
        ln1_gain.reshape(1, width), ln1_shift.reshape(1, width),
        ln2_gain.reshape(1, width), ln2_shift.reshape(1, width),
    )


def solution(mesh):
    in_specs = (
        P("group", None),
        P("group"),
        P(("group", "mp"), None),
        P(("group", "mp"), None),
        P(("group", "mp"), None),
        P(("group", "mp"), None),
        P(),
        P(),
        P(),
        P(),
    )
    out_specs = (P(("group", "mp"), None), P("group", "mp"), P("group", "mp"))
    whole_tiles = mesh.shape["group"] == 8 and mesh.shape["mp"] == 4
    body = kernel_body if whole_tiles else plain_body
    return jax.shard_map(body, mesh=mesh, in_specs=in_specs, out_specs=out_specs, check_vma=False)
```

```python
import functools

import jax
import jax.numpy as jnp
from jax import lax
from jax.experimental import pallas as pl
from jax.experimental.pallas import tpu as pltpu
from jax.sharding import PartitionSpec as P

HD = 64
SHORT = 64


def swapped(value, axis, distance):
    return lax.ppermute(value, axis, [(i, i ^ 1 << distance) for i in range(lax.axis_size(axis))])


def layer_norm(values_in, norm_gain, norm_shift):
    center = values_in - jnp.mean(values_in, axis=-1, keepdims=True)
    spread = jnp.mean(center * center, axis=-1, keepdims=True)
    return center * lax.rsqrt(spread + 1e-05) * norm_gain + norm_shift


def plain_body(
    hidden_in, request_ids, w_qkv, w_out, w_up, w_down, ln1_gain, ln1_shift, ln2_gain, ln2_shift
):
    groups = lax.axis_size("group")
    shards = lax.axis_size("mp")
    model_width = hidden_in.shape[1]
    local_width = model_width // shards
    local_hidden = w_up.shape[1] // shards
    tok_rows = hidden_in.shape[0]
    part_rows = w_qkv.shape[0]
    pieces = (
        w_qkv.astype(jnp.bfloat16).reshape(part_rows, 3, shards, local_width),
        w_out.astype(jnp.bfloat16).reshape(part_rows, 1, shards, local_width),
        w_up.astype(jnp.bfloat16).reshape(part_rows, 1, shards, local_hidden),
        w_down.astype(jnp.bfloat16).reshape(part_rows, 1, shards, local_hidden),
    )
    gathered = (
        lax.all_gather(pieces[0], "group", axis=0, tiled=True),
        lax.all_gather(pieces[1], "group", axis=0, tiled=True),
        lax.all_gather(pieces[2], "group", axis=0, tiled=True),
        lax.all_gather(pieces[3], "group", axis=0, tiled=True),
    )
    exchanged = (
        lax.all_to_all(gathered[0], "mp", split_axis=2, concat_axis=0, tiled=True),
        lax.all_to_all(gathered[1], "mp", split_axis=2, concat_axis=0, tiled=True),
        lax.all_to_all(gathered[2], "mp", split_axis=2, concat_axis=0, tiled=True),
        lax.all_to_all(gathered[3], "mp", split_axis=2, concat_axis=0, tiled=True),
    )
    served = tuple(
        (
            jnp.transpose(
                weight_piece.reshape(shards, groups, part_rows, -1), (1, 0, 2, 3)
            ).reshape(model_width, -1)
            for weight_piece in exchanged
        )
    )
    qkv_local, out_local, up_local, down_local = served
    projected = jnp.dot(hidden_in, qkv_local, preferred_element_type=jnp.float32)
    queries = projected[:, :local_width].astype(jnp.bfloat16)
    key_rows = projected[:, local_width : 2 * local_width].astype(jnp.bfloat16)
    value_rows = projected[:, 2 * local_width :].astype(jnp.bfloat16)
    partner_keys, partner_values = swapped((key_rows, value_rows), "group", 0)
    group_index = lax.axis_index("group")
    parity = group_index % 2
    long_id = jnp.where(parity == 0, request_ids[-1], request_ids[0])
    own_long = request_ids == long_id
    local_heads = local_width // HD
    score_scale = HD ** (-0.5)
    block_total = tok_rows // SHORT
    short_q = queries.reshape(block_total, SHORT, local_heads, HD)
    short_k = key_rows.reshape(block_total, SHORT, local_heads, HD)
    short_v = value_rows.reshape(block_total, SHORT, local_heads, HD)
    short_ids = request_ids.reshape(block_total, SHORT)
    short_scores = (
        jnp.einsum("bqhd,bkhd->bhqk", short_q, short_k, preferred_element_type=jnp.float32)
        * score_scale
    )
    short_mask = short_ids[:, :, None] == short_ids[:, None, :]
    short_scores = jnp.where(short_mask[:, None], short_scores, -1e30)
    short_peak = jnp.max(short_scores, axis=-1, keepdims=True)
    short_weights = jnp.exp(short_scores - short_peak).astype(jnp.bfloat16)
    short_totals = jnp.sum(short_weights.astype(jnp.float32), axis=-1)
    short_mixed = jnp.einsum(
        "bhqk,bkhd->bqhd", short_weights, short_v, preferred_element_type=jnp.float32
    )
    short_out = (
        (short_mixed / jnp.transpose(short_totals, (0, 2, 1))[:, :, :, None])
        .astype(jnp.bfloat16)
        .reshape(tok_rows, local_width)
    )
    first_keys = jnp.where(parity == 0, key_rows, partner_keys)
    second_keys = jnp.where(parity == 0, partner_keys, key_rows)
    first_values = jnp.where(parity == 0, value_rows, partner_values)
    second_values = jnp.where(parity == 0, partner_values, value_rows)
    pair_base = (group_index - parity) * tok_rows
    span_start = long_id - tok_rows + 1 - pair_base
    long_keys = lax.dynamic_slice_in_dim(
        jnp.concatenate([first_keys, second_keys], 0), span_start, tok_rows, 0
    ).reshape(tok_rows, local_heads, HD)
    long_values = lax.dynamic_slice_in_dim(
        jnp.concatenate([first_values, second_values], 0), span_start, tok_rows, 0
    ).reshape(tok_rows, local_heads, HD)
    query_rows = min(512, tok_rows)
    query_blocks = tok_rows // query_rows

    def long_attend(block_queries):
        heads_view = block_queries.reshape(query_rows, local_heads, HD)
        scores = (
            jnp.einsum("qhd,khd->hqk", heads_view, long_keys, preferred_element_type=jnp.float32)
            * score_scale
        )
        row_peak = jnp.max(scores, axis=-1, keepdims=True)
        weights = jnp.exp(scores - row_peak).astype(jnp.bfloat16)
        totals = jnp.sum(weights.astype(jnp.float32), axis=-1)
        mixed_heads = jnp.einsum(
            "hqk,khd->qhd", weights, long_values, preferred_element_type=jnp.float32
        )
        return (
            (mixed_heads / jnp.transpose(totals)[:, :, None])
            .astype(jnp.bfloat16)
            .reshape(query_rows, local_width)
        )

    def skipped(block_queries):
        return jnp.zeros((query_rows, local_width), jnp.bfloat16)

    def long_block(query_block):
        block_queries, block_long = query_block
        return lax.cond(jnp.any(block_long), long_attend, skipped, block_queries)

    long_out = lax.map(
        long_block,
        (
            queries.reshape(query_blocks, query_rows, local_width),
            own_long.reshape(query_blocks, query_rows),
        ),
    ).reshape(tok_rows, local_width)
    attended = jnp.where(own_long[:, None], long_out, short_out)
    share_rows = tok_rows // shards
    row_start = lax.axis_index("mp") * share_rows

    def combine(term_fn, residual, norm_gain, norm_shift):
        summed = lax.psum(term_fn(0, tok_rows), "mp")
        whole_rows = layer_norm(
            residual.astype(jnp.float32) + summed, norm_gain, norm_shift
        ).astype(jnp.bfloat16)
        normed = lax.dynamic_slice_in_dim(whole_rows, row_start, share_rows, 0)
        return (normed, whole_rows)

    def attn_term(row_begin, row_count):
        return lax.dot_general(
            attended, out_local, (((1,), (1,)), ((), ())), preferred_element_type=jnp.float32
        )

    attn_share, attn_normed = combine(attn_term, hidden_in, ln1_gain, ln1_shift)
    activated = jax.nn.gelu(
        jnp.dot(attn_normed, up_local, preferred_element_type=jnp.float32), approximate=False
    ).astype(jnp.bfloat16)

    def feed_term(row_begin, row_count):
        return lax.dot_general(
            activated, down_local, (((1,), (1,)), ((), ())), preferred_element_type=jnp.float32
        )

    final_share, unused = combine(feed_term, attn_normed, ln2_gain, ln2_shift)
    return (final_share, key_rows, value_rows)


MESH = pl.DeviceIdType.MESH
Q, O, U, W = range(4)


def layer_kernel(
    shards, hid_in, id_col, id_row, w_qkv_in, w_out_in, w_up_in, w_down_in,
    gain1, shift1, gain2, shift2,
    out, k_out, v_out,
    hid, w_qkv, w_out, w_up, w_down,
    stage_q, stage_o, stage_u, stage_d, full_q, full_o, full_u, full_d,
    bias, queries, kv, vals_ones, att, att_in, sums, normed, act, rs_send, rs_recv,
    in_sem, z_send, z_recv, p_send, p_recv, kv_send, kv_recv, a_send, a_recv,
    n_send, n_recv, r_send, r_recv,
):
    g = lax.axis_index("group")
    m = lax.axis_index("mp")
    core = lax.rem(g, 2)
    x = lax.rem(g // 2, 2)
    y = g // 4
    half = m // 2
    side = lax.rem(m, 2)
    sib = g + 1 - 2 * core
    gx = g + 2 - 4 * x
    gy = g + 4 - 8 * y
    gd = gx + gy - g
    m1 = m + 1 - 2 * side
    m2 = m + 2 - 4 * half
    rows = hid.shape[0]
    width = hid.shape[1]
    part = w_qkv.shape[0]
    lw = queries.shape[1]
    lh = act.shape[1]
    pairs = lw // 128
    share = rows // shards
    f32, b16 = jnp.float32, jnp.bfloat16
    fulls = (full_q, full_o, full_u, full_d)
    stages = (stage_q, stage_o, stage_u, stage_d)
    peers = [lax.rem(m + k, shards) for k in range(1, shards)]
    spot = 2 * x + side
    square = ((g, m1), (gx, m), (gx, m1))
    square_spot = (2 * x + 1 - side, 2 - 2 * x + side, 3 - 2 * x - side)

    def block_at(on_y, on_core, on_half):
        return (on_y * 2 + on_core) * 2 + on_half

    mine = (g * shards + m,) * 2 + (block_at(y, core, half) * 4 + spot,) * 2

    def z_copy(kind, k):
        if kind == Q:
            chunk, target = stage_q.at[peers[k]], (g, peers[k])
        elif kind == O:
            chunk, target = stage_o.at[0], (g, peers[k])
        else:
            chunk, target = stages[kind].at[square_spot[k]], square[k]
        return pltpu.make_async_remote_copy(
            src_ref=chunk, dst_ref=fulls[kind].at[mine[kind]],
            send_sem=z_send.at[kind, k], recv_sem=z_recv.at[kind, k],
            device_id=target, device_id_type=MESH)

    plane_hops = (
        (g, (gx, m)), (g, (gy, m)), (gy, (gx, m)),
        (g, (sib, m)), (gx, (sib, m)), (gy, (sib, m)), (gd, (sib, m)))
    b_own = block_at(y, core, half)
    b_z = block_at(y, core, 1 - half)
    b_y = block_at(1 - y, core, half)
    b_d = block_at(1 - y, core, 1 - half)
    hidden_hops = (
        (b_own, (g, m2)), (b_own, (gy, m)), (b_z, (gy, m)),
        (b_own, (sib, m)), (b_z, (sib, m)), (b_y, (sib, m)), (b_d, (sib, m)))

    def p_copy(kind, step):
        block, target = (plane_hops if kind in (Q, O) else hidden_hops)[step]
        place = fulls[kind].at[pl.ds(block * 4, 4)]
        return pltpu.make_async_remote_copy(
            src_ref=place, dst_ref=place,
            send_sem=p_send.at[kind, step], recv_sem=p_recv.at[kind, step],
            device_id=target, device_id_type=MESH)

    def arrived(kind):
        for k in range(shards - 1):
            z_copy(kind, k).wait_recv()

    def go(kind, *steps):
        for step in steps:
            p_copy(kind, step).start()

    def landed(kind, *steps):
        for step in steps:
            p_copy(kind, step).wait_recv()

    def kv_copy(i):
        return pltpu.make_async_remote_copy(
            src_ref=kv.at[i, 0], dst_ref=kv.at[i, 1],
            send_sem=kv_send.at[i], recv_sem=kv_recv.at[i],
            device_id=(sib, m), device_id_type=MESH)

    def a_copy(p, k):
        return pltpu.make_async_remote_copy(
            src_ref=att.at[p, k],
            dst_ref=att_in.at[m * pairs + p],
            send_sem=a_send.at[p, k], recv_sem=a_recv.at[p, k],
            device_id=(g, lax.rem(m + 1 + k, shards)), device_id_type=MESH)

    def n_copy(k):
        return pltpu.make_async_remote_copy(
            src_ref=normed.at[spot], dst_ref=normed.at[spot],
            send_sem=n_send.at[k], recv_sem=n_recv.at[k],
            device_id=square[k], device_id_type=MESH)

    tiles = rs_send.shape[1]
    tile = rs_send.shape[3]

    def r_copy(n, k):
        return pltpu.make_async_remote_copy(
            src_ref=rs_send.at[k, n],
            dst_ref=rs_recv.at[k, n],
            send_sem=r_send.at[n, k], recv_sem=r_recv.at[n, k],
            device_id=square[k], device_id_type=MESH)

    loads = [
        pltpu.make_async_copy(far, near, in_sem.at[i])
        for i, (far, near) in enumerate((
            (w_qkv_in, w_qkv), (w_out_in, w_out), (w_up_in, w_up), (w_down_in, w_down),
            (hid_in, hid)))
    ]

    def stage(kind):
        loads[kind].wait()
        if kind == Q:
            for d in range(shards):
                for j in range(3):
                    stage_q[d, :, j * lw:(j + 1) * lw] = w_qkv[
                        :, j * width + d * lw:j * width + (d + 1) * lw].astype(b16)
        elif kind == O:
            stage_o[0] = w_out[...].astype(b16)
        else:
            source = w_up if kind == U else w_down
            for d in range(shards):
                stages[kind][d] = source[:, d * lh:(d + 1) * lh].astype(b16)
        fulls[kind][mine[kind]] = stages[kind][(m, 0, spot, spot)[kind]]

    barrier = pltpu.get_barrier_semaphore()
    everyone = [(g, peer) for peer in peers] + [(gx, m), (gy, m), (sib, m), (gx, m1)]
    for target in everyone:
        pl.semaphore_signal(barrier, inc=1, device_id=target, device_id_type=MESH)
    for load in loads:
        load.start()
    stage(Q)
    pl.semaphore_wait(barrier, len(everyone))

    def depart(kind):
        for k in range(shards - 1):
            z_copy(kind, k).start()

    depart(Q)
    stage(U)
    depart(U)
    stage(O)
    stage(W)

    long_id = jnp.where(core == 0, id_col[rows - 1:rows, :], id_col[0:1, :])
    slot = sib * rows + lax.broadcasted_iota(jnp.int32, (1, rows), 1)
    reach = jnp.where((slot > long_id - rows) & (slot <= long_id), long_id, -1)
    few = 32

    def bias_step(i, carry):
        here = pl.ds(pl.multiple_of(i * few, few), few)
        ids = id_col[here, :]
        bias[here, :rows] = jnp.where(ids == id_row[...], 0.0, -1e30).astype(f32)
        bias[here, rows:] = jnp.where(ids == reach, 0.0, -1e30).astype(f32)
        return carry

    lax.fori_loop(0, rows // few, bias_step, 0)
    for p in range(pairs):
        for i in range(2):
            vals_ones[p, i, :, 128:] = jnp.ones((rows, 128), b16)

    arrived(Q)
    go(Q, 0, 1, 3)
    depart(O)
    arrived(U)
    go(U, 0)
    depart(W)
    loads[4].wait()
    landed(Q, 0, 1)
    go(Q, 2, 4, 5)
    arrived(O)
    go(O, 0, 1, 3)
    landed(Q, 2)
    go(Q, 6)
    landed(Q, 3, 4, 5, 6)

    def project(i, carry):
        j = lax.rem(i + 1, 3)
        here = pl.ds(pl.multiple_of(j * lw, lw), lw)
        block = full_q[:, :, here].reshape(width, lw)
        some = jnp.dot(hid[...], block, preferred_element_type=f32).astype(b16)

        @pl.when(i < 2)
        def _():
            kv[i, 0] = some
            kv_copy(i).start()

        @pl.when(i == 2)
        def _():
            queries[...] = some * jnp.asarray(HD ** -0.5, b16)

        return carry

    lax.fori_loop(0, 3, project, 0)
    go(U, 1, 3)
    arrived(W)
    go(W, 0, 1, 3)
    k_out[...] = kv[0, 0]
    v_out[...] = kv[1, 0]
    for i in range(2):
        kv_copy(i).wait_recv()
    for p in range(pairs):
        vals_ones[p, :, :, :128] = kv[1, :, :, p * 128:(p + 1) * 128]

    lane = lax.broadcasted_iota(jnp.int32, (share, 128), 1)
    own_rows = pl.ds(pl.multiple_of(m * share, share), share)

    def attend(p, carry):
        cols = pl.ds(pl.multiple_of(p * 128, 128), 128)

        def step(k, carry):
            here = pl.ds(pl.multiple_of(lax.rem(m + 1 + k, shards) * share, share), share)
            pair_q = queries[here, cols]
            halves = []
            for h in range(2):
                own = (lane < HD) if h == 0 else (lane >= HD)
                head_q = jnp.where(own, pair_q, jnp.zeros_like(pair_q))
                scores = lax.dot_general(
                    head_q, kv[0, :, :, cols].reshape(2 * rows, 128),
                    (((1,), (1,)), ((), ())), preferred_element_type=f32) + bias[here, :]
                peak = jnp.max(scores, axis=-1, keepdims=True)
                weights = jnp.exp(scores - peak).astype(b16)
                mixed = jnp.dot(
                    weights, vals_ones[p].reshape(2 * rows, 256), preferred_element_type=f32)
                halves.append(mixed[:, :128] / mixed[:, 128:])
            mixed_rows = jnp.where(lane < HD, halves[0], halves[1]).astype(b16)

            @pl.when(k < shards - 1)
            def _():
                att[p, k] = mixed_rows
                a_copy(p, k).start()

            @pl.when(k == shards - 1)
            def _():
                att_in[m * pairs + p] = mixed_rows

            return carry

        lax.fori_loop(0, shards, step, 0)

        @pl.when(p == 0)
        def _():
            landed(O, 0, 1)
            go(O, 2, 4, 5)
            landed(U, 0, 1)
            go(U, 2, 4, 5)

        return carry

    lax.fori_loop(0, pairs, attend, 0)
    landed(O, 2)
    go(O, 6)
    landed(U, 2)
    go(U, 6)
    landed(O, 3, 4, 5, 6)
    for p in range(pairs):
        for k in range(shards - 1):
            a_copy(p, k).wait_recv()

    n_wide = 256
    o_parts = n_wide // part

    def out_step(n, carry):
        here = pl.ds(pl.multiple_of(n * n_wide, n_wide), n_wide)
        joined = jnp.concatenate([att_in[i] for i in range(shards * pairs)], axis=1)
        block = full_o[pl.ds(n * o_parts, o_parts)].reshape(n_wide, width)
        sums[:, here] = lax.dot_general(
            joined, block, (((1,), (1,)), ((), ())), preferred_element_type=f32)
        return carry

    lax.fori_loop(0, width // n_wide, out_step, 0)

    def ln_step(i, carry):
        here = pl.ds(pl.multiple_of(i * few, few), few)
        there = pl.ds(pl.multiple_of(m * share + i * few, few), few)
        normed[spot, here, :] = layer_norm(
            hid[there, :].astype(f32) + sums[here, :], gain1[...], shift1[...]).astype(b16)
        return carry

    lax.fori_loop(0, share // few, ln_step, 0)
    for k in (1, 0, 2):
        n_copy(k).start()
    landed(W, 0, 1)
    go(W, 2, 4, 5)
    landed(U, 3, 4, 5, 6)

    order = []
    for r in range(8 * shards):
        group_r, z_r = r // shards, r % shards
        order.append(((group_r // 4 * 2 + group_r % 2) * 2 + z_r // 2) * 4
                     + group_r // 2 % 2 * 2 + z_r % 2)
    d_parts = tile // part

    def feed(batch, carry):
        first = spot * (1 - batch) + square_spot[2] * batch
        second = square_spot[1] * (1 - batch) + square_spot[0] * batch

        @pl.when(batch == 0)
        def _():
            n_copy(1).wait_recv()

        @pl.when(batch == 1)
        def _():
            n_copy(0).wait_recv()
            n_copy(2).wait_recv()

        def up_step(n, carry):
            here = pl.ds(pl.multiple_of(n * n_wide, n_wide), n_wide)
            block = jnp.concatenate([full_u[r, :, here] for r in order], axis=0)
            tokens = jnp.concatenate([normed[first], normed[second]], axis=0)
            pre = jnp.dot(tokens, block, preferred_element_type=f32)
            act[:, here] = (0.5 * pre * (1.0 + lax.erf(pre * (0.5 ** 0.5)))).astype(b16)
            return carry

        lax.fori_loop(0, lh // n_wide, up_step, 0)

        @pl.when(batch == 0)
        def _():
            landed(W, 2)
            go(W, 6)
            landed(W, 3, 4, 5, 6)

        def down_step(n, carry):
            start = n // 2 * 16 + lax.rem(n, 2) * 2
            block = jnp.concatenate(
                [full_d[start + i // 4 * 8 + i % 4 // 2 * 4 + i % 2] for i in range(d_parts)], axis=0)
            term = lax.dot_general(
                act[...], block, (((1,), (1,)), ((), ())), preferred_element_type=f32)

            @pl.when(batch == 0)
            def _():
                rs_send[1, n] = term[share:].astype(b16)
                r_copy(n, 1).start()
                sums[:, pl.ds(pl.multiple_of(n * tile, tile), tile)] = term[:share]

            @pl.when(batch == 1)
            def _():
                rs_send[2, n] = term[:share].astype(b16)
                r_copy(n, 2).start()
                rs_send[0, n] = term[share:].astype(b16)
                r_copy(n, 0).start()

            return carry

        lax.fori_loop(0, tiles, down_step, 0)
        return carry

    lax.fori_loop(0, 2, feed, 0)

    def total_step(n, carry):
        cols = pl.ds(pl.multiple_of(n * tile, tile), tile)
        total = normed[spot, :, cols].astype(f32) + sums[:, cols]
        for k in (1, 0, 2):
            r_copy(n, k).wait_recv()
            total = total + rs_recv[k, n].astype(f32)
        sums[:, cols] = total
        return carry

    lax.fori_loop(0, tiles, total_step, 0)

    def last_step(i, carry):
        here = pl.ds(pl.multiple_of(i * few, few), few)
        out[here, :] = layer_norm(sums[here, :], gain2[...], shift2[...]).astype(b16)
        return carry

    lax.fori_loop(0, share // few, last_step, 0)

    for kind in (Q, O, U, W):
        for k in range(shards - 1):
            z_copy(kind, k).wait_send()
        for step in range(7):
            p_copy(kind, step).wait_send()
    for i in range(2):
        kv_copy(i).wait_send()
    for k in range(shards - 1):
        n_copy(k).wait_send()
        for p in range(pairs):
            a_copy(p, k).wait_send()
        for n in range(tiles):
            r_copy(n, k).wait_send()


def kernel_body(
    hidden_in, request_ids, w_qkv, w_out, w_up, w_down, ln1_gain, ln1_shift, ln2_gain, ln2_shift
):
    groups = lax.axis_size("group")
    shards = lax.axis_size("mp")
    rows, width = hidden_in.shape
    part = w_qkv.shape[0]
    parts = groups * shards
    lw = width // shards
    lh = w_up.shape[1] // shards
    share = rows // shards
    pairs = lw // 128
    tile = 256
    tiles = width // tile
    b16, f32 = jnp.bfloat16, jnp.float32
    vmem = pl.BlockSpec(memory_space=pltpu.VMEM)
    hbm = pl.BlockSpec(memory_space=pltpu.HBM)
    dma = pltpu.SemaphoreType.DMA
    others = shards - 1
    return pl.pallas_call(
        functools.partial(layer_kernel, shards),
        out_shape=(
            jax.ShapeDtypeStruct((share, width), b16),
            jax.ShapeDtypeStruct((rows, lw), b16),
            jax.ShapeDtypeStruct((rows, lw), b16),
        ),
        in_specs=[hbm] + [vmem] * 2 + [hbm] * 4 + [vmem] * 4,
        out_specs=(vmem,) * 3,
        scratch_shapes=[
            pltpu.VMEM((rows, width), b16),
            pltpu.VMEM(w_qkv.shape, f32),
            pltpu.VMEM(w_out.shape, f32),
            pltpu.VMEM(w_up.shape, f32),
            pltpu.VMEM(w_down.shape, f32),
            pltpu.VMEM((shards, part, 3 * lw), b16),
            pltpu.VMEM((1, part, width), b16),
            pltpu.VMEM((shards, part, lh), b16),
            pltpu.VMEM((shards, part, lh), b16),
            pltpu.VMEM((parts, part, 3 * lw), b16),
            pltpu.VMEM((parts, part, width), b16),
            pltpu.VMEM((parts, part, lh), b16),
            pltpu.VMEM((parts, part, lh), b16),
            pltpu.VMEM((rows, 2 * rows), f32),
            pltpu.VMEM((rows, lw), b16),
            pltpu.VMEM((2, 2, rows, lw), b16),
            pltpu.VMEM((pairs, 2, rows, 256), b16),
            pltpu.VMEM((pairs, others, share, 128), b16),
            pltpu.VMEM((shards * pairs, share, 128), b16),
            pltpu.VMEM((share, width), f32),
            pltpu.VMEM((shards, share, width), b16),
            pltpu.VMEM((rows // 2, lh), b16),
            pltpu.VMEM((others, tiles, share, tile), b16),
            pltpu.VMEM((others, tiles, share, tile), b16),
            dma((5,)),
            dma((4, others)), dma((4, others)),
            dma((4, 7)), dma((4, 7)),
            dma((2,)), dma((2,)),
            dma((pairs, others)), dma((pairs, others)),
            dma((others,)), dma((others,)),
            dma((tiles, others)), dma((tiles, others)),
        ],
        compiler_params=pltpu.CompilerParams(
            collective_id=0, has_side_effects=True, vmem_limit_bytes=56 * 1024 * 1024),
        cost_estimate=pl.CostEstimate(
            flops=6 * rows * width * (4 * lw + 2 * lh), bytes_accessed=16 * 1024 * 1024,
            transcendentals=0),
        name="encoder_layer",
    )(
        hidden_in, request_ids.reshape(rows, 1), request_ids.reshape(1, rows),
        w_qkv, w_out, w_up, w_down,
        ln1_gain.reshape(1, width), ln1_shift.reshape(1, width),
        ln2_gain.reshape(1, width), ln2_shift.reshape(1, width),
    )


def solution(mesh):
    in_specs = (
        P("group", None),
        P("group"),
        P(("group", "mp"), None),
        P(("group", "mp"), None),
        P(("group", "mp"), None),
        P(("group", "mp"), None),
        P(),
        P(),
        P(),
        P(),
    )
    out_specs = (P(("group", "mp"), None), P("group", "mp"), P("group", "mp"))
    whole_tiles = mesh.shape["group"] == 8 and mesh.shape["mp"] == 4
    body = kernel_body if whole_tiles else plain_body
    return jax.shard_map(body, mesh=mesh, in_specs=in_specs, out_specs=out_specs, check_vma=False)
```

```python
import functools

import jax
import jax.numpy as jnp
from jax import lax
from jax.experimental import pallas as pl
from jax.experimental.pallas import tpu as pltpu
from jax.sharding import PartitionSpec as P

HD = 64
SHORT = 64


def swapped(value, axis, distance):
    return lax.ppermute(value, axis, [(i, i ^ 1 << distance) for i in range(lax.axis_size(axis))])


def layer_norm(values_in, norm_gain, norm_shift):
    center = values_in - jnp.mean(values_in, axis=-1, keepdims=True)
    spread = jnp.mean(center * center, axis=-1, keepdims=True)
    return center * lax.rsqrt(spread + 1e-05) * norm_gain + norm_shift


def plain_body(
    hidden_in, request_ids, w_qkv, w_out, w_up, w_down, ln1_gain, ln1_shift, ln2_gain, ln2_shift
):
    groups = lax.axis_size("group")
    shards = lax.axis_size("mp")
    model_width = hidden_in.shape[1]
    local_width = model_width // shards
    local_hidden = w_up.shape[1] // shards
    tok_rows = hidden_in.shape[0]
    part_rows = w_qkv.shape[0]
    pieces = (
        w_qkv.astype(jnp.bfloat16).reshape(part_rows, 3, shards, local_width),
        w_out.astype(jnp.bfloat16).reshape(part_rows, 1, shards, local_width),
        w_up.astype(jnp.bfloat16).reshape(part_rows, 1, shards, local_hidden),
        w_down.astype(jnp.bfloat16).reshape(part_rows, 1, shards, local_hidden),
    )
    gathered = (
        lax.all_gather(pieces[0], "group", axis=0, tiled=True),
        lax.all_gather(pieces[1], "group", axis=0, tiled=True),
        lax.all_gather(pieces[2], "group", axis=0, tiled=True),
        lax.all_gather(pieces[3], "group", axis=0, tiled=True),
    )
    exchanged = (
        lax.all_to_all(gathered[0], "mp", split_axis=2, concat_axis=0, tiled=True),
        lax.all_to_all(gathered[1], "mp", split_axis=2, concat_axis=0, tiled=True),
        lax.all_to_all(gathered[2], "mp", split_axis=2, concat_axis=0, tiled=True),
        lax.all_to_all(gathered[3], "mp", split_axis=2, concat_axis=0, tiled=True),
    )
    served = tuple(
        (
            jnp.transpose(
                weight_piece.reshape(shards, groups, part_rows, -1), (1, 0, 2, 3)
            ).reshape(model_width, -1)
            for weight_piece in exchanged
        )
    )
    qkv_local, out_local, up_local, down_local = served
    projected = jnp.dot(hidden_in, qkv_local, preferred_element_type=jnp.float32)
    queries = projected[:, :local_width].astype(jnp.bfloat16)
    key_rows = projected[:, local_width : 2 * local_width].astype(jnp.bfloat16)
    value_rows = projected[:, 2 * local_width :].astype(jnp.bfloat16)
    partner_keys, partner_values = swapped((key_rows, value_rows), "group", 0)
    group_index = lax.axis_index("group")
    parity = group_index % 2
    long_id = jnp.where(parity == 0, request_ids[-1], request_ids[0])
    own_long = request_ids == long_id
    local_heads = local_width // HD
    score_scale = HD ** (-0.5)
    block_total = tok_rows // SHORT
    short_q = queries.reshape(block_total, SHORT, local_heads, HD)
    short_k = key_rows.reshape(block_total, SHORT, local_heads, HD)
    short_v = value_rows.reshape(block_total, SHORT, local_heads, HD)
    short_ids = request_ids.reshape(block_total, SHORT)
    short_scores = (
        jnp.einsum("bqhd,bkhd->bhqk", short_q, short_k, preferred_element_type=jnp.float32)
        * score_scale
    )
    short_mask = short_ids[:, :, None] == short_ids[:, None, :]
    short_scores = jnp.where(short_mask[:, None], short_scores, -1e30)
    short_peak = jnp.max(short_scores, axis=-1, keepdims=True)
    short_weights = jnp.exp(short_scores - short_peak).astype(jnp.bfloat16)
    short_totals = jnp.sum(short_weights.astype(jnp.float32), axis=-1)
    short_mixed = jnp.einsum(
        "bhqk,bkhd->bqhd", short_weights, short_v, preferred_element_type=jnp.float32
    )
    short_out = (
        (short_mixed / jnp.transpose(short_totals, (0, 2, 1))[:, :, :, None])
        .astype(jnp.bfloat16)
        .reshape(tok_rows, local_width)
    )
    first_keys = jnp.where(parity == 0, key_rows, partner_keys)
    second_keys = jnp.where(parity == 0, partner_keys, key_rows)
    first_values = jnp.where(parity == 0, value_rows, partner_values)
    second_values = jnp.where(parity == 0, partner_values, value_rows)
    pair_base = (group_index - parity) * tok_rows
    span_start = long_id - tok_rows + 1 - pair_base
    long_keys = lax.dynamic_slice_in_dim(
        jnp.concatenate([first_keys, second_keys], 0), span_start, tok_rows, 0
    ).reshape(tok_rows, local_heads, HD)
    long_values = lax.dynamic_slice_in_dim(
        jnp.concatenate([first_values, second_values], 0), span_start, tok_rows, 0
    ).reshape(tok_rows, local_heads, HD)
    query_rows = min(512, tok_rows)
    query_blocks = tok_rows // query_rows

    def long_attend(block_queries):
        heads_view = block_queries.reshape(query_rows, local_heads, HD)
        scores = (
            jnp.einsum("qhd,khd->hqk", heads_view, long_keys, preferred_element_type=jnp.float32)
            * score_scale
        )
        row_peak = jnp.max(scores, axis=-1, keepdims=True)
        weights = jnp.exp(scores - row_peak).astype(jnp.bfloat16)
        totals = jnp.sum(weights.astype(jnp.float32), axis=-1)
        mixed_heads = jnp.einsum(
            "hqk,khd->qhd", weights, long_values, preferred_element_type=jnp.float32
        )
        return (
            (mixed_heads / jnp.transpose(totals)[:, :, None])
            .astype(jnp.bfloat16)
            .reshape(query_rows, local_width)
        )

    def skipped(block_queries):
        return jnp.zeros((query_rows, local_width), jnp.bfloat16)

    def long_block(query_block):
        block_queries, block_long = query_block
        return lax.cond(jnp.any(block_long), long_attend, skipped, block_queries)

    long_out = lax.map(
        long_block,
        (
            queries.reshape(query_blocks, query_rows, local_width),
            own_long.reshape(query_blocks, query_rows),
        ),
    ).reshape(tok_rows, local_width)
    attended = jnp.where(own_long[:, None], long_out, short_out)
    share_rows = tok_rows // shards
    row_start = lax.axis_index("mp") * share_rows

    def combine(term_fn, residual, norm_gain, norm_shift):
        summed = lax.psum(term_fn(0, tok_rows), "mp")
        whole_rows = layer_norm(
            residual.astype(jnp.float32) + summed, norm_gain, norm_shift
        ).astype(jnp.bfloat16)
        normed = lax.dynamic_slice_in_dim(whole_rows, row_start, share_rows, 0)
        return (normed, whole_rows)

    def attn_term(row_begin, row_count):
        return lax.dot_general(
            attended, out_local, (((1,), (1,)), ((), ())), preferred_element_type=jnp.float32
        )

    attn_share, attn_normed = combine(attn_term, hidden_in, ln1_gain, ln1_shift)
    activated = jax.nn.gelu(
        jnp.dot(attn_normed, up_local, preferred_element_type=jnp.float32), approximate=False
    ).astype(jnp.bfloat16)

    def feed_term(row_begin, row_count):
        return lax.dot_general(
            activated, down_local, (((1,), (1,)), ((), ())), preferred_element_type=jnp.float32
        )

    final_share, unused = combine(feed_term, attn_normed, ln2_gain, ln2_shift)
    return (final_share, key_rows, value_rows)


MESH = pl.DeviceIdType.MESH
Q, O, U, W = range(4)


def layer_kernel(
    shards, hid_in, id_col, id_row, w_qkv_in, w_out_in, w_up_in, w_down_in,
    gain1, shift1, gain2, shift2,
    out, k_out, v_out,
    hid, w_qkv, w_out, w_up, w_down,
    stage_q, stage_o, stage_u, stage_d, full_q, full_o, full_u, full_d,
    bias, queries, kv, vals_ones, att, att_in, sums, normed, act, rs_send, rs_recv,
    in_sem, z_send, z_recv, p_send, p_recv, kv_send, kv_recv, a_send, a_recv,
    n_send, n_recv, r_send, r_recv,
):
    g = lax.axis_index("group")
    m = lax.axis_index("mp")
    core = lax.rem(g, 2)
    x = lax.rem(g // 2, 2)
    y = g // 4
    half = m // 2
    side = lax.rem(m, 2)
    sib = g + 1 - 2 * core
    gx = g + 2 - 4 * x
    gy = g + 4 - 8 * y
    gd = gx + gy - g
    m1 = m + 1 - 2 * side
    m2 = m + 2 - 4 * half
    rows = hid.shape[0]
    width = hid.shape[1]
    part = w_qkv.shape[0]
    lw = queries.shape[1]
    lh = act.shape[1]
    pairs = lw // 128
    share = rows // shards
    f32, b16 = jnp.float32, jnp.bfloat16
    fulls = (full_q, full_o, full_u, full_d)
    stages = (stage_q, stage_o, stage_u, stage_d)
    peers = [lax.rem(m + k, shards) for k in range(1, shards)]
    spot = 2 * x + side
    square = ((g, m1), (gx, m), (gx, m1))
    square_spot = (2 * x + 1 - side, 2 - 2 * x + side, 3 - 2 * x - side)

    def block_at(on_y, on_core, on_half):
        return (on_y * 2 + on_core) * 2 + on_half

    mine = (g * shards + m,) * 2 + (block_at(y, core, half) * 4 + spot,) * 2

    def z_copy(kind, k):
        if kind == Q:
            chunk, target = stage_q.at[peers[k]], (g, peers[k])
        elif kind == O:
            chunk, target = stage_o.at[0], (g, peers[k])
        else:
            chunk, target = stages[kind].at[square_spot[k]], square[k]
        return pltpu.make_async_remote_copy(
            src_ref=chunk, dst_ref=fulls[kind].at[mine[kind]],
            send_sem=z_send.at[kind, k], recv_sem=z_recv.at[kind, k],
            device_id=target, device_id_type=MESH)

    plane_hops = (
        (g, (gx, m)), (g, (gy, m)), (gy, (gx, m)),
        (g, (sib, m)), (gx, (sib, m)), (gy, (sib, m)), (gd, (sib, m)))
    b_own = block_at(y, core, half)
    b_z = block_at(y, core, 1 - half)
    b_y = block_at(1 - y, core, half)
    b_d = block_at(1 - y, core, 1 - half)
    hidden_hops = (
        (b_own, (g, m2)), (b_own, (gy, m)), (b_z, (gy, m)),
        (b_own, (sib, m)), (b_z, (sib, m)), (b_y, (sib, m)), (b_d, (sib, m)))

    def p_copy(kind, step):
        block, target = (plane_hops if kind in (Q, O) else hidden_hops)[step]
        place = fulls[kind].at[pl.ds(block * 4, 4)]
        return pltpu.make_async_remote_copy(
            src_ref=place, dst_ref=place,
            send_sem=p_send.at[kind, step], recv_sem=p_recv.at[kind, step],
            device_id=target, device_id_type=MESH)

    def arrived(kind):
        for k in range(shards - 1):
            z_copy(kind, k).wait_recv()

    def go(kind, *steps):
        for step in steps:
            p_copy(kind, step).start()

    def landed(kind, *steps):
        for step in steps:
            p_copy(kind, step).wait_recv()

    def kv_copy(i):
        return pltpu.make_async_remote_copy(
            src_ref=kv.at[i, 0], dst_ref=kv.at[i, 1],
            send_sem=kv_send.at[i], recv_sem=kv_recv.at[i],
            device_id=(sib, m), device_id_type=MESH)

    def a_copy(p, k):
        return pltpu.make_async_remote_copy(
            src_ref=att.at[p, k],
            dst_ref=att_in.at[m * pairs + p],
            send_sem=a_send.at[p, k], recv_sem=a_recv.at[p, k],
            device_id=(g, lax.rem(m + 1 + k, shards)), device_id_type=MESH)

    def n_copy(k):
        return pltpu.make_async_remote_copy(
            src_ref=normed.at[spot], dst_ref=normed.at[spot],
            send_sem=n_send.at[k], recv_sem=n_recv.at[k],
            device_id=square[k], device_id_type=MESH)

    tiles = rs_send.shape[1]
    tile = rs_send.shape[3]

    def r_copy(n, k):
        return pltpu.make_async_remote_copy(
            src_ref=rs_send.at[k, n],
            dst_ref=rs_recv.at[k, n],
            send_sem=r_send.at[n, k], recv_sem=r_recv.at[n, k],
            device_id=square[k], device_id_type=MESH)

    loads = [
        pltpu.make_async_copy(far, near, in_sem.at[i])
        for i, (far, near) in enumerate((
            (w_qkv_in, w_qkv), (w_out_in, w_out), (w_up_in, w_up), (w_down_in, w_down),
            (hid_in, hid)))
    ]

    def stage(kind):
        loads[kind].wait()
        if kind == Q:
            for d in range(shards):
                for j in range(3):
                    stage_q[d, :, j * lw:(j + 1) * lw] = w_qkv[
                        :, j * width + d * lw:j * width + (d + 1) * lw].astype(b16)
        elif kind == O:
            stage_o[0] = w_out[...].astype(b16)
        else:
            source = w_up if kind == U else w_down
            for d in range(shards):
                stages[kind][d] = source[:, d * lh:(d + 1) * lh].astype(b16)
        fulls[kind][mine[kind]] = stages[kind][(m, 0, spot, spot)[kind]]

    barrier = pltpu.get_barrier_semaphore()
    everyone = [(g, peer) for peer in peers] + [(gx, m), (gy, m), (sib, m), (gx, m1)]
    for target in everyone:
        pl.semaphore_signal(barrier, inc=1, device_id=target, device_id_type=MESH)
    for load in loads:
        load.start()
    stage(Q)
    pl.semaphore_wait(barrier, len(everyone))

    def depart(kind):
        for k in range(shards - 1):
            z_copy(kind, k).start()

    depart(Q)
    stage(U)
    depart(U)
    stage(O)
    stage(W)

    long_id = jnp.where(core == 0, id_col[rows - 1:rows, :], id_col[0:1, :])
    slot = sib * rows + lax.broadcasted_iota(jnp.int32, (1, rows), 1)
    reach = jnp.where((slot > long_id - rows) & (slot <= long_id), long_id, -1)
    few = 32

    def bias_step(i, carry):
        here = pl.ds(pl.multiple_of(i * few, few), few)
        ids = id_col[here, :]
        bias[here, :rows] = jnp.where(ids == id_row[...], 0.0, -1e30).astype(f32)
        bias[here, rows:] = jnp.where(ids == reach, 0.0, -1e30).astype(f32)
        return carry

    lax.fori_loop(0, rows // few, bias_step, 0)
    for p in range(pairs):
        for i in range(2):
            vals_ones[p, i, :, 128:] = jnp.ones((rows, 128), b16)

    arrived(Q)
    go(Q, 0, 1, 3)
    depart(O)
    loads[4].wait()
    landed(Q, 0, 1)
    go(Q, 2, 4, 5)
    arrived(O)
    go(O, 0, 1, 3)
    arrived(U)
    go(U, 0)
    depart(W)
    landed(Q, 2)
    go(Q, 6)
    landed(Q, 3, 4, 5, 6)

    def project(i, carry):
        j = lax.rem(i + 1, 3)
        here = pl.ds(pl.multiple_of(j * lw, lw), lw)
        block = full_q[:, :, here].reshape(width, lw)
        some = jnp.dot(hid[...], block, preferred_element_type=f32).astype(b16)

        @pl.when(i < 2)
        def _():
            kv[i, 0] = some
            kv_copy(i).start()

        @pl.when(i == 2)
        def _():
            queries[...] = some * jnp.asarray(HD ** -0.5, b16)

        return carry

    lax.fori_loop(0, 3, project, 0)
    go(U, 1, 3)
    k_out[...] = kv[0, 0]
    v_out[...] = kv[1, 0]
    for i in range(2):
        kv_copy(i).wait_recv()
    landed(O, 0, 1)
    go(O, 2, 4, 5)
    for p in range(pairs):
        vals_ones[p, :, :, :128] = kv[1, :, :, p * 128:(p + 1) * 128]

    lane = lax.broadcasted_iota(jnp.int32, (share, 128), 1)
    own_rows = pl.ds(pl.multiple_of(m * share, share), share)

    def attend(p, carry):
        cols = pl.ds(pl.multiple_of(p * 128, 128), 128)

        def step(k, carry):
            here = pl.ds(pl.multiple_of(lax.rem(m + 1 + k, shards) * share, share), share)
            pair_q = queries[here, cols]
            halves = []
            for h in range(2):
                own = (lane < HD) if h == 0 else (lane >= HD)
                head_q = jnp.where(own, pair_q, jnp.zeros_like(pair_q))
                scores = lax.dot_general(
                    head_q, kv[0, :, :, cols].reshape(2 * rows, 128),
                    (((1,), (1,)), ((), ())), preferred_element_type=f32) + bias[here, :]
                peak = jnp.max(scores, axis=-1, keepdims=True)
                weights = jnp.exp(scores - peak).astype(b16)
                mixed = jnp.dot(
                    weights, vals_ones[p].reshape(2 * rows, 256), preferred_element_type=f32)
                halves.append(mixed[:, :128] / mixed[:, 128:])
            mixed_rows = jnp.where(lane < HD, halves[0], halves[1]).astype(b16)

            @pl.when(k < shards - 1)
            def _():
                att[p, k] = mixed_rows
                a_copy(p, k).start()

            @pl.when(k == shards - 1)
            def _():
                att_in[m * pairs + p] = mixed_rows

            return carry

        lax.fori_loop(0, shards, step, 0)

        @pl.when(p == 0)
        def _():
            landed(O, 2)
            go(O, 6)
            arrived(W)
            landed(U, 0)
            go(U, 2, 4)
            go(W, 0)

        return carry

    lax.fori_loop(0, pairs, attend, 0)
    landed(U, 1)
    go(U, 5)
    go(W, 1, 3)
    landed(O, 3, 4, 5, 6)
    for p in range(pairs):
        for k in range(shards - 1):
            a_copy(p, k).wait_recv()

    n_wide = 256
    o_parts = n_wide // part

    def out_step(n, carry):
        here = pl.ds(pl.multiple_of(n * n_wide, n_wide), n_wide)
        joined = jnp.concatenate([att_in[i] for i in range(shards * pairs)], axis=1)
        block = full_o[pl.ds(n * o_parts, o_parts)].reshape(n_wide, width)
        sums[:, here] = lax.dot_general(
            joined, block, (((1,), (1,)), ((), ())), preferred_element_type=f32)
        return carry

    lax.fori_loop(0, width // n_wide, out_step, 0)

    def ln_step(i, carry):
        here = pl.ds(pl.multiple_of(i * few, few), few)
        there = pl.ds(pl.multiple_of(m * share + i * few, few), few)
        normed[spot, here, :] = layer_norm(
            hid[there, :].astype(f32) + sums[here, :], gain1[...], shift1[...]).astype(b16)
        return carry

    lax.fori_loop(0, share // few, ln_step, 0)
    for k in (1, 0, 2):
        n_copy(k).start()
    landed(U, 2)
    go(U, 6)
    landed(W, 0)
    go(W, 2, 4)
    landed(W, 1)
    go(W, 5)
    landed(U, 3, 4, 5, 6)

    order = []
    for r in range(8 * shards):
        group_r, z_r = r // shards, r % shards
        order.append(((group_r // 4 * 2 + group_r % 2) * 2 + z_r // 2) * 4
                     + group_r // 2 % 2 * 2 + z_r % 2)
    d_parts = tile // part

    def feed(batch, carry):
        first = spot * (1 - batch) + square_spot[2] * batch
        second = square_spot[1] * (1 - batch) + square_spot[0] * batch

        @pl.when(batch == 0)
        def _():
            n_copy(1).wait_recv()

        @pl.when(batch == 1)
        def _():
            n_copy(0).wait_recv()
            n_copy(2).wait_recv()

        def up_step(n, carry):
            here = pl.ds(pl.multiple_of(n * n_wide, n_wide), n_wide)
            block = jnp.concatenate([full_u[r, :, here] for r in order], axis=0)
            tokens = jnp.concatenate([normed[first], normed[second]], axis=0)
            pre = jnp.dot(tokens, block, preferred_element_type=f32)
            act[:, here] = (0.5 * pre * (1.0 + lax.erf(pre * (0.5 ** 0.5)))).astype(b16)
            return carry

        lax.fori_loop(0, lh // n_wide, up_step, 0)

        @pl.when(batch == 0)
        def _():
            landed(W, 2)
            go(W, 6)
            landed(W, 3, 4, 5, 6)

        def down_step(n, carry):
            start = n // 2 * 16 + lax.rem(n, 2) * 2
            block = jnp.concatenate(
                [full_d[start + i // 4 * 8 + i % 4 // 2 * 4 + i % 2] for i in range(d_parts)], axis=0)
            term = lax.dot_general(
                act[...], block, (((1,), (1,)), ((), ())), preferred_element_type=f32)

            @pl.when(batch == 0)
            def _():
                rs_send[1, n] = term[share:].astype(b16)
                r_copy(n, 1).start()
                sums[:, pl.ds(pl.multiple_of(n * tile, tile), tile)] = term[:share]

            @pl.when(batch == 1)
            def _():
                rs_send[2, n] = term[:share].astype(b16)
                r_copy(n, 2).start()
                rs_send[0, n] = term[share:].astype(b16)
                r_copy(n, 0).start()

            return carry

        lax.fori_loop(0, tiles, down_step, 0)
        return carry

    lax.fori_loop(0, 2, feed, 0)

    def total_step(n, carry):
        cols = pl.ds(pl.multiple_of(n * tile, tile), tile)
        total = normed[spot, :, cols].astype(f32) + sums[:, cols]
        for k in (1, 0, 2):
            r_copy(n, k).wait_recv()
            total = total + rs_recv[k, n].astype(f32)
        sums[:, cols] = total
        return carry

    lax.fori_loop(0, tiles, total_step, 0)

    def last_step(i, carry):
        here = pl.ds(pl.multiple_of(i * few, few), few)
        out[here, :] = layer_norm(sums[here, :], gain2[...], shift2[...]).astype(b16)
        return carry

    lax.fori_loop(0, share // few, last_step, 0)

    for kind in (Q, O, U, W):
        for k in range(shards - 1):
            z_copy(kind, k).wait_send()
        for step in range(7):
            p_copy(kind, step).wait_send()
    for i in range(2):
        kv_copy(i).wait_send()
    for k in range(shards - 1):
        n_copy(k).wait_send()
        for p in range(pairs):
            a_copy(p, k).wait_send()
        for n in range(tiles):
            r_copy(n, k).wait_send()


def kernel_body(
    hidden_in, request_ids, w_qkv, w_out, w_up, w_down, ln1_gain, ln1_shift, ln2_gain, ln2_shift
):
    groups = lax.axis_size("group")
    shards = lax.axis_size("mp")
    rows, width = hidden_in.shape
    part = w_qkv.shape[0]
    parts = groups * shards
    lw = width // shards
    lh = w_up.shape[1] // shards
    share = rows // shards
    pairs = lw // 128
    tile = 256
    tiles = width // tile
    b16, f32 = jnp.bfloat16, jnp.float32
    vmem = pl.BlockSpec(memory_space=pltpu.VMEM)
    hbm = pl.BlockSpec(memory_space=pltpu.HBM)
    dma = pltpu.SemaphoreType.DMA
    others = shards - 1
    return pl.pallas_call(
        functools.partial(layer_kernel, shards),
        out_shape=(
            jax.ShapeDtypeStruct((share, width), b16),
            jax.ShapeDtypeStruct((rows, lw), b16),
            jax.ShapeDtypeStruct((rows, lw), b16),
        ),
        in_specs=[hbm] + [vmem] * 2 + [hbm] * 4 + [vmem] * 4,
        out_specs=(vmem,) * 3,
        scratch_shapes=[
            pltpu.VMEM((rows, width), b16),
            pltpu.VMEM(w_qkv.shape, f32),
            pltpu.VMEM(w_out.shape, f32),
            pltpu.VMEM(w_up.shape, f32),
            pltpu.VMEM(w_down.shape, f32),
            pltpu.VMEM((shards, part, 3 * lw), b16),
            pltpu.VMEM((1, part, width), b16),
            pltpu.VMEM((shards, part, lh), b16),
            pltpu.VMEM((shards, part, lh), b16),
            pltpu.VMEM((parts, part, 3 * lw), b16),
            pltpu.VMEM((parts, part, width), b16),
            pltpu.VMEM((parts, part, lh), b16),
            pltpu.VMEM((parts, part, lh), b16),
            pltpu.VMEM((rows, 2 * rows), f32),
            pltpu.VMEM((rows, lw), b16),
            pltpu.VMEM((2, 2, rows, lw), b16),
            pltpu.VMEM((pairs, 2, rows, 256), b16),
            pltpu.VMEM((pairs, others, share, 128), b16),
            pltpu.VMEM((shards * pairs, share, 128), b16),
            pltpu.VMEM((share, width), f32),
            pltpu.VMEM((shards, share, width), b16),
            pltpu.VMEM((rows // 2, lh), b16),
            pltpu.VMEM((others, tiles, share, tile), b16),
            pltpu.VMEM((others, tiles, share, tile), b16),
            dma((5,)),
            dma((4, others)), dma((4, others)),
            dma((4, 7)), dma((4, 7)),
            dma((2,)), dma((2,)),
            dma((pairs, others)), dma((pairs, others)),
            dma((others,)), dma((others,)),
            dma((tiles, others)), dma((tiles, others)),
        ],
        compiler_params=pltpu.CompilerParams(
            collective_id=0, has_side_effects=True, vmem_limit_bytes=56 * 1024 * 1024),
        cost_estimate=pl.CostEstimate(
            flops=6 * rows * width * (4 * lw + 2 * lh), bytes_accessed=16 * 1024 * 1024,
            transcendentals=0),
        name="encoder_layer",
    )(
        hidden_in, request_ids.reshape(rows, 1), request_ids.reshape(1, rows),
        w_qkv, w_out, w_up, w_down,
        ln1_gain.reshape(1, width), ln1_shift.reshape(1, width),
        ln2_gain.reshape(1, width), ln2_shift.reshape(1, width),
    )


def solution(mesh):
    in_specs = (
        P("group", None),
        P("group"),
        P(("group", "mp"), None),
        P(("group", "mp"), None),
        P(("group", "mp"), None),
        P(("group", "mp"), None),
        P(),
        P(),
        P(),
        P(),
    )
    out_specs = (P(("group", "mp"), None), P("group", "mp"), P("group", "mp"))
    whole_tiles = mesh.shape["group"] == 8 and mesh.shape["mp"] == 4
    body = kernel_body if whole_tiles else plain_body
    return jax.shard_map(body, mesh=mesh, in_specs=in_specs, out_specs=out_specs, check_vma=False)
```

```python
import functools

import jax
import jax.numpy as jnp
from jax import lax
from jax.experimental import pallas as pl
from jax.experimental.pallas import tpu as pltpu
from jax.sharding import PartitionSpec as P

HD = 64
SHORT = 64


def swapped(value, axis, distance):
    return lax.ppermute(value, axis, [(i, i ^ 1 << distance) for i in range(lax.axis_size(axis))])


def layer_norm(values_in, norm_gain, norm_shift):
    center = values_in - jnp.mean(values_in, axis=-1, keepdims=True)
    spread = jnp.mean(center * center, axis=-1, keepdims=True)
    return center * lax.rsqrt(spread + 1e-05) * norm_gain + norm_shift


def plain_body(
    hidden_in, request_ids, w_qkv, w_out, w_up, w_down, ln1_gain, ln1_shift, ln2_gain, ln2_shift
):
    groups = lax.axis_size("group")
    shards = lax.axis_size("mp")
    model_width = hidden_in.shape[1]
    local_width = model_width // shards
    local_hidden = w_up.shape[1] // shards
    tok_rows = hidden_in.shape[0]
    part_rows = w_qkv.shape[0]
    pieces = (
        w_qkv.astype(jnp.bfloat16).reshape(part_rows, 3, shards, local_width),
        w_out.astype(jnp.bfloat16).reshape(part_rows, 1, shards, local_width),
        w_up.astype(jnp.bfloat16).reshape(part_rows, 1, shards, local_hidden),
        w_down.astype(jnp.bfloat16).reshape(part_rows, 1, shards, local_hidden),
    )
    gathered = (
        lax.all_gather(pieces[0], "group", axis=0, tiled=True),
        lax.all_gather(pieces[1], "group", axis=0, tiled=True),
        lax.all_gather(pieces[2], "group", axis=0, tiled=True),
        lax.all_gather(pieces[3], "group", axis=0, tiled=True),
    )
    exchanged = (
        lax.all_to_all(gathered[0], "mp", split_axis=2, concat_axis=0, tiled=True),
        lax.all_to_all(gathered[1], "mp", split_axis=2, concat_axis=0, tiled=True),
        lax.all_to_all(gathered[2], "mp", split_axis=2, concat_axis=0, tiled=True),
        lax.all_to_all(gathered[3], "mp", split_axis=2, concat_axis=0, tiled=True),
    )
    served = tuple(
        (
            jnp.transpose(
                weight_piece.reshape(shards, groups, part_rows, -1), (1, 0, 2, 3)
            ).reshape(model_width, -1)
            for weight_piece in exchanged
        )
    )
    qkv_local, out_local, up_local, down_local = served
    projected = jnp.dot(hidden_in, qkv_local, preferred_element_type=jnp.float32)
    queries = projected[:, :local_width].astype(jnp.bfloat16)
    key_rows = projected[:, local_width : 2 * local_width].astype(jnp.bfloat16)
    value_rows = projected[:, 2 * local_width :].astype(jnp.bfloat16)
    partner_keys, partner_values = swapped((key_rows, value_rows), "group", 0)
    group_index = lax.axis_index("group")
    parity = group_index % 2
    long_id = jnp.where(parity == 0, request_ids[-1], request_ids[0])
    own_long = request_ids == long_id
    local_heads = local_width // HD
    score_scale = HD ** (-0.5)
    block_total = tok_rows // SHORT
    short_q = queries.reshape(block_total, SHORT, local_heads, HD)
    short_k = key_rows.reshape(block_total, SHORT, local_heads, HD)
    short_v = value_rows.reshape(block_total, SHORT, local_heads, HD)
    short_ids = request_ids.reshape(block_total, SHORT)
    short_scores = (
        jnp.einsum("bqhd,bkhd->bhqk", short_q, short_k, preferred_element_type=jnp.float32)
        * score_scale
    )
    short_mask = short_ids[:, :, None] == short_ids[:, None, :]
    short_scores = jnp.where(short_mask[:, None], short_scores, -1e30)
    short_peak = jnp.max(short_scores, axis=-1, keepdims=True)
    short_weights = jnp.exp(short_scores - short_peak).astype(jnp.bfloat16)
    short_totals = jnp.sum(short_weights.astype(jnp.float32), axis=-1)
    short_mixed = jnp.einsum(
        "bhqk,bkhd->bqhd", short_weights, short_v, preferred_element_type=jnp.float32
    )
    short_out = (
        (short_mixed / jnp.transpose(short_totals, (0, 2, 1))[:, :, :, None])
        .astype(jnp.bfloat16)
        .reshape(tok_rows, local_width)
    )
    first_keys = jnp.where(parity == 0, key_rows, partner_keys)
    second_keys = jnp.where(parity == 0, partner_keys, key_rows)
    first_values = jnp.where(parity == 0, value_rows, partner_values)
    second_values = jnp.where(parity == 0, partner_values, value_rows)
    pair_base = (group_index - parity) * tok_rows
    span_start = long_id - tok_rows + 1 - pair_base
    long_keys = lax.dynamic_slice_in_dim(
        jnp.concatenate([first_keys, second_keys], 0), span_start, tok_rows, 0
    ).reshape(tok_rows, local_heads, HD)
    long_values = lax.dynamic_slice_in_dim(
        jnp.concatenate([first_values, second_values], 0), span_start, tok_rows, 0
    ).reshape(tok_rows, local_heads, HD)
    query_rows = min(512, tok_rows)
    query_blocks = tok_rows // query_rows

    def long_attend(block_queries):
        heads_view = block_queries.reshape(query_rows, local_heads, HD)
        scores = (
            jnp.einsum("qhd,khd->hqk", heads_view, long_keys, preferred_element_type=jnp.float32)
            * score_scale
        )
        row_peak = jnp.max(scores, axis=-1, keepdims=True)
        weights = jnp.exp(scores - row_peak).astype(jnp.bfloat16)
        totals = jnp.sum(weights.astype(jnp.float32), axis=-1)
        mixed_heads = jnp.einsum(
            "hqk,khd->qhd", weights, long_values, preferred_element_type=jnp.float32
        )
        return (
            (mixed_heads / jnp.transpose(totals)[:, :, None])
            .astype(jnp.bfloat16)
            .reshape(query_rows, local_width)
        )

    def skipped(block_queries):
        return jnp.zeros((query_rows, local_width), jnp.bfloat16)

    def long_block(query_block):
        block_queries, block_long = query_block
        return lax.cond(jnp.any(block_long), long_attend, skipped, block_queries)

    long_out = lax.map(
        long_block,
        (
            queries.reshape(query_blocks, query_rows, local_width),
            own_long.reshape(query_blocks, query_rows),
        ),
    ).reshape(tok_rows, local_width)
    attended = jnp.where(own_long[:, None], long_out, short_out)
    share_rows = tok_rows // shards
    row_start = lax.axis_index("mp") * share_rows

    def combine(term_fn, residual, norm_gain, norm_shift):
        summed = lax.psum(term_fn(0, tok_rows), "mp")
        whole_rows = layer_norm(
            residual.astype(jnp.float32) + summed, norm_gain, norm_shift
        ).astype(jnp.bfloat16)
        normed = lax.dynamic_slice_in_dim(whole_rows, row_start, share_rows, 0)
        return (normed, whole_rows)

    def attn_term(row_begin, row_count):
        return lax.dot_general(
            attended, out_local, (((1,), (1,)), ((), ())), preferred_element_type=jnp.float32
        )

    attn_share, attn_normed = combine(attn_term, hidden_in, ln1_gain, ln1_shift)
    activated = jax.nn.gelu(
        jnp.dot(attn_normed, up_local, preferred_element_type=jnp.float32), approximate=False
    ).astype(jnp.bfloat16)

    def feed_term(row_begin, row_count):
        return lax.dot_general(
            activated, down_local, (((1,), (1,)), ((), ())), preferred_element_type=jnp.float32
        )

    final_share, unused = combine(feed_term, attn_normed, ln2_gain, ln2_shift)
    return (final_share, key_rows, value_rows)


MESH = pl.DeviceIdType.MESH
Q, O, U, W = range(4)


def layer_kernel(
    shards, hid_in, id_col, id_row, w_qkv_in, w_out_in, w_up_in, w_down_in,
    gain1, shift1, gain2, shift2,
    out, k_out, v_out,
    hid, w_qkv, w_out, w_up, w_down,
    stage_q, stage_o, stage_u, stage_d, full_q, full_o, full_u, full_d,
    bias, queries, kv, vals_ones, att, att_in, sums, normed, act, rs_send, rs_recv,
    in_sem, z_send, z_recv, p_send, p_recv, kv_send, kv_recv, a_send, a_recv,
    n_send, n_recv, r_send, r_recv,
):
    g = lax.axis_index("group")
    m = lax.axis_index("mp")
    core = lax.rem(g, 2)
    x = lax.rem(g // 2, 2)
    y = g // 4
    half = m // 2
    side = lax.rem(m, 2)
    sib = g + 1 - 2 * core
    gx = g + 2 - 4 * x
    gy = g + 4 - 8 * y
    gd = gx + gy - g
    m1 = m + 1 - 2 * side
    m2 = m + 2 - 4 * half
    rows = hid.shape[0]
    width = hid.shape[1]
    part = w_qkv.shape[0]
    lw = queries.shape[1]
    lh = act.shape[1]
    pairs = lw // 128
    share = rows // shards
    f32, b16 = jnp.float32, jnp.bfloat16
    fulls = (full_q, full_o, full_u, full_d)
    stages = (stage_q, stage_o, stage_u, stage_d)
    peers = [lax.rem(m + k, shards) for k in range(1, shards)]
    spot = 2 * x + side
    square = ((g, m1), (gx, m), (gx, m1))
    square_spot = (2 * x + 1 - side, 2 - 2 * x + side, 3 - 2 * x - side)

    def block_at(on_y, on_core, on_half):
        return (on_y * 2 + on_core) * 2 + on_half

    mine = (g * shards + m,) * 2 + (block_at(y, core, half) * 4 + spot,) * 2

    def z_copy(kind, k):
        if kind == Q:
            chunk, target = stage_q.at[peers[k]], (g, peers[k])
        elif kind == O:
            chunk, target = stage_o.at[0], (g, peers[k])
        else:
            chunk, target = stages[kind].at[square_spot[k]], square[k]
        return pltpu.make_async_remote_copy(
            src_ref=chunk, dst_ref=fulls[kind].at[mine[kind]],
            send_sem=z_send.at[kind, k], recv_sem=z_recv.at[kind, k],
            device_id=target, device_id_type=MESH)

    plane_hops = (
        (g, (gx, m)), (g, (gy, m)), (gy, (gx, m)),
        (g, (sib, m)), (gx, (sib, m)), (gy, (sib, m)), (gd, (sib, m)))
    b_own = block_at(y, core, half)
    b_z = block_at(y, core, 1 - half)
    b_y = block_at(1 - y, core, half)
    b_d = block_at(1 - y, core, 1 - half)
    hidden_hops = (
        (b_own, (g, m2)), (b_own, (gy, m)), (b_z, (gy, m)),
        (b_own, (sib, m)), (b_z, (sib, m)), (b_y, (sib, m)), (b_d, (sib, m)))

    def p_copy(kind, step):
        block, target = (plane_hops if kind in (Q, O) else hidden_hops)[step]
        place = fulls[kind].at[pl.ds(block * 4, 4)]
        return pltpu.make_async_remote_copy(
            src_ref=place, dst_ref=place,
            send_sem=p_send.at[kind, step], recv_sem=p_recv.at[kind, step],
            device_id=target, device_id_type=MESH)

    def arrived(kind):
        for k in range(shards - 1):
            z_copy(kind, k).wait_recv()

    def go(kind, *steps):
        for step in steps:
            p_copy(kind, step).start()

    def landed(kind, *steps):
        for step in steps:
            p_copy(kind, step).wait_recv()

    def kv_copy(i):
        return pltpu.make_async_remote_copy(
            src_ref=kv.at[i, 0], dst_ref=kv.at[i, 1],
            send_sem=kv_send.at[i], recv_sem=kv_recv.at[i],
            device_id=(sib, m), device_id_type=MESH)

    def a_copy(p, k):
        return pltpu.make_async_remote_copy(
            src_ref=att.at[p, k],
            dst_ref=att_in.at[m * pairs + p],
            send_sem=a_send.at[p, k], recv_sem=a_recv.at[p, k],
            device_id=(g, lax.rem(m + 1 + k, shards)), device_id_type=MESH)

    def n_copy(k):
        return pltpu.make_async_remote_copy(
            src_ref=normed.at[spot], dst_ref=normed.at[spot],
            send_sem=n_send.at[k], recv_sem=n_recv.at[k],
            device_id=square[k], device_id_type=MESH)

    tiles = rs_send.shape[1]
    tile = rs_send.shape[3]

    def r_copy(n, k):
        return pltpu.make_async_remote_copy(
            src_ref=rs_send.at[k, n],
            dst_ref=rs_recv.at[k, n],
            send_sem=r_send.at[n, k], recv_sem=r_recv.at[n, k],
            device_id=square[k], device_id_type=MESH)

    loads = [
        pltpu.make_async_copy(far, near, in_sem.at[i])
        for i, (far, near) in enumerate((
            (w_qkv_in, w_qkv), (w_out_in, w_out), (w_up_in, w_up), (w_down_in, w_down),
            (hid_in, hid)))
    ]

    def stage(kind):
        loads[kind].wait()
        if kind == Q:
            for d in range(shards):
                for j in range(3):
                    stage_q[d, :, j * lw:(j + 1) * lw] = w_qkv[
                        :, j * width + d * lw:j * width + (d + 1) * lw].astype(b16)
        elif kind == O:
            stage_o[0] = w_out[...].astype(b16)
        else:
            source = w_up if kind == U else w_down
            for d in range(shards):
                stages[kind][d] = source[:, d * lh:(d + 1) * lh].astype(b16)
        fulls[kind][mine[kind]] = stages[kind][(m, 0, spot, spot)[kind]]

    barrier = pltpu.get_barrier_semaphore()
    everyone = [(g, peer) for peer in peers] + [(gx, m), (gy, m), (sib, m), (gx, m1)]
    for target in everyone:
        pl.semaphore_signal(barrier, inc=1, device_id=target, device_id_type=MESH)
    for load in loads:
        load.start()
    stage(Q)
    pl.semaphore_wait(barrier, len(everyone))

    def depart(kind):
        for k in range(shards - 1):
            z_copy(kind, k).start()

    depart(Q)
    for kind in (U, O, W):
        stage(kind)
        depart(kind)

    long_id = jnp.where(core == 0, id_col[rows - 1:rows, :], id_col[0:1, :])
    slot = sib * rows + lax.broadcasted_iota(jnp.int32, (1, rows), 1)
    reach = jnp.where((slot > long_id - rows) & (slot <= long_id), long_id, -1)
    few = 32

    def bias_step(i, carry):
        here = pl.ds(pl.multiple_of(i * few, few), few)
        ids = id_col[here, :]
        bias[here, :rows] = jnp.where(ids == id_row[...], 0.0, -1e30).astype(f32)
        bias[here, rows:] = jnp.where(ids == reach, 0.0, -1e30).astype(f32)
        return carry

    lax.fori_loop(0, rows // few, bias_step, 0)
    for p in range(pairs):
        for i in range(2):
            vals_ones[p, i, :, 128:] = jnp.ones((rows, 128), b16)

    arrived(Q)
    go(Q, 0, 1, 3)
    arrived(U)
    go(U, 0, 1, 3)
    loads[4].wait()
    landed(Q, 0, 1)
    go(Q, 2, 4, 5)
    arrived(O)
    go(O, 0, 1, 3)
    arrived(W)
    go(W, 0, 1, 3)
    landed(Q, 2)
    go(Q, 6)
    landed(Q, 3, 4, 5, 6)

    def project(i, carry):
        j = lax.rem(i + 1, 3)
        here = pl.ds(pl.multiple_of(j * lw, lw), lw)
        block = full_q[:, :, here].reshape(width, lw)
        some = jnp.dot(hid[...], block, preferred_element_type=f32).astype(b16)

        @pl.when(i < 2)
        def _():
            kv[i, 0] = some
            kv_copy(i).start()

        @pl.when(i == 2)
        def _():
            queries[...] = some * jnp.asarray(HD ** -0.5, b16)

        return carry

    lax.fori_loop(0, 3, project, 0)
    k_out[...] = kv[0, 0]
    v_out[...] = kv[1, 0]
    for i in range(2):
        kv_copy(i).wait_recv()
    for p in range(pairs):
        vals_ones[p, :, :, :128] = kv[1, :, :, p * 128:(p + 1) * 128]

    lane = lax.broadcasted_iota(jnp.int32, (2 * share, 128), 1)
    own_rows = pl.ds(pl.multiple_of(m * share, share), share)

    def attend(p, carry):
        cols = pl.ds(pl.multiple_of(p * 128, 128), 128)

        def step(j, carry):
            spans = [
                pl.ds(pl.multiple_of(lax.rem(m + 1 + 2 * j + i, shards) * share, share), share)
                for i in range(2)
            ]
            pair_q = jnp.concatenate([queries[here, cols] for here in spans], axis=0)
            halves = []
            for h in range(2):
                own = (lane < HD) if h == 0 else (lane >= HD)
                head_q = jnp.where(own, pair_q, jnp.zeros_like(pair_q))
                scores = lax.dot_general(
                    head_q, kv[0, :, :, cols].reshape(2 * rows, 128),
                    (((1,), (1,)), ((), ())), preferred_element_type=f32)
                scores = scores + jnp.concatenate([bias[here, :] for here in spans], axis=0)
                peak = jnp.max(scores, axis=-1, keepdims=True)
                weights = jnp.exp(scores - peak).astype(b16)
                mixed = jnp.dot(
                    weights, vals_ones[p].reshape(2 * rows, 256), preferred_element_type=f32)
                halves.append(mixed[:, :128] / mixed[:, 128:])
            mixed_rows = jnp.where(lane < HD, halves[0], halves[1]).astype(b16)
            for i in range(2):
                k = 2 * j + i

                @pl.when(k < shards - 1)
                def _():
                    att[p, k] = mixed_rows[i * share:(i + 1) * share]
                    a_copy(p, k).start()

                @pl.when(k == shards - 1)
                def _():
                    att_in[m * pairs + p] = mixed_rows[i * share:(i + 1) * share]

            return carry

        lax.fori_loop(0, shards // 2, step, 0)

        @pl.when(p == 0)
        def _():
            landed(O, 0, 1)
            go(O, 2, 4, 5)

        return carry

    lax.fori_loop(0, pairs, attend, 0)
    landed(O, 2)
    go(O, 6)
    landed(U, 0, 1)
    go(U, 2, 4, 5)
    landed(O, 3, 4, 5, 6)
    for p in range(pairs):
        for k in range(shards - 1):
            a_copy(p, k).wait_recv()

    n_wide = 256
    o_parts = n_wide // part

    def out_step(n, carry):
        here = pl.ds(pl.multiple_of(n * n_wide, n_wide), n_wide)
        joined = jnp.concatenate([att_in[i] for i in range(shards * pairs)], axis=1)
        block = full_o[pl.ds(n * o_parts, o_parts)].reshape(n_wide, width)
        sums[:, here] = lax.dot_general(
            joined, block, (((1,), (1,)), ((), ())), preferred_element_type=f32)
        return carry

    lax.fori_loop(0, width // n_wide, out_step, 0)

    def ln_step(i, carry):
        here = pl.ds(pl.multiple_of(i * few, few), few)
        there = pl.ds(pl.multiple_of(m * share + i * few, few), few)
        normed[spot, here, :] = layer_norm(
            hid[there, :].astype(f32) + sums[here, :], gain1[...], shift1[...]).astype(b16)
        return carry

    lax.fori_loop(0, share // few, ln_step, 0)
    for k in (1, 0, 2):
        n_copy(k).start()
    landed(U, 2)
    go(U, 6)
    landed(W, 0, 1)
    go(W, 2, 4, 5)
    landed(U, 3, 4, 5, 6)

    order = []
    for r in range(8 * shards):
        group_r, z_r = r // shards, r % shards
        order.append(((group_r // 4 * 2 + group_r % 2) * 2 + z_r // 2) * 4
                     + group_r // 2 % 2 * 2 + z_r % 2)
    d_parts = tile // part

    def feed(batch, carry):
        first = spot * (1 - batch) + square_spot[2] * batch
        second = square_spot[1] * (1 - batch) + square_spot[0] * batch

        @pl.when(batch == 0)
        def _():
            n_copy(1).wait_recv()

        @pl.when(batch == 1)
        def _():
            n_copy(0).wait_recv()
            n_copy(2).wait_recv()

        def up_step(n, carry):
            here = pl.ds(pl.multiple_of(n * n_wide, n_wide), n_wide)
            block = jnp.concatenate([full_u[r, :, here] for r in order], axis=0)
            tokens = jnp.concatenate([normed[first], normed[second]], axis=0)
            pre = jnp.dot(tokens, block, preferred_element_type=f32)
            act[:, here] = (0.5 * pre * (1.0 + lax.erf(pre * (0.5 ** 0.5)))).astype(b16)
            return carry

        lax.fori_loop(0, lh // n_wide, up_step, 0)

        @pl.when(batch == 0)
        def _():
            landed(W, 2)
            go(W, 6)
            landed(W, 3, 4, 5, 6)

        def down_step(n, carry):
            start = n // 2 * 16 + lax.rem(n, 2) * 2
            block = jnp.concatenate(
                [full_d[start + i // 4 * 8 + i % 4 // 2 * 4 + i % 2] for i in range(d_parts)], axis=0)
            term = lax.dot_general(
                act[...], block, (((1,), (1,)), ((), ())), preferred_element_type=f32)

            @pl.when(batch == 0)
            def _():
                rs_send[1, n] = term[share:].astype(b16)
                r_copy(n, 1).start()
                sums[:, pl.ds(pl.multiple_of(n * tile, tile), tile)] = term[:share]

            @pl.when(batch == 1)
            def _():
                rs_send[2, n] = term[:share].astype(b16)
                r_copy(n, 2).start()
                rs_send[0, n] = term[share:].astype(b16)
                r_copy(n, 0).start()

            return carry

        lax.fori_loop(0, tiles, down_step, 0)
        return carry

    lax.fori_loop(0, 2, feed, 0)

    def total_step(n, carry):
        cols = pl.ds(pl.multiple_of(n * tile, tile), tile)
        total = normed[spot, :, cols].astype(f32) + sums[:, cols]
        for k in (1, 0, 2):
            r_copy(n, k).wait_recv()
            total = total + rs_recv[k, n].astype(f32)
        sums[:, cols] = total
        return carry

    lax.fori_loop(0, tiles, total_step, 0)

    def last_step(i, carry):
        here = pl.ds(pl.multiple_of(i * few, few), few)
        out[here, :] = layer_norm(sums[here, :], gain2[...], shift2[...]).astype(b16)
        return carry

    lax.fori_loop(0, share // few, last_step, 0)

    for kind in (Q, O, U, W):
        for k in range(shards - 1):
            z_copy(kind, k).wait_send()
        for step in range(7):
            p_copy(kind, step).wait_send()
    for i in range(2):
        kv_copy(i).wait_send()
    for k in range(shards - 1):
        n_copy(k).wait_send()
        for p in range(pairs):
            a_copy(p, k).wait_send()
        for n in range(tiles):
            r_copy(n, k).wait_send()


def kernel_body(
    hidden_in, request_ids, w_qkv, w_out, w_up, w_down, ln1_gain, ln1_shift, ln2_gain, ln2_shift
):
    groups = lax.axis_size("group")
    shards = lax.axis_size("mp")
    rows, width = hidden_in.shape
    part = w_qkv.shape[0]
    parts = groups * shards
    lw = width // shards
    lh = w_up.shape[1] // shards
    share = rows // shards
    pairs = lw // 128
    tile = 256
    tiles = width // tile
    b16, f32 = jnp.bfloat16, jnp.float32
    vmem = pl.BlockSpec(memory_space=pltpu.VMEM)
    hbm = pl.BlockSpec(memory_space=pltpu.HBM)
    dma = pltpu.SemaphoreType.DMA
    others = shards - 1
    return pl.pallas_call(
        functools.partial(layer_kernel, shards),
        out_shape=(
            jax.ShapeDtypeStruct((share, width), b16),
            jax.ShapeDtypeStruct((rows, lw), b16),
            jax.ShapeDtypeStruct((rows, lw), b16),
        ),
        in_specs=[hbm] + [vmem] * 2 + [hbm] * 4 + [vmem] * 4,
        out_specs=(vmem,) * 3,
        scratch_shapes=[
            pltpu.VMEM((rows, width), b16),
            pltpu.VMEM(w_qkv.shape, f32),
            pltpu.VMEM(w_out.shape, f32),
            pltpu.VMEM(w_up.shape, f32),
            pltpu.VMEM(w_down.shape, f32),
            pltpu.VMEM((shards, part, 3 * lw), b16),
            pltpu.VMEM((1, part, width), b16),
            pltpu.VMEM((shards, part, lh), b16),
            pltpu.VMEM((shards, part, lh), b16),
            pltpu.VMEM((parts, part, 3 * lw), b16),
            pltpu.VMEM((parts, part, width), b16),
            pltpu.VMEM((parts, part, lh), b16),
            pltpu.VMEM((parts, part, lh), b16),
            pltpu.VMEM((rows, 2 * rows), f32),
            pltpu.VMEM((rows, lw), b16),
            pltpu.VMEM((2, 2, rows, lw), b16),
            pltpu.VMEM((pairs, 2, rows, 256), b16),
            pltpu.VMEM((pairs, others, share, 128), b16),
            pltpu.VMEM((shards * pairs, share, 128), b16),
            pltpu.VMEM((share, width), f32),
            pltpu.VMEM((shards, share, width), b16),
            pltpu.VMEM((rows // 2, lh), b16),
            pltpu.VMEM((others, tiles, share, tile), b16),
            pltpu.VMEM((others, tiles, share, tile), b16),
            dma((5,)),
            dma((4, others)), dma((4, others)),
            dma((4, 7)), dma((4, 7)),
            dma((2,)), dma((2,)),
            dma((pairs, others)), dma((pairs, others)),
            dma((others,)), dma((others,)),
            dma((tiles, others)), dma((tiles, others)),
        ],
        compiler_params=pltpu.CompilerParams(
            collective_id=0, has_side_effects=True, vmem_limit_bytes=56 * 1024 * 1024),
        cost_estimate=pl.CostEstimate(
            flops=6 * rows * width * (4 * lw + 2 * lh), bytes_accessed=16 * 1024 * 1024,
            transcendentals=0),
        name="encoder_layer",
    )(
        hidden_in, request_ids.reshape(rows, 1), request_ids.reshape(1, rows),
        w_qkv, w_out, w_up, w_down,
        ln1_gain.reshape(1, width), ln1_shift.reshape(1, width),
        ln2_gain.reshape(1, width), ln2_shift.reshape(1, width),
    )


def solution(mesh):
    in_specs = (
        P("group", None),
        P("group"),
        P(("group", "mp"), None),
        P(("group", "mp"), None),
        P(("group", "mp"), None),
        P(("group", "mp"), None),
        P(),
        P(),
        P(),
        P(),
    )
    out_specs = (P(("group", "mp"), None), P("group", "mp"), P("group", "mp"))
    whole_tiles = mesh.shape["group"] == 8 and mesh.shape["mp"] == 4
    body = kernel_body if whole_tiles else plain_body
    return jax.shard_map(body, mesh=mesh, in_specs=in_specs, out_specs=out_specs, check_vma=False)
```

```python
import functools

import jax
import jax.numpy as jnp
from jax import lax
from jax.experimental import pallas as pl
from jax.experimental.pallas import tpu as pltpu
from jax.sharding import PartitionSpec as P

HD = 64
SHORT = 64


def swapped(value, axis, distance):
    return lax.ppermute(value, axis, [(i, i ^ 1 << distance) for i in range(lax.axis_size(axis))])


def layer_norm(values_in, norm_gain, norm_shift):
    center = values_in - jnp.mean(values_in, axis=-1, keepdims=True)
    spread = jnp.mean(center * center, axis=-1, keepdims=True)
    return center * lax.rsqrt(spread + 1e-05) * norm_gain + norm_shift


def plain_body(
    hidden_in, request_ids, w_qkv, w_out, w_up, w_down, ln1_gain, ln1_shift, ln2_gain, ln2_shift
):
    groups = lax.axis_size("group")
    shards = lax.axis_size("mp")
    model_width = hidden_in.shape[1]
    local_width = model_width // shards
    local_hidden = w_up.shape[1] // shards
    tok_rows = hidden_in.shape[0]
    part_rows = w_qkv.shape[0]
    pieces = (
        w_qkv.astype(jnp.bfloat16).reshape(part_rows, 3, shards, local_width),
        w_out.astype(jnp.bfloat16).reshape(part_rows, 1, shards, local_width),
        w_up.astype(jnp.bfloat16).reshape(part_rows, 1, shards, local_hidden),
        w_down.astype(jnp.bfloat16).reshape(part_rows, 1, shards, local_hidden),
    )
    gathered = (
        lax.all_gather(pieces[0], "group", axis=0, tiled=True),
        lax.all_gather(pieces[1], "group", axis=0, tiled=True),
        lax.all_gather(pieces[2], "group", axis=0, tiled=True),
        lax.all_gather(pieces[3], "group", axis=0, tiled=True),
    )
    exchanged = (
        lax.all_to_all(gathered[0], "mp", split_axis=2, concat_axis=0, tiled=True),
        lax.all_to_all(gathered[1], "mp", split_axis=2, concat_axis=0, tiled=True),
        lax.all_to_all(gathered[2], "mp", split_axis=2, concat_axis=0, tiled=True),
        lax.all_to_all(gathered[3], "mp", split_axis=2, concat_axis=0, tiled=True),
    )
    served = tuple(
        (
            jnp.transpose(
                weight_piece.reshape(shards, groups, part_rows, -1), (1, 0, 2, 3)
            ).reshape(model_width, -1)
            for weight_piece in exchanged
        )
    )
    qkv_local, out_local, up_local, down_local = served
    projected = jnp.dot(hidden_in, qkv_local, preferred_element_type=jnp.float32)
    queries = projected[:, :local_width].astype(jnp.bfloat16)
    key_rows = projected[:, local_width : 2 * local_width].astype(jnp.bfloat16)
    value_rows = projected[:, 2 * local_width :].astype(jnp.bfloat16)
    partner_keys, partner_values = swapped((key_rows, value_rows), "group", 0)
    group_index = lax.axis_index("group")
    parity = group_index % 2
    long_id = jnp.where(parity == 0, request_ids[-1], request_ids[0])
    own_long = request_ids == long_id
    local_heads = local_width // HD
    score_scale = HD ** (-0.5)
    block_total = tok_rows // SHORT
    short_q = queries.reshape(block_total, SHORT, local_heads, HD)
    short_k = key_rows.reshape(block_total, SHORT, local_heads, HD)
    short_v = value_rows.reshape(block_total, SHORT, local_heads, HD)
    short_ids = request_ids.reshape(block_total, SHORT)
    short_scores = (
        jnp.einsum("bqhd,bkhd->bhqk", short_q, short_k, preferred_element_type=jnp.float32)
        * score_scale
    )
    short_mask = short_ids[:, :, None] == short_ids[:, None, :]
    short_scores = jnp.where(short_mask[:, None], short_scores, -1e30)
    short_peak = jnp.max(short_scores, axis=-1, keepdims=True)
    short_weights = jnp.exp(short_scores - short_peak).astype(jnp.bfloat16)
    short_totals = jnp.sum(short_weights.astype(jnp.float32), axis=-1)
    short_mixed = jnp.einsum(
        "bhqk,bkhd->bqhd", short_weights, short_v, preferred_element_type=jnp.float32
    )
    short_out = (
        (short_mixed / jnp.transpose(short_totals, (0, 2, 1))[:, :, :, None])
        .astype(jnp.bfloat16)
        .reshape(tok_rows, local_width)
    )
    first_keys = jnp.where(parity == 0, key_rows, partner_keys)
    second_keys = jnp.where(parity == 0, partner_keys, key_rows)
    first_values = jnp.where(parity == 0, value_rows, partner_values)
    second_values = jnp.where(parity == 0, partner_values, value_rows)
    pair_base = (group_index - parity) * tok_rows
    span_start = long_id - tok_rows + 1 - pair_base
    long_keys = lax.dynamic_slice_in_dim(
        jnp.concatenate([first_keys, second_keys], 0), span_start, tok_rows, 0
    ).reshape(tok_rows, local_heads, HD)
    long_values = lax.dynamic_slice_in_dim(
        jnp.concatenate([first_values, second_values], 0), span_start, tok_rows, 0
    ).reshape(tok_rows, local_heads, HD)
    query_rows = min(512, tok_rows)
    query_blocks = tok_rows // query_rows

    def long_attend(block_queries):
        heads_view = block_queries.reshape(query_rows, local_heads, HD)
        scores = (
            jnp.einsum("qhd,khd->hqk", heads_view, long_keys, preferred_element_type=jnp.float32)
            * score_scale
        )
        row_peak = jnp.max(scores, axis=-1, keepdims=True)
        weights = jnp.exp(scores - row_peak).astype(jnp.bfloat16)
        totals = jnp.sum(weights.astype(jnp.float32), axis=-1)
        mixed_heads = jnp.einsum(
            "hqk,khd->qhd", weights, long_values, preferred_element_type=jnp.float32
        )
        return (
            (mixed_heads / jnp.transpose(totals)[:, :, None])
            .astype(jnp.bfloat16)
            .reshape(query_rows, local_width)
        )

    def skipped(block_queries):
        return jnp.zeros((query_rows, local_width), jnp.bfloat16)

    def long_block(query_block):
        block_queries, block_long = query_block
        return lax.cond(jnp.any(block_long), long_attend, skipped, block_queries)

    long_out = lax.map(
        long_block,
        (
            queries.reshape(query_blocks, query_rows, local_width),
            own_long.reshape(query_blocks, query_rows),
        ),
    ).reshape(tok_rows, local_width)
    attended = jnp.where(own_long[:, None], long_out, short_out)
    share_rows = tok_rows // shards
    row_start = lax.axis_index("mp") * share_rows

    def combine(term_fn, residual, norm_gain, norm_shift):
        summed = lax.psum(term_fn(0, tok_rows), "mp")
        whole_rows = layer_norm(
            residual.astype(jnp.float32) + summed, norm_gain, norm_shift
        ).astype(jnp.bfloat16)
        normed = lax.dynamic_slice_in_dim(whole_rows, row_start, share_rows, 0)
        return (normed, whole_rows)

    def attn_term(row_begin, row_count):
        return lax.dot_general(
            attended, out_local, (((1,), (1,)), ((), ())), preferred_element_type=jnp.float32
        )

    attn_share, attn_normed = combine(attn_term, hidden_in, ln1_gain, ln1_shift)
    activated = jax.nn.gelu(
        jnp.dot(attn_normed, up_local, preferred_element_type=jnp.float32), approximate=False
    ).astype(jnp.bfloat16)

    def feed_term(row_begin, row_count):
        return lax.dot_general(
            activated, down_local, (((1,), (1,)), ((), ())), preferred_element_type=jnp.float32
        )

    final_share, unused = combine(feed_term, attn_normed, ln2_gain, ln2_shift)
    return (final_share, key_rows, value_rows)


MESH = pl.DeviceIdType.MESH
Q, O, U, W = range(4)


def layer_kernel(
    shards, hid_in, id_col, id_row, w_qkv_in, w_out_in, w_up_in, w_down_in,
    gain1, shift1, gain2, shift2,
    out, k_out, v_out,
    hid, w_qkv, w_out, w_up, w_down,
    stage_q, stage_o, stage_u, stage_d, full_q, full_o, full_u, full_d,
    bias, queries, kv, vals_ones, att, att_in, sums, normed, act, rs_send, rs_recv,
    in_sem, z_send, z_recv, p_send, p_recv, kv_send, kv_recv, a_send, a_recv,
    n_send, n_recv, r_send, r_recv,
):
    g = lax.axis_index("group")
    m = lax.axis_index("mp")
    core = lax.rem(g, 2)
    x = lax.rem(g // 2, 2)
    y = g // 4
    half = m // 2
    side = lax.rem(m, 2)
    sib = g + 1 - 2 * core
    gx = g + 2 - 4 * x
    gy = g + 4 - 8 * y
    gd = gx + gy - g
    m1 = m + 1 - 2 * side
    m2 = m + 2 - 4 * half
    rows = hid.shape[0]
    width = hid.shape[1]
    part = w_qkv.shape[0]
    lw = queries.shape[1]
    lh = act.shape[1]
    pairs = lw // 128
    share = rows // shards
    f32, b16 = jnp.float32, jnp.bfloat16
    fulls = (full_q, full_o, full_u, full_d)
    stages = (stage_q, stage_o, stage_u, stage_d)
    peers = [lax.rem(m + k, shards) for k in range(1, shards)]
    spot = 2 * x + side
    square = ((g, m1), (gx, m), (gx, m1))
    square_spot = (2 * x + 1 - side, 2 - 2 * x + side, 3 - 2 * x - side)

    def block_at(on_y, on_core, on_half):
        return (on_y * 2 + on_core) * 2 + on_half

    mine = (g * shards + m,) * 2 + (block_at(y, core, half) * 4 + spot,) * 2

    def z_copy(kind, k):
        if kind == Q:
            chunk, target = stage_q.at[peers[k]], (g, peers[k])
        elif kind == O:
            chunk, target = stage_o.at[0], (g, peers[k])
        else:
            chunk, target = stages[kind].at[square_spot[k]], square[k]
        return pltpu.make_async_remote_copy(
            src_ref=chunk, dst_ref=fulls[kind].at[mine[kind]],
            send_sem=z_send.at[kind, k], recv_sem=z_recv.at[kind, k],
            device_id=target, device_id_type=MESH)

    plane_hops = (
        (g, (gx, m)), (g, (gy, m)), (gy, (gx, m)),
        (g, (sib, m)), (gx, (sib, m)), (gy, (sib, m)), (gd, (sib, m)))
    b_own = block_at(y, core, half)
    b_z = block_at(y, core, 1 - half)
    b_y = block_at(1 - y, core, half)
    b_d = block_at(1 - y, core, 1 - half)
    hidden_hops = (
        (b_own, (g, m2)), (b_own, (gy, m)), (b_z, (gy, m)),
        (b_own, (sib, m)), (b_z, (sib, m)), (b_y, (sib, m)), (b_d, (sib, m)))

    def p_copy(kind, step):
        block, target = (plane_hops if kind in (Q, O) else hidden_hops)[step]
        place = fulls[kind].at[pl.ds(block * 4, 4)]
        return pltpu.make_async_remote_copy(
            src_ref=place, dst_ref=place,
            send_sem=p_send.at[kind, step], recv_sem=p_recv.at[kind, step],
            device_id=target, device_id_type=MESH)

    def arrived(kind):
        for k in range(shards - 1):
            z_copy(kind, k).wait_recv()

    def go(kind, *steps):
        for step in steps:
            p_copy(kind, step).start()

    def landed(kind, *steps):
        for step in steps:
            p_copy(kind, step).wait_recv()

    def kv_copy(i):
        return pltpu.make_async_remote_copy(
            src_ref=kv.at[i, 0], dst_ref=kv.at[i, 1],
            send_sem=kv_send.at[i], recv_sem=kv_recv.at[i],
            device_id=(sib, m), device_id_type=MESH)

    def a_copy(p, k):
        return pltpu.make_async_remote_copy(
            src_ref=att.at[p, k],
            dst_ref=att_in.at[m * pairs + p],
            send_sem=a_send.at[p, k], recv_sem=a_recv.at[p, k],
            device_id=(g, lax.rem(m + 1 + k, shards)), device_id_type=MESH)

    def n_copy(k):
        return pltpu.make_async_remote_copy(
            src_ref=normed.at[spot], dst_ref=normed.at[spot],
            send_sem=n_send.at[k], recv_sem=n_recv.at[k],
            device_id=square[k], device_id_type=MESH)

    tiles = rs_send.shape[1]
    tile = rs_send.shape[3]

    def r_copy(n, k):
        return pltpu.make_async_remote_copy(
            src_ref=rs_send.at[k, n],
            dst_ref=rs_recv.at[k, n],
            send_sem=r_send.at[n, k], recv_sem=r_recv.at[n, k],
            device_id=square[k], device_id_type=MESH)

    loads = [
        pltpu.make_async_copy(far, near, in_sem.at[i])
        for i, (far, near) in enumerate((
            (w_qkv_in, w_qkv), (w_out_in, w_out), (w_up_in, w_up), (w_down_in, w_down),
            (hid_in, hid)))
    ]

    def stage(kind):
        loads[kind].wait()
        if kind == Q:
            for d in range(shards):
                for j in range(3):
                    stage_q[d, :, j * lw:(j + 1) * lw] = w_qkv[
                        :, j * width + d * lw:j * width + (d + 1) * lw].astype(b16)
        elif kind == O:
            stage_o[0] = w_out[...].astype(b16)
        else:
            source = w_up if kind == U else w_down
            for d in range(shards):
                stages[kind][d] = source[:, d * lh:(d + 1) * lh].astype(b16)
        fulls[kind][mine[kind]] = stages[kind][(m, 0, spot, spot)[kind]]

    barrier = pltpu.get_barrier_semaphore()
    everyone = [(g, peer) for peer in peers] + [(gx, m), (gy, m), (sib, m), (gx, m1)]
    for target in everyone:
        pl.semaphore_signal(barrier, inc=1, device_id=target, device_id_type=MESH)
    for load in loads:
        load.start()
    stage(Q)
    pl.semaphore_wait(barrier, len(everyone))

    def depart(kind):
        for k in range(shards - 1):
            z_copy(kind, k).start()

    depart(Q)
    for kind in (U, O, W):
        stage(kind)
        depart(kind)

    long_id = jnp.where(core == 0, id_col[rows - 1:rows, :], id_col[0:1, :])
    slot = sib * rows + lax.broadcasted_iota(jnp.int32, (1, rows), 1)
    reach = jnp.where((slot > long_id - rows) & (slot <= long_id), long_id, -1)
    few = 32

    def bias_step(i, carry):
        here = pl.ds(pl.multiple_of(i * few, few), few)
        ids = id_col[here, :]
        bias[here, :rows] = jnp.where(ids == id_row[...], 0.0, -1e30).astype(f32)
        bias[here, rows:] = jnp.where(ids == reach, 0.0, -1e30).astype(f32)
        return carry

    lax.fori_loop(0, rows // few, bias_step, 0)
    for p in range(pairs):
        for i in range(2):
            vals_ones[p, i, :, 128:] = jnp.ones((rows, 128), b16)

    arrived(Q)
    go(Q, 0, 1, 3)
    arrived(U)
    go(U, 0, 1, 3)
    loads[4].wait()
    landed(Q, 0, 1)
    go(Q, 2, 4, 5)
    arrived(O)
    go(O, 0, 1, 3)
    arrived(W)
    go(W, 1, 3)
    landed(Q, 2)
    go(Q, 6)
    landed(Q, 3, 4, 5, 6)

    def project(i, carry):
        j = lax.rem(i + 1, 3)
        here = pl.ds(pl.multiple_of(j * lw, lw), lw)
        block = full_q[:, :, here].reshape(width, lw)
        some = jnp.dot(hid[...], block, preferred_element_type=f32).astype(b16)

        @pl.when(i < 2)
        def _():
            kv[i, 0] = some
            kv_copy(i).start()

        @pl.when(i == 2)
        def _():
            queries[...] = some * jnp.asarray(HD ** -0.5, b16)

        return carry

    lax.fori_loop(0, 3, project, 0)
    go(W, 0)
    k_out[...] = kv[0, 0]
    v_out[...] = kv[1, 0]
    for i in range(2):
        kv_copy(i).wait_recv()
    for p in range(pairs):
        vals_ones[p, :, :, :128] = kv[1, :, :, p * 128:(p + 1) * 128]

    lane = lax.broadcasted_iota(jnp.int32, (2 * share, 128), 1)

    def attend(p, carry):
        cols = pl.ds(pl.multiple_of(p * 128, 128), 128)

        def step(j, carry):
            spans = [
                pl.ds(pl.multiple_of(lax.rem(m + 1 + 2 * j + i, shards) * share, share), share)
                for i in range(2)
            ]
            pair_q = jnp.concatenate([queries[here, cols] for here in spans], axis=0)
            halves = []
            for h in range(2):
                own = (lane < HD) if h == 0 else (lane >= HD)
                head_q = jnp.where(own, pair_q, jnp.zeros_like(pair_q))
                scores = lax.dot_general(
                    head_q, kv[0, :, :, cols].reshape(2 * rows, 128),
                    (((1,), (1,)), ((), ())), preferred_element_type=f32)
                scores = scores + jnp.concatenate([bias[here, :] for here in spans], axis=0)
                peak = jnp.max(scores, axis=-1, keepdims=True)
                weights = jnp.exp(scores - peak).astype(b16)
                mixed = jnp.dot(
                    weights, vals_ones[p].reshape(2 * rows, 256), preferred_element_type=f32)
                halves.append(mixed[:, :128] / mixed[:, 128:])
            mixed_rows = jnp.where(lane < HD, halves[0], halves[1]).astype(b16)
            for i in range(2):
                k = 2 * j + i

                @pl.when(k < shards - 1)
                def _():
                    att[p, k] = mixed_rows[i * share:(i + 1) * share]
                    a_copy(p, k).start()

                @pl.when(k == shards - 1)
                def _():
                    att_in[m * pairs + p] = mixed_rows[i * share:(i + 1) * share]

            return carry

        lax.fori_loop(0, shards // 2, step, 0)

        @pl.when(p == 0)
        def _():
            landed(O, 0, 1)
            go(O, 2, 4, 5)

        return carry

    lax.fori_loop(0, pairs, attend, 0)
    landed(O, 2)
    go(O, 6)
    landed(O, 3, 4, 5, 6)
    for p in range(pairs):
        for k in range(shards - 1):
            a_copy(p, k).wait_recv()

    n_wide = 256
    o_parts = n_wide // part

    def out_step(n, carry):
        here = pl.ds(pl.multiple_of(n * n_wide, n_wide), n_wide)
        joined = jnp.concatenate([att_in[i] for i in range(shards * pairs)], axis=1)
        block = full_o[pl.ds(n * o_parts, o_parts)].reshape(n_wide, width)
        sums[:, here] = lax.dot_general(
            joined, block, (((1,), (1,)), ((), ())), preferred_element_type=f32)
        return carry

    lax.fori_loop(0, width // n_wide, out_step, 0)

    def ln_step(i, carry):
        here = pl.ds(pl.multiple_of(i * few, few), few)
        there = pl.ds(pl.multiple_of(m * share + i * few, few), few)
        normed[spot, here, :] = layer_norm(
            hid[there, :].astype(f32) + sums[here, :], gain1[...], shift1[...]).astype(b16)
        return carry

    lax.fori_loop(0, share // few, ln_step, 0)
    for k in (1, 0, 2):
        n_copy(k).start()
    landed(U, 0, 1)
    go(U, 2, 4, 5)
    landed(W, 1)
    go(W, 5)
    landed(U, 2)
    go(U, 6)
    landed(W, 0)
    go(W, 2, 4)
    landed(U, 3, 4, 5, 6)

    order = []
    for r in range(8 * shards):
        group_r, z_r = r // shards, r % shards
        order.append(((group_r // 4 * 2 + group_r % 2) * 2 + z_r // 2) * 4
                     + group_r // 2 % 2 * 2 + z_r % 2)
    d_parts = tile // part

    def feed(batch, carry):
        first = spot * (1 - batch) + square_spot[2] * batch
        second = square_spot[1] * (1 - batch) + square_spot[0] * batch

        @pl.when(batch == 0)
        def _():
            n_copy(1).wait_recv()

        @pl.when(batch == 1)
        def _():
            n_copy(0).wait_recv()
            n_copy(2).wait_recv()

        def up_step(n, carry):
            here = pl.ds(pl.multiple_of(n * n_wide, n_wide), n_wide)
            block = jnp.concatenate([full_u[r, :, here] for r in order], axis=0)
            tokens = jnp.concatenate([normed[first], normed[second]], axis=0)
            pre = jnp.dot(tokens, block, preferred_element_type=f32)
            act[:, here] = (0.5 * pre * (1.0 + lax.erf(pre * (0.5 ** 0.5)))).astype(b16)
            return carry

        lax.fori_loop(0, lh // n_wide, up_step, 0)

        @pl.when(batch == 0)
        def _():
            landed(W, 2)
            go(W, 6)
            landed(W, 3, 4, 5, 6)

        def down_step(n, carry):
            start = n // 2 * 16 + lax.rem(n, 2) * 2
            block = jnp.concatenate(
                [full_d[start + i // 4 * 8 + i % 4 // 2 * 4 + i % 2] for i in range(d_parts)], axis=0)
            term = lax.dot_general(
                act[...], block, (((1,), (1,)), ((), ())), preferred_element_type=f32)

            @pl.when(batch == 0)
            def _():
                rs_send[1, n] = term[share:].astype(b16)
                r_copy(n, 1).start()
                sums[:, pl.ds(pl.multiple_of(n * tile, tile), tile)] = term[:share]

            @pl.when(batch == 1)
            def _():
                rs_send[2, n] = term[:share].astype(b16)
                r_copy(n, 2).start()
                rs_send[0, n] = term[share:].astype(b16)
                r_copy(n, 0).start()

            return carry

        lax.fori_loop(0, tiles, down_step, 0)
        return carry

    lax.fori_loop(0, 2, feed, 0)

    def total_step(n, carry):
        cols = pl.ds(pl.multiple_of(n * tile, tile), tile)
        total = normed[spot, :, cols].astype(f32) + sums[:, cols]
        for k in (1, 0, 2):
            r_copy(n, k).wait_recv()
            total = total + rs_recv[k, n].astype(f32)
        sums[:, cols] = total
        return carry

    lax.fori_loop(0, tiles, total_step, 0)

    def last_step(i, carry):
        here = pl.ds(pl.multiple_of(i * few, few), few)
        out[here, :] = layer_norm(sums[here, :], gain2[...], shift2[...]).astype(b16)
        return carry

    lax.fori_loop(0, share // few, last_step, 0)

    for kind in (Q, O, U, W):
        for k in range(shards - 1):
            z_copy(kind, k).wait_send()
        for step in range(7):
            p_copy(kind, step).wait_send()
    for i in range(2):
        kv_copy(i).wait_send()
    for k in range(shards - 1):
        n_copy(k).wait_send()
        for p in range(pairs):
            a_copy(p, k).wait_send()
        for n in range(tiles):
            r_copy(n, k).wait_send()


def kernel_body(
    hidden_in, request_ids, w_qkv, w_out, w_up, w_down, ln1_gain, ln1_shift, ln2_gain, ln2_shift
):
    groups = lax.axis_size("group")
    shards = lax.axis_size("mp")
    rows, width = hidden_in.shape
    part = w_qkv.shape[0]
    parts = groups * shards
    lw = width // shards
    lh = w_up.shape[1] // shards
    share = rows // shards
    pairs = lw // 128
    tile = 256
    tiles = width // tile
    b16, f32 = jnp.bfloat16, jnp.float32
    vmem = pl.BlockSpec(memory_space=pltpu.VMEM)
    hbm = pl.BlockSpec(memory_space=pltpu.HBM)
    dma = pltpu.SemaphoreType.DMA
    others = shards - 1
    return pl.pallas_call(
        functools.partial(layer_kernel, shards),
        out_shape=(
            jax.ShapeDtypeStruct((share, width), b16),
            jax.ShapeDtypeStruct((rows, lw), b16),
            jax.ShapeDtypeStruct((rows, lw), b16),
        ),
        in_specs=[hbm] + [vmem] * 2 + [hbm] * 4 + [vmem] * 4,
        out_specs=(vmem,) * 3,
        scratch_shapes=[
            pltpu.VMEM((rows, width), b16),
            pltpu.VMEM(w_qkv.shape, f32),
            pltpu.VMEM(w_out.shape, f32),
            pltpu.VMEM(w_up.shape, f32),
            pltpu.VMEM(w_down.shape, f32),
            pltpu.VMEM((shards, part, 3 * lw), b16),
            pltpu.VMEM((1, part, width), b16),
            pltpu.VMEM((shards, part, lh), b16),
            pltpu.VMEM((shards, part, lh), b16),
            pltpu.VMEM((parts, part, 3 * lw), b16),
            pltpu.VMEM((parts, part, width), b16),
            pltpu.VMEM((parts, part, lh), b16),
            pltpu.VMEM((parts, part, lh), b16),
            pltpu.VMEM((rows, 2 * rows), f32),
            pltpu.VMEM((rows, lw), b16),
            pltpu.VMEM((2, 2, rows, lw), b16),
            pltpu.VMEM((pairs, 2, rows, 256), b16),
            pltpu.VMEM((pairs, others, share, 128), b16),
            pltpu.VMEM((shards * pairs, share, 128), b16),
            pltpu.VMEM((share, width), f32),
            pltpu.VMEM((shards, share, width), b16),
            pltpu.VMEM((rows // 2, lh), b16),
            pltpu.VMEM((others, tiles, share, tile), b16),
            pltpu.VMEM((others, tiles, share, tile), b16),
            dma((5,)),
            dma((4, others)), dma((4, others)),
            dma((4, 7)), dma((4, 7)),
            dma((2,)), dma((2,)),
            dma((pairs, others)), dma((pairs, others)),
            dma((others,)), dma((others,)),
            dma((tiles, others)), dma((tiles, others)),
        ],
        compiler_params=pltpu.CompilerParams(
            collective_id=0, has_side_effects=True, vmem_limit_bytes=56 * 1024 * 1024),
        cost_estimate=pl.CostEstimate(
            flops=6 * rows * width * (4 * lw + 2 * lh), bytes_accessed=16 * 1024 * 1024,
            transcendentals=0),
        name="encoder_layer",
    )(
        hidden_in, request_ids.reshape(rows, 1), request_ids.reshape(1, rows),
        w_qkv, w_out, w_up, w_down,
        ln1_gain.reshape(1, width), ln1_shift.reshape(1, width),
        ln2_gain.reshape(1, width), ln2_shift.reshape(1, width),
    )


def solution(mesh):
    in_specs = (
        P("group", None),
        P("group"),
        P(("group", "mp"), None),
        P(("group", "mp"), None),
        P(("group", "mp"), None),
        P(("group", "mp"), None),
        P(),
        P(),
        P(),
        P(),
    )
    out_specs = (P(("group", "mp"), None), P("group", "mp"), P("group", "mp"))
    whole_tiles = mesh.shape["group"] == 8 and mesh.shape["mp"] == 4
    body = kernel_body if whole_tiles else plain_body
    return jax.shard_map(body, mesh=mesh, in_specs=in_specs, out_specs=out_specs, check_vma=False)
```

```python
import functools

import jax
import jax.numpy as jnp
from jax import lax
from jax.experimental import pallas as pl
from jax.experimental.pallas import tpu as pltpu
from jax.sharding import PartitionSpec as P

HD = 64
SHORT = 64


def swapped(value, axis, distance):
    return lax.ppermute(value, axis, [(i, i ^ 1 << distance) for i in range(lax.axis_size(axis))])


def layer_norm(values_in, norm_gain, norm_shift):
    center = values_in - jnp.mean(values_in, axis=-1, keepdims=True)
    spread = jnp.mean(center * center, axis=-1, keepdims=True)
    return center * lax.rsqrt(spread + 1e-05) * norm_gain + norm_shift


def plain_body(
    hidden_in, request_ids, w_qkv, w_out, w_up, w_down, ln1_gain, ln1_shift, ln2_gain, ln2_shift
):
    groups = lax.axis_size("group")
    shards = lax.axis_size("mp")
    model_width = hidden_in.shape[1]
    local_width = model_width // shards
    local_hidden = w_up.shape[1] // shards
    tok_rows = hidden_in.shape[0]
    part_rows = w_qkv.shape[0]
    pieces = (
        w_qkv.astype(jnp.bfloat16).reshape(part_rows, 3, shards, local_width),
        w_out.astype(jnp.bfloat16).reshape(part_rows, 1, shards, local_width),
        w_up.astype(jnp.bfloat16).reshape(part_rows, 1, shards, local_hidden),
        w_down.astype(jnp.bfloat16).reshape(part_rows, 1, shards, local_hidden),
    )
    gathered = (
        lax.all_gather(pieces[0], "group", axis=0, tiled=True),
        lax.all_gather(pieces[1], "group", axis=0, tiled=True),
        lax.all_gather(pieces[2], "group", axis=0, tiled=True),
        lax.all_gather(pieces[3], "group", axis=0, tiled=True),
    )
    exchanged = (
        lax.all_to_all(gathered[0], "mp", split_axis=2, concat_axis=0, tiled=True),
        lax.all_to_all(gathered[1], "mp", split_axis=2, concat_axis=0, tiled=True),
        lax.all_to_all(gathered[2], "mp", split_axis=2, concat_axis=0, tiled=True),
        lax.all_to_all(gathered[3], "mp", split_axis=2, concat_axis=0, tiled=True),
    )
    served = tuple(
        (
            jnp.transpose(
                weight_piece.reshape(shards, groups, part_rows, -1), (1, 0, 2, 3)
            ).reshape(model_width, -1)
            for weight_piece in exchanged
        )
    )
    qkv_local, out_local, up_local, down_local = served
    projected = jnp.dot(hidden_in, qkv_local, preferred_element_type=jnp.float32)
    queries = projected[:, :local_width].astype(jnp.bfloat16)
    key_rows = projected[:, local_width : 2 * local_width].astype(jnp.bfloat16)
    value_rows = projected[:, 2 * local_width :].astype(jnp.bfloat16)
    partner_keys, partner_values = swapped((key_rows, value_rows), "group", 0)
    group_index = lax.axis_index("group")
    parity = group_index % 2
    long_id = jnp.where(parity == 0, request_ids[-1], request_ids[0])
    own_long = request_ids == long_id
    local_heads = local_width // HD
    score_scale = HD ** (-0.5)
    block_total = tok_rows // SHORT
    short_q = queries.reshape(block_total, SHORT, local_heads, HD)
    short_k = key_rows.reshape(block_total, SHORT, local_heads, HD)
    short_v = value_rows.reshape(block_total, SHORT, local_heads, HD)
    short_ids = request_ids.reshape(block_total, SHORT)
    short_scores = (
        jnp.einsum("bqhd,bkhd->bhqk", short_q, short_k, preferred_element_type=jnp.float32)
        * score_scale
    )
    short_mask = short_ids[:, :, None] == short_ids[:, None, :]
    short_scores = jnp.where(short_mask[:, None], short_scores, -1e30)
    short_peak = jnp.max(short_scores, axis=-1, keepdims=True)
    short_weights = jnp.exp(short_scores - short_peak).astype(jnp.bfloat16)
    short_totals = jnp.sum(short_weights.astype(jnp.float32), axis=-1)
    short_mixed = jnp.einsum(
        "bhqk,bkhd->bqhd", short_weights, short_v, preferred_element_type=jnp.float32
    )
    short_out = (
        (short_mixed / jnp.transpose(short_totals, (0, 2, 1))[:, :, :, None])
        .astype(jnp.bfloat16)
        .reshape(tok_rows, local_width)
    )
    first_keys = jnp.where(parity == 0, key_rows, partner_keys)
    second_keys = jnp.where(parity == 0, partner_keys, key_rows)
    first_values = jnp.where(parity == 0, value_rows, partner_values)
    second_values = jnp.where(parity == 0, partner_values, value_rows)
    pair_base = (group_index - parity) * tok_rows
    span_start = long_id - tok_rows + 1 - pair_base
    long_keys = lax.dynamic_slice_in_dim(
        jnp.concatenate([first_keys, second_keys], 0), span_start, tok_rows, 0
    ).reshape(tok_rows, local_heads, HD)
    long_values = lax.dynamic_slice_in_dim(
        jnp.concatenate([first_values, second_values], 0), span_start, tok_rows, 0
    ).reshape(tok_rows, local_heads, HD)
    query_rows = min(512, tok_rows)
    query_blocks = tok_rows // query_rows

    def long_attend(block_queries):
        heads_view = block_queries.reshape(query_rows, local_heads, HD)
        scores = (
            jnp.einsum("qhd,khd->hqk", heads_view, long_keys, preferred_element_type=jnp.float32)
            * score_scale
        )
        row_peak = jnp.max(scores, axis=-1, keepdims=True)
        weights = jnp.exp(scores - row_peak).astype(jnp.bfloat16)
        totals = jnp.sum(weights.astype(jnp.float32), axis=-1)
        mixed_heads = jnp.einsum(
            "hqk,khd->qhd", weights, long_values, preferred_element_type=jnp.float32
        )
        return (
            (mixed_heads / jnp.transpose(totals)[:, :, None])
            .astype(jnp.bfloat16)
            .reshape(query_rows, local_width)
        )

    def skipped(block_queries):
        return jnp.zeros((query_rows, local_width), jnp.bfloat16)

    def long_block(query_block):
        block_queries, block_long = query_block
        return lax.cond(jnp.any(block_long), long_attend, skipped, block_queries)

    long_out = lax.map(
        long_block,
        (
            queries.reshape(query_blocks, query_rows, local_width),
            own_long.reshape(query_blocks, query_rows),
        ),
    ).reshape(tok_rows, local_width)
    attended = jnp.where(own_long[:, None], long_out, short_out)
    share_rows = tok_rows // shards
    row_start = lax.axis_index("mp") * share_rows

    def combine(term_fn, residual, norm_gain, norm_shift):
        summed = lax.psum(term_fn(0, tok_rows), "mp")
        whole_rows = layer_norm(
            residual.astype(jnp.float32) + summed, norm_gain, norm_shift
        ).astype(jnp.bfloat16)
        normed = lax.dynamic_slice_in_dim(whole_rows, row_start, share_rows, 0)
        return (normed, whole_rows)

    def attn_term(row_begin, row_count):
        return lax.dot_general(
            attended, out_local, (((1,), (1,)), ((), ())), preferred_element_type=jnp.float32
        )

    attn_share, attn_normed = combine(attn_term, hidden_in, ln1_gain, ln1_shift)
    activated = jax.nn.gelu(
        jnp.dot(attn_normed, up_local, preferred_element_type=jnp.float32), approximate=False
    ).astype(jnp.bfloat16)

    def feed_term(row_begin, row_count):
        return lax.dot_general(
            activated, down_local, (((1,), (1,)), ((), ())), preferred_element_type=jnp.float32
        )

    final_share, unused = combine(feed_term, attn_normed, ln2_gain, ln2_shift)
    return (final_share, key_rows, value_rows)


MESH = pl.DeviceIdType.MESH
Q, O, U, W = range(4)


def layer_kernel(
    shards, hid_in, id_col, id_row, w_qkv_in, w_out_in, w_up_in, w_down_in,
    gain1, shift1, gain2, shift2,
    out, k_out, v_out,
    hid, w_qkv, w_out, w_up, w_down,
    stage_q, stage_o, stage_u, stage_d, full_q, full_o, full_u, full_d,
    bias, queries, kv, vals_ones, att, att_in, sums, normed, act, rs_send, rs_recv,
    in_sem, z_send, z_recv, p_send, p_recv, kv_send, kv_recv, a_send, a_recv,
    n_send, n_recv, r_send, r_recv,
):
    g = lax.axis_index("group")
    m = lax.axis_index("mp")
    core = lax.rem(g, 2)
    x = lax.rem(g // 2, 2)
    y = g // 4
    half = m // 2
    side = lax.rem(m, 2)
    sib = g + 1 - 2 * core
    gx = g + 2 - 4 * x
    gy = g + 4 - 8 * y
    gd = gx + gy - g
    m1 = m + 1 - 2 * side
    m2 = m + 2 - 4 * half
    rows = hid.shape[0]
    width = hid.shape[1]
    part = w_qkv.shape[0]
    lw = queries.shape[1]
    lh = act.shape[1]
    pairs = lw // 128
    share = rows // shards
    f32, b16 = jnp.float32, jnp.bfloat16
    fulls = (full_q, full_o, full_u, full_d)
    stages = (stage_q, stage_o, stage_u, stage_d)
    peers = [lax.rem(m + k, shards) for k in range(1, shards)]
    spot = 2 * x + side
    square = ((g, m1), (gx, m), (gx, m1))
    square_spot = (2 * x + 1 - side, 2 - 2 * x + side, 3 - 2 * x - side)

    def block_at(on_y, on_core, on_half):
        return (on_y * 2 + on_core) * 2 + on_half

    mine = (g * shards + m,) * 2 + (block_at(y, core, half) * 4 + spot,) * 2

    def z_copy(kind, k):
        if kind == Q:
            chunk, target = stage_q.at[peers[k]], (g, peers[k])
        elif kind == O:
            chunk, target = stage_o.at[0], (g, peers[k])
        else:
            chunk, target = stages[kind].at[square_spot[k]], square[k]
        return pltpu.make_async_remote_copy(
            src_ref=chunk, dst_ref=fulls[kind].at[mine[kind]],
            send_sem=z_send.at[kind, k], recv_sem=z_recv.at[kind, k],
            device_id=target, device_id_type=MESH)

    plane_hops = (
        (g, (gx, m)), (g, (gy, m)), (gy, (gx, m)),
        (g, (sib, m)), (gx, (sib, m)), (gy, (sib, m)), (gd, (sib, m)))
    b_own = block_at(y, core, half)
    b_z = block_at(y, core, 1 - half)
    b_y = block_at(1 - y, core, half)
    b_d = block_at(1 - y, core, 1 - half)
    hidden_hops = (
        (b_own, (g, m2)), (b_own, (gy, m)), (b_z, (gy, m)),
        (b_own, (sib, m)), (b_z, (sib, m)), (b_y, (sib, m)), (b_d, (sib, m)))

    def p_copy(kind, step):
        block, target = (plane_hops if kind in (Q, O) else hidden_hops)[step]
        place = fulls[kind].at[pl.ds(block * 4, 4)]
        return pltpu.make_async_remote_copy(
            src_ref=place, dst_ref=place,
            send_sem=p_send.at[kind, step], recv_sem=p_recv.at[kind, step],
            device_id=target, device_id_type=MESH)

    def arrived(kind):
        for k in range(shards - 1):
            z_copy(kind, k).wait_recv()

    def go(kind, *steps):
        for step in steps:
            p_copy(kind, step).start()

    def landed(kind, *steps):
        for step in steps:
            p_copy(kind, step).wait_recv()

    def kv_copy(i):
        return pltpu.make_async_remote_copy(
            src_ref=kv.at[i, 0], dst_ref=kv.at[i, 1],
            send_sem=kv_send.at[i], recv_sem=kv_recv.at[i],
            device_id=(sib, m), device_id_type=MESH)

    def a_copy(p, k):
        return pltpu.make_async_remote_copy(
            src_ref=att.at[p, k],
            dst_ref=att_in.at[m * pairs + p],
            send_sem=a_send.at[p, k], recv_sem=a_recv.at[p, k],
            device_id=(g, lax.rem(m + 1 + k, shards)), device_id_type=MESH)

    def n_copy(k):
        return pltpu.make_async_remote_copy(
            src_ref=normed.at[spot], dst_ref=normed.at[spot],
            send_sem=n_send.at[k], recv_sem=n_recv.at[k],
            device_id=square[k], device_id_type=MESH)

    tiles = rs_send.shape[1]
    tile = rs_send.shape[3]

    def r_copy(n, k):
        return pltpu.make_async_remote_copy(
            src_ref=rs_send.at[k, n],
            dst_ref=rs_recv.at[k, n],
            send_sem=r_send.at[n, k], recv_sem=r_recv.at[n, k],
            device_id=square[k], device_id_type=MESH)

    loads = [
        pltpu.make_async_copy(far, near, in_sem.at[i])
        for i, (far, near) in enumerate((
            (w_qkv_in, w_qkv), (w_out_in, w_out), (w_up_in, w_up), (w_down_in, w_down),
            (hid_in, hid)))
    ]

    def stage(kind):
        loads[kind].wait()
        if kind == Q:
            for d in range(shards):
                for j in range(3):
                    stage_q[d, :, j * lw:(j + 1) * lw] = w_qkv[
                        :, j * width + d * lw:j * width + (d + 1) * lw].astype(b16)
        elif kind == O:
            stage_o[0] = w_out[...].astype(b16)
        else:
            source = w_up if kind == U else w_down
            for d in range(shards):
                stages[kind][d] = source[:, d * lh:(d + 1) * lh].astype(b16)
        fulls[kind][mine[kind]] = stages[kind][(m, 0, spot, spot)[kind]]

    barrier = pltpu.get_barrier_semaphore()
    everyone = [(g, peer) for peer in peers] + [(gx, m), (gy, m), (sib, m), (gx, m1)]
    for target in everyone:
        pl.semaphore_signal(barrier, inc=1, device_id=target, device_id_type=MESH)
    for load in loads:
        load.start()
    stage(Q)
    pl.semaphore_wait(barrier, len(everyone))

    def depart(kind):
        for k in range(shards - 1):
            z_copy(kind, k).start()

    depart(Q)
    for kind in (U, W, O):
        stage(kind)
        depart(kind)

    long_id = jnp.where(core == 0, id_col[rows - 1:rows, :], id_col[0:1, :])
    slot = sib * rows + lax.broadcasted_iota(jnp.int32, (1, rows), 1)
    reach = jnp.where((slot > long_id - rows) & (slot <= long_id), long_id, -1)
    few = 32

    def bias_step(i, carry):
        here = pl.ds(pl.multiple_of(i * few, few), few)
        ids = id_col[here, :]
        bias[here, :rows] = jnp.where(ids == id_row[...], 0.0, -1e30).astype(f32)
        bias[here, rows:] = jnp.where(ids == reach, 0.0, -1e30).astype(f32)
        return carry

    lax.fori_loop(0, rows // few, bias_step, 0)
    for p in range(pairs):
        for i in range(2):
            vals_ones[p, i, :, 128:] = jnp.ones((rows, 128), b16)

    arrived(Q)
    go(Q, 0, 1, 3)
    arrived(U)
    go(U, 0, 1, 3)
    arrived(W)
    go(W, 0, 1, 3)
    loads[4].wait()
    landed(Q, 0, 1)
    go(Q, 2, 4, 5)
    arrived(O)
    go(O, 0, 1, 3)
    landed(Q, 2)
    go(Q, 6)
    landed(Q, 3, 4, 5, 6)

    def project(i, carry):
        j = lax.rem(i + 1, 3)
        here = pl.ds(pl.multiple_of(j * lw, lw), lw)
        block = full_q[:, :, here].reshape(width, lw)
        some = jnp.dot(hid[...], block, preferred_element_type=f32).astype(b16)

        @pl.when(i < 2)
        def _():
            kv[i, 0] = some
            kv_copy(i).start()

        @pl.when(i == 2)
        def _():
            queries[...] = some * jnp.asarray(HD ** -0.5, b16)

        return carry

    lax.fori_loop(0, 3, project, 0)
    k_out[...] = kv[0, 0]
    v_out[...] = kv[1, 0]
    for i in range(2):
        kv_copy(i).wait_recv()
    for p in range(pairs):
        vals_ones[p, :, :, :128] = kv[1, :, :, p * 128:(p + 1) * 128]

    lane = lax.broadcasted_iota(jnp.int32, (2 * share, 128), 1)
    own_rows = pl.ds(pl.multiple_of(m * share, share), share)

    def attend(p, carry):
        cols = pl.ds(pl.multiple_of(p * 128, 128), 128)

        def step(j, carry):
            spans = [
                pl.ds(pl.multiple_of(lax.rem(m + 1 + 2 * j + i, shards) * share, share), share)
                for i in range(2)
            ]
            pair_q = jnp.concatenate([queries[here, cols] for here in spans], axis=0)
            halves = []
            for h in range(2):
                own = (lane < HD) if h == 0 else (lane >= HD)
                head_q = jnp.where(own, pair_q, jnp.zeros_like(pair_q))
                scores = lax.dot_general(
                    head_q, kv[0, :, :, cols].reshape(2 * rows, 128),
                    (((1,), (1,)), ((), ())), preferred_element_type=f32)
                scores = scores + jnp.concatenate([bias[here, :] for here in spans], axis=0)
                peak = jnp.max(scores, axis=-1, keepdims=True)
                weights = jnp.exp(scores - peak).astype(b16)
                mixed = jnp.dot(
                    weights, vals_ones[p].reshape(2 * rows, 256), preferred_element_type=f32)
                halves.append(mixed[:, :128] / mixed[:, 128:])
            mixed_rows = jnp.where(lane < HD, halves[0], halves[1]).astype(b16)
            for i in range(2):
                k = 2 * j + i

                @pl.when(k < shards - 1)
                def _():
                    att[p, k] = mixed_rows[i * share:(i + 1) * share]
                    a_copy(p, k).start()

                @pl.when(k == shards - 1)
                def _():
                    att_in[m * pairs + p] = mixed_rows[i * share:(i + 1) * share]

            return carry

        lax.fori_loop(0, shards // 2, step, 0)

        @pl.when(p == 0)
        def _():
            landed(O, 0, 1)
            go(O, 2, 4, 5)

        return carry

    lax.fori_loop(0, pairs, attend, 0)
    landed(O, 2)
    go(O, 6)
    landed(U, 0, 1)
    go(U, 2, 4, 5)
    landed(W, 0, 1)
    go(W, 2, 4, 5)
    landed(O, 3, 4, 5, 6)
    for p in range(pairs):
        for k in range(shards - 1):
            a_copy(p, k).wait_recv()

    n_wide = 256
    o_parts = n_wide // part

    def out_step(n, carry):
        here = pl.ds(pl.multiple_of(n * n_wide, n_wide), n_wide)
        joined = jnp.concatenate([att_in[i] for i in range(shards * pairs)], axis=1)
        block = full_o[pl.ds(n * o_parts, o_parts)].reshape(n_wide, width)
        sums[:, here] = lax.dot_general(
            joined, block, (((1,), (1,)), ((), ())), preferred_element_type=f32)
        return carry

    lax.fori_loop(0, width // n_wide, out_step, 0)

    def ln_step(i, carry):
        here = pl.ds(pl.multiple_of(i * few, few), few)
        there = pl.ds(pl.multiple_of(m * share + i * few, few), few)
        normed[spot, here, :] = layer_norm(
            hid[there, :].astype(f32) + sums[here, :], gain1[...], shift1[...]).astype(b16)
        return carry

    lax.fori_loop(0, share // few, ln_step, 0)
    for k in (1, 0, 2):
        n_copy(k).start()
    landed(U, 2)
    go(U, 6)
    landed(U, 3, 4, 5, 6)

    order = []
    for r in range(8 * shards):
        group_r, z_r = r // shards, r % shards
        order.append(((group_r // 4 * 2 + group_r % 2) * 2 + z_r // 2) * 4
                     + group_r // 2 % 2 * 2 + z_r % 2)
    d_parts = tile // part

    def feed(batch, carry):
        first = spot * (1 - batch) + square_spot[2] * batch
        second = square_spot[1] * (1 - batch) + square_spot[0] * batch

        @pl.when(batch == 0)
        def _():
            n_copy(1).wait_recv()

        @pl.when(batch == 1)
        def _():
            n_copy(0).wait_recv()
            n_copy(2).wait_recv()

        def up_step(n, carry):
            here = pl.ds(pl.multiple_of(n * n_wide, n_wide), n_wide)
            block = jnp.concatenate([full_u[r, :, here] for r in order], axis=0)
            tokens = jnp.concatenate([normed[first], normed[second]], axis=0)
            pre = jnp.dot(tokens, block, preferred_element_type=f32)
            act[:, here] = (0.5 * pre * (1.0 + lax.erf(pre * (0.5 ** 0.5)))).astype(b16)
            return carry

        lax.fori_loop(0, lh // n_wide, up_step, 0)

        @pl.when(batch == 0)
        def _():
            landed(W, 2)
            go(W, 6)
            landed(W, 3, 4, 5, 6)

        def down_step(n, carry):
            start = n // 2 * 16 + lax.rem(n, 2) * 2
            block = jnp.concatenate(
                [full_d[start + i // 4 * 8 + i % 4 // 2 * 4 + i % 2] for i in range(d_parts)], axis=0)
            term = lax.dot_general(
                act[...], block, (((1,), (1,)), ((), ())), preferred_element_type=f32)

            @pl.when(batch == 0)
            def _():
                rs_send[1, n] = term[share:].astype(b16)
                r_copy(n, 1).start()
                sums[:, pl.ds(pl.multiple_of(n * tile, tile), tile)] = term[:share]

            @pl.when(batch == 1)
            def _():
                rs_send[2, n] = term[:share].astype(b16)
                r_copy(n, 2).start()
                rs_send[0, n] = term[share:].astype(b16)
                r_copy(n, 0).start()

            return carry

        lax.fori_loop(0, tiles, down_step, 0)
        return carry

    lax.fori_loop(0, 2, feed, 0)

    def total_step(n, carry):
        cols = pl.ds(pl.multiple_of(n * tile, tile), tile)
        total = normed[spot, :, cols].astype(f32) + sums[:, cols]
        for k in (1, 0, 2):
            r_copy(n, k).wait_recv()
            total = total + rs_recv[k, n].astype(f32)
        sums[:, cols] = total
        return carry

    lax.fori_loop(0, tiles, total_step, 0)

    def last_step(i, carry):
        here = pl.ds(pl.multiple_of(i * few, few), few)
        out[here, :] = layer_norm(sums[here, :], gain2[...], shift2[...]).astype(b16)
        return carry

    lax.fori_loop(0, share // few, last_step, 0)

    for kind in (Q, O, U, W):
        for k in range(shards - 1):
            z_copy(kind, k).wait_send()
        for step in range(7):
            p_copy(kind, step).wait_send()
    for i in range(2):
        kv_copy(i).wait_send()
    for k in range(shards - 1):
        n_copy(k).wait_send()
        for p in range(pairs):
            a_copy(p, k).wait_send()
        for n in range(tiles):
            r_copy(n, k).wait_send()


def kernel_body(
    hidden_in, request_ids, w_qkv, w_out, w_up, w_down, ln1_gain, ln1_shift, ln2_gain, ln2_shift
):
    groups = lax.axis_size("group")
    shards = lax.axis_size("mp")
    rows, width = hidden_in.shape
    part = w_qkv.shape[0]
    parts = groups * shards
    lw = width // shards
    lh = w_up.shape[1] // shards
    share = rows // shards
    pairs = lw // 128
    tile = 256
    tiles = width // tile
    b16, f32 = jnp.bfloat16, jnp.float32
    vmem = pl.BlockSpec(memory_space=pltpu.VMEM)
    hbm = pl.BlockSpec(memory_space=pltpu.HBM)
    dma = pltpu.SemaphoreType.DMA
    others = shards - 1
    return pl.pallas_call(
        functools.partial(layer_kernel, shards),
        out_shape=(
            jax.ShapeDtypeStruct((share, width), b16),
            jax.ShapeDtypeStruct((rows, lw), b16),
            jax.ShapeDtypeStruct((rows, lw), b16),
        ),
        in_specs=[hbm] + [vmem] * 2 + [hbm] * 4 + [vmem] * 4,
        out_specs=(vmem,) * 3,
        scratch_shapes=[
            pltpu.VMEM((rows, width), b16),
            pltpu.VMEM(w_qkv.shape, f32),
            pltpu.VMEM(w_out.shape, f32),
            pltpu.VMEM(w_up.shape, f32),
            pltpu.VMEM(w_down.shape, f32),
            pltpu.VMEM((shards, part, 3 * lw), b16),
            pltpu.VMEM((1, part, width), b16),
            pltpu.VMEM((shards, part, lh), b16),
            pltpu.VMEM((shards, part, lh), b16),
            pltpu.VMEM((parts, part, 3 * lw), b16),
            pltpu.VMEM((parts, part, width), b16),
            pltpu.VMEM((parts, part, lh), b16),
            pltpu.VMEM((parts, part, lh), b16),
            pltpu.VMEM((rows, 2 * rows), f32),
            pltpu.VMEM((rows, lw), b16),
            pltpu.VMEM((2, 2, rows, lw), b16),
            pltpu.VMEM((pairs, 2, rows, 256), b16),
            pltpu.VMEM((pairs, others, share, 128), b16),
            pltpu.VMEM((shards * pairs, share, 128), b16),
            pltpu.VMEM((share, width), f32),
            pltpu.VMEM((shards, share, width), b16),
            pltpu.VMEM((rows // 2, lh), b16),
            pltpu.VMEM((others, tiles, share, tile), b16),
            pltpu.VMEM((others, tiles, share, tile), b16),
            dma((5,)),
            dma((4, others)), dma((4, others)),
            dma((4, 7)), dma((4, 7)),
            dma((2,)), dma((2,)),
            dma((pairs, others)), dma((pairs, others)),
            dma((others,)), dma((others,)),
            dma((tiles, others)), dma((tiles, others)),
        ],
        compiler_params=pltpu.CompilerParams(
            collective_id=0, has_side_effects=True, vmem_limit_bytes=56 * 1024 * 1024),
        cost_estimate=pl.CostEstimate(
            flops=6 * rows * width * (4 * lw + 2 * lh), bytes_accessed=16 * 1024 * 1024,
            transcendentals=0),
        name="encoder_layer",
    )(
        hidden_in, request_ids.reshape(rows, 1), request_ids.reshape(1, rows),
        w_qkv, w_out, w_up, w_down,
        ln1_gain.reshape(1, width), ln1_shift.reshape(1, width),
        ln2_gain.reshape(1, width), ln2_shift.reshape(1, width),
    )


def solution(mesh):
    in_specs = (
        P("group", None),
        P("group"),
        P(("group", "mp"), None),
        P(("group", "mp"), None),
        P(("group", "mp"), None),
        P(("group", "mp"), None),
        P(),
        P(),
        P(),
        P(),
    )
    out_specs = (P(("group", "mp"), None), P("group", "mp"), P("group", "mp"))
    whole_tiles = mesh.shape["group"] == 8 and mesh.shape["mp"] == 4
    body = kernel_body if whole_tiles else plain_body
    return jax.shard_map(body, mesh=mesh, in_specs=in_specs, out_specs=out_specs, check_vma=False)
```
